128 devices in a mesh: batch: 32 (over x, z, core), pass: 4 (over y).
Axes of the slice: x: 4, y: 4, z: 4, core: 2. Of those that a mesh axis runs over, the one named last changes fastest.
Arguments:
- embedded: bfloat16 [64, 128, 768], P('batch'), may hold values from -6 to 6
- cotangent: bfloat16 [4, 64, 128, 768], P('pass', 'batch'), may hold values from -6 to 6
- lengths: int32 [64], P('batch'), may hold values from 64 to 128, as said below
- starts: int32 [64], P('batch'), may hold values from 1 to 32, as said below
- ln1_gain: float32 [768], replicated, may hold values from 0.5 to 1.5
- ln1_shift: float32 [768], replicated, may hold values from -3 to 3
- w_qkv: bfloat16 [768, 2304], replicated, may hold values from -0.21875 to 0.21875
- b_qv: float32 [1536], replicated, may hold values from -3 to 3
- w_out: bfloat16 [768, 768], replicated, may hold values from -1.75 to 1.75
- b_out: float32 [768], replicated, may hold values from -3 to 3
- ln2_gain: float32 [768], replicated, may hold values from 0.5 to 1.5
- ln2_shift: float32 [768], replicated, may hold values from -3 to 3
- w_up: bfloat16 [768, 3072], replicated, may hold values from -0.21875 to 0.21875
- b_up: float32 [3072], replicated, may hold values from -3 to 3
- w_down: bfloat16 [3072, 768], replicated, may hold values from -0.109375 to 0.109375
- b_down: float32 [768], replicated, may hold values from -3 to 3
Outputs:
- activations: bfloat16 [4, 64, 128, 768], P('pass', 'batch')
- input_grad: bfloat16 [64, 128, 768], P('batch')
- grad_ln1_gain: float32 [768], replicated
- grad_ln1_shift: float32 [768], replicated
- grad_w_qkv: float32 [768, 2304], replicated
- grad_b_qv: float32 [1536], replicated
- grad_w_out: float32 [768, 768], replicated
- grad_b_out: float32 [768], replicated
- grad_ln2_gain: float32 [768], replicated
- grad_ln2_shift: float32 [768], replicated
- grad_w_up: float32 [768, 3072], replicated
- grad_b_up: float32 [3072], replicated
- grad_w_down: float32 [3072, 768], replicated
- grad_b_down: float32 [768], replicated
The draws below stay inside these ranges and needn't reach their ends.
Inputs may be any that keep to these rules, and one draw needn't show every extreme that they name: `lengths`: each question has at least 64 true tokens; in every draw some question has exactly 128. The thought slots of a question are the 6 positions from its start on, all within its true length; in every draw some question starts at 32.
All inputs are finite; a program needn't handle non-finite values.
Results may differ from the reference program's by a relative error of at most 0.017.
Values may be sent and summed in bfloat16 or wider, within the bound.
A program may use at most 192 MiB of HBM per device.

```python
import jax
import jax.numpy as jnp
from jax import lax

D = 768
HEADS = 12
FF = 3072
LEN = 128
THOUGHT_SLOTS = 6
QTOT = 64
N_BATCH = 32
N_PASS = 4


def draw_lengths(key, part):
    key = jax.random.fold_in(key, 11)
    first_key, second_key = jax.random.split(key)
    drawn = jax.random.randint(first_key, (QTOT,), LEN // 2, LEN + 1)
    chosen = jax.random.randint(second_key, (), 0, QTOT)
    return jnp.where(jnp.arange(QTOT) == chosen, LEN, drawn).astype(jnp.int32)


def draw_starts(key, part):
    key = jax.random.fold_in(key, 23)
    first_key, second_key = jax.random.split(key)
    drawn = jax.random.randint(first_key, (QTOT,), 1, LEN // 4 + 1)
    chosen = jax.random.randint(second_key, (), 0, QTOT)
    return jnp.where(jnp.arange(QTOT) == chosen, LEN // 4, drawn).astype(jnp.int32)


def shard_levels(own_key, dims, cuts, low, top_value):
    loudness, own = 1.0, jax.random.fold_in(own_key, 6)
    for position, blocks in cuts:
        draws = jnp.exp(jax.random.uniform(jax.random.fold_in(own, position), (blocks,), jnp.float32, low / len(cuts), top_value / len(cuts)))
        loudness = loudness * jnp.repeat(draws, dims[position] // blocks).reshape([-1 if axis == position else 1 for axis in range(len(dims))])
    return loudness


def centred(rng, dims, spread, limit, cuts=(), held_as=jnp.bfloat16):
    entries = jax.random.normal(rng, dims, jnp.float32) * spread
    if len(cuts) > 0:
        entries = shard_levels(rng, dims, cuts, -0.22, 0.18) * entries
    return jnp.clip(entries, min=-limit, max=limit).astype(held_as)


def setup_inputs(seed: int = 0) -> dict:
    streams_of = jax.random.split(jax.random.key(seed), 17)
    return {
        "embedded": centred(streams_of[0], (QTOT, LEN, D), 1.0, 6.0, ((0, 32),)),
        "cotangent": centred(streams_of[1], (N_PASS, QTOT, LEN, D), 1.0, 6.0, ((0, 4), (1, 32))),
        "lengths": draw_lengths(jax.random.fold_in(streams_of[16], 71), 0),
        "starts": draw_starts(jax.random.fold_in(streams_of[16], 71), 0),
        "ln1_gain": jnp.clip(1.0 + 0.1 * jax.random.normal(streams_of[4], (D,), jnp.float32), 0.5, 1.5),
        "ln1_shift": centred(streams_of[5], (D,), 0.2, 3.0, (), jnp.float32),
        "w_qkv": centred(streams_of[6], (D, 3 * D), D ** -0.5, 0.21875),
        "b_qv": centred(streams_of[7], (2 * D,), 0.2, 3.0, (), jnp.float32),
        "w_out": centred(streams_of[8], (D, D), (D // 64) ** -0.5, 1.75),
        "b_out": centred(streams_of[9], (D,), 0.2, 3.0, (), jnp.float32),
        "ln2_gain": jnp.clip(1.0 + 0.1 * jax.random.normal(streams_of[10], (D,), jnp.float32), 0.5, 1.5),
        "ln2_shift": centred(streams_of[11], (D,), 0.2, 3.0, (), jnp.float32),
        "w_up": centred(streams_of[12], (D, FF), D ** -0.5, 0.21875),
        "b_up": centred(streams_of[13], (FF,), 0.3, 3.0, (), jnp.float32),
        "w_down": centred(streams_of[14], (FF, D), FF ** -0.5, 0.109375),
        "b_down": centred(streams_of[15], (D,), 0.2, 3.0, (), jnp.float32),
    }


@jax.custom_vjp
def low(v):
    return lax.optimization_barrier(v.astype(jnp.bfloat16)).astype(jnp.float32)

@jax.custom_vjp
def low_back(v):
    return v

def low_keep(v):
    return (low(v), None)

def low_pass(kept, grad):
    return (grad,)

def back_keep(v):
    return (v, None)

def back_low(kept, grad):
    return (low(grad),)
low.defvjp(low_keep, low_pass)
low_back.defvjp(back_keep, back_low)
epsilon = 1e-05
highest = lax.Precision.HIGHEST

def layer_norm(field, gain, shift):
    row_mean = lax.optimization_barrier(jnp.mean(field, -1, keepdims=True))
    centered = field - row_mean
    variance = lax.optimization_barrier(jnp.mean(centered * centered, -1, keepdims=True))
    return centered * lax.rsqrt(variance + epsilon) * gain + shift

def block(field, lengths, params):
    ln1_gain, ln1_shift, w_qkv, b_qv, w_out, b_out, ln2_gain, ln2_shift, w_up, b_up, w_down, b_down = params
    batch_size, row_count, embedding_width = field.shape
    head_size = embedding_width // HEADS
    scale_factor = head_size ** (-0.5)
    normed = low(layer_norm(field, ln1_gain, ln1_shift))
    projected = jnp.einsum('bld,de->ble', normed, w_qkv, precision=highest)
    queries = low_back(low(projected[..., :embedding_width] + b_qv[:embedding_width]))
    key_rows = low_back(low(projected[..., embedding_width:2 * embedding_width]))
    value_rows = low_back(low(projected[..., 2 * embedding_width:] + b_qv[embedding_width:]))
    split_shape = (batch_size, row_count, HEADS, head_size)
    scores = jnp.einsum('bqhe,bkhe->bhqk', queries.reshape(split_shape), key_rows.reshape(split_shape), precision=highest)
    scores = low_back(scores * scale_factor)
    token_position = jnp.arange(row_count, dtype=jnp.int32)
    allowed = (token_position[:, None] >= token_position[None, :])[None, None] & (token_position[None, None, None, :] < lengths[:, None, None, None])
    scores = jnp.where(allowed, scores, -1e+30)
    top_score = lax.optimization_barrier(jnp.max(scores, -1, keepdims=True))
    expo = jnp.exp(scores - top_score)
    attn_probs = low(expo / lax.optimization_barrier(jnp.sum(expo, -1, keepdims=True)))
    mixed_heads = jnp.einsum('bhqk,bkhe->bqhe', attn_probs, value_rows.reshape(split_shape), precision=highest)
    mixed_heads = low_back(low(mixed_heads.reshape(batch_size, row_count, embedding_width)))
    attn_out = low_back(jnp.einsum('bld,de->ble', mixed_heads, w_out, precision=highest) + b_out)
    residual = field + attn_out
    normed_two = low(layer_norm(residual, ln2_gain, ln2_shift))
    hidden = low_back(jnp.einsum('bld,di->bli', normed_two, w_up, precision=highest) + b_up)
    active = low(jax.nn.gelu(hidden, approximate=True))
    branch = low_back(jnp.einsum('bli,id->bld', active, w_down, precision=highest) + b_down)
    return residual + branch

def chain(field, params, lengths, starts):
    token_position = jnp.arange(LEN, dtype=jnp.int32)
    thought_mask = ((token_position[None, :] >= starts[:, None]) & (token_position[None, :] < starts[:, None] + THOUGHT_SLOTS))[:, :, None]
    current = field
    pass_outs = []
    for section_step in range(N_PASS):
        block_result = block(current, lengths, params)
        pass_outs.append(block_result)
        moved_rows = jnp.concatenate([jnp.zeros_like(block_result[:, :1]), block_result[:, :-1]], 1)
        current = jnp.where(thought_mask, low_back(low(moved_rows)), field)
    return jnp.stack(pass_outs)

def reference(embedded, cotangent, lengths, starts, ln1_gain, ln1_shift, w_qkv, b_qv, w_out, b_out, ln2_gain, ln2_shift, w_up, b_up, w_down, b_down):
    params = tuple((p.astype(jnp.float32) for p in (ln1_gain, ln1_shift, w_qkv, b_qv, w_out, b_out, ln2_gain, ln2_shift, w_up, b_up, w_down, b_down)))
    group_count = QTOT // N_BATCH
    fields = embedded.astype(jnp.float32).reshape(group_count, N_BATCH, LEN, D)
    cots = cotangent.astype(jnp.float32).reshape(N_PASS, group_count, N_BATCH, LEN, D).transpose(1, 0, 2, 3, 4)
    length_groups = lengths.reshape(group_count, N_BATCH)
    start_groups = starts.reshape(group_count, N_BATCH)

    def group_step(totals, pieces):
        field_group, cot_group, length_group, start_group = pieces
        outputs, pull_back = jax.vjp(lambda field_in, param_in: chain(field_in, param_in, length_group, start_group), field_group, params)
        field_gradient, grad_params = pull_back(cot_group)
        totals = jax.tree.map(lambda left, right: left + right, totals, grad_params)
        return (totals, (outputs, field_gradient))
    zero_grads = tuple((jnp.zeros_like(p) for p in params))
    totals, (outputs, grad_fields) = lax.scan(group_step, zero_grads, (fields, cots, length_groups, start_groups))
    activations = outputs.transpose(1, 0, 2, 3, 4).reshape(N_PASS, QTOT, LEN, D).astype(jnp.bfloat16)
    input_grad = grad_fields.reshape(QTOT, LEN, D).astype(jnp.bfloat16)
    return (activations, input_grad, totals[0], totals[1], totals[2], totals[3], totals[4], totals[5], totals[6], totals[7], totals[8], totals[9], totals[10], totals[11])
```

```python
import jax
import jax.numpy as jnp
from jax import lax
from jax.experimental import pallas as pl
from jax.experimental.pallas import tpu as pltpu
from jax.sharding import PartitionSpec as P

HEADS = 12
THOUGHT_SLOTS = 6


epsilon = 1e-05


def from_behind(value, axis, by):
    length = lax.axis_size(axis)
    pairs = [(i, i + by) for i in range(length) if 0 <= i + by < length]
    return lax.ppermute(value, axis, pairs)


def layer_norm(field, gain, shift):
    row_mean = jnp.mean(field, -1, keepdims=True)
    centered = field - row_mean
    variance = jnp.mean(centered * centered, -1, keepdims=True)
    return centered * lax.rsqrt(variance + epsilon) * gain + shift


def gelu_tanh(field):
    return jax.nn.gelu(field, approximate=True)


def allowed_mask(lengths, row_count):
    token_position = jnp.arange(row_count, dtype=jnp.int32)
    causal = (token_position[:, None] >= token_position[None, :])[None, None]
    return causal & (token_position[None, None, None, :] < lengths[:, None, None, None])


def select_rows(field, first_row, slot_count):
    return jax.vmap(lambda single, begin: lax.dynamic_slice_in_dim(single, begin, slot_count, 0))(
        field, first_row
    )


def put_rows(field, new_rows, first_row):
    return jax.vmap(
        lambda single, block_rows, begin: lax.dynamic_update_slice_in_dim(
            single, block_rows, begin, 0
        )
    )(field, new_rows, first_row)


def forward_sweep(sent_rows):
    return from_behind(sent_rows, "pass", 1)


def backward_sweep(sent_rows):
    return from_behind(sent_rows, "pass", -1)


def forward(field, lengths, params):
    (
        ln1_gain,
        ln1_shift,
        w_qkv,
        b_qv,
        w_out,
        b_out,
        ln2_gain,
        ln2_shift,
        w_up,
        b_up,
        w_down,
        b_down,
    ) = params
    batch_size, row_count, embedding_width = field.shape
    head_size = embedding_width // HEADS
    scale_factor = head_size ** (-0.5)
    split_shape = (batch_size, row_count, HEADS, head_size)
    normed = layer_norm(field, ln1_gain, ln1_shift).astype(jnp.bfloat16)
    projected = jnp.einsum("bld,de->ble", normed, w_qkv, preferred_element_type=jnp.float32)
    queries = (
        (projected[..., :embedding_width] + b_qv[:embedding_width])
        .astype(jnp.bfloat16)
        .reshape(split_shape)
    )
    key_rows = (
        projected[..., embedding_width : 2 * embedding_width]
        .astype(jnp.bfloat16)
        .reshape(split_shape)
    )
    value_rows = (
        (projected[..., 2 * embedding_width :] + b_qv[embedding_width:])
        .astype(jnp.bfloat16)
        .reshape(split_shape)
    )
    scores = (
        jnp.einsum("bqhe,bkhe->bhqk", queries, key_rows, preferred_element_type=jnp.float32)
        * scale_factor
    )
    scores = jnp.where(allowed_mask(lengths, row_count), scores, -1e30)
    top_score = jnp.max(scores, -1, keepdims=True)
    log_total = top_score + jnp.log(jnp.sum(jnp.exp(scores - top_score), -1, keepdims=True))
    attn_probs = jnp.exp(scores - log_total).astype(jnp.bfloat16)
    mixed_heads = jnp.einsum(
        "bhqk,bkhe->bqhe", attn_probs, value_rows, preferred_element_type=jnp.float32
    )
    mixed_heads = mixed_heads.reshape(batch_size, row_count, embedding_width).astype(jnp.bfloat16)
    attn_out = (
        jnp.einsum("bld,de->ble", mixed_heads, w_out, preferred_element_type=jnp.float32) + b_out
    )
    residual = field + attn_out
    normed_two = layer_norm(residual, ln2_gain, ln2_shift).astype(jnp.bfloat16)
    hidden = jnp.einsum("bld,di->bli", normed_two, w_up, preferred_element_type=jnp.float32) + b_up
    active = gelu_tanh(hidden).astype(jnp.bfloat16)
    block_result = (
        residual
        + jnp.einsum("bli,id->bld", active, w_down, preferred_element_type=jnp.float32)
        + b_down
    )
    kept = (
        field,
        normed,
        queries,
        key_rows,
        value_rows,
        log_total,
        mixed_heads,
        residual,
        normed_two,
        hidden,
        active,
    )
    return (block_result, kept)


def backward(kept, grad_out, lengths, params):
    (
        ln1_gain,
        ln1_shift,
        w_qkv,
        b_qv,
        w_out,
        b_out,
        ln2_gain,
        ln2_shift,
        w_up,
        b_up,
        w_down,
        b_down,
    ) = params
    (
        field,
        normed,
        queries,
        key_rows,
        value_rows,
        log_total,
        mixed_heads,
        residual,
        normed_two,
        hidden,
        active,
    ) = kept
    batch_size, row_count, embedding_width = field.shape
    head_size = embedding_width // HEADS
    scale_factor = head_size ** (-0.5)
    split_shape = (batch_size, row_count, HEADS, head_size)
    grad_branch = grad_out.astype(jnp.bfloat16)
    grad_w_down = jnp.einsum("bli,bld->id", active, grad_branch, preferred_element_type=jnp.float32)
    grad_b_down = jnp.sum(grad_branch.astype(jnp.float32), (0, 1))
    grad_active = jnp.einsum("bld,id->bli", grad_branch, w_down, preferred_element_type=jnp.float32)
    gelu_value, gelu_pull = jax.vjp(gelu_tanh, hidden)
    grad_hidden = gelu_pull(grad_active)[0].astype(jnp.bfloat16)
    grad_w_up = jnp.einsum(
        "bld,bli->di", normed_two, grad_hidden, preferred_element_type=jnp.float32
    )
    grad_b_up = jnp.sum(grad_hidden.astype(jnp.float32), (0, 1))
    grad_normed_two = jnp.einsum(
        "bli,di->bld", grad_hidden, w_up, preferred_element_type=jnp.float32
    )
    norm_value, norm_pull = jax.vjp(layer_norm, residual, ln2_gain, ln2_shift)
    grad_res_part, grad_ln2_gain, grad_ln2_shift = norm_pull(grad_normed_two)
    grad_residual = grad_out + grad_res_part
    grad_attn = grad_residual.astype(jnp.bfloat16)
    grad_w_out = jnp.einsum(
        "bld,ble->de", mixed_heads, grad_attn, preferred_element_type=jnp.float32
    )
    grad_b_out = jnp.sum(grad_attn.astype(jnp.float32), (0, 1))
    grad_mixed = jnp.einsum("ble,de->bld", grad_attn, w_out, preferred_element_type=jnp.float32)
    grad_mixed = grad_mixed.astype(jnp.bfloat16).reshape(split_shape)
    scores = (
        jnp.einsum("bqhe,bkhe->bhqk", queries, key_rows, preferred_element_type=jnp.float32)
        * scale_factor
    )
    scores = jnp.where(allowed_mask(lengths, row_count), scores, -1e30)
    probs_full = jnp.exp(scores - log_total)
    probs_low = probs_full.astype(jnp.bfloat16)
    grad_values = jnp.einsum(
        "bhqk,bqhe->bkhe", probs_low, grad_mixed, preferred_element_type=jnp.float32
    )
    grad_probs = jnp.einsum(
        "bqhe,bkhe->bhqk", grad_mixed, value_rows, preferred_element_type=jnp.float32
    )
    grad_scores = probs_full * (grad_probs - jnp.sum(probs_full * grad_probs, -1, keepdims=True))
    grad_scores = grad_scores.astype(jnp.bfloat16)
    grad_queries = (
        jnp.einsum("bhqk,bkhe->bqhe", grad_scores, key_rows, preferred_element_type=jnp.float32)
        * scale_factor
    )
    grad_keys = (
        jnp.einsum("bhqk,bqhe->bkhe", grad_scores, queries, preferred_element_type=jnp.float32)
        * scale_factor
    )
    flat_shape = (batch_size, row_count, embedding_width)
    grad_qkv = jnp.concatenate(
        [
            grad_queries.reshape(flat_shape),
            grad_keys.reshape(flat_shape),
            grad_values.reshape(flat_shape),
        ],
        -1,
    ).astype(jnp.bfloat16)
    grad_w_qkv = jnp.einsum("bld,ble->de", normed, grad_qkv, preferred_element_type=jnp.float32)
    grad_bias_sums = jnp.sum(grad_qkv.astype(jnp.float32), (0, 1))
    grad_b_qv = jnp.concatenate(
        [grad_bias_sums[:embedding_width], grad_bias_sums[2 * embedding_width :]]
    )
    grad_normed = jnp.einsum("ble,de->bld", grad_qkv, w_qkv, preferred_element_type=jnp.float32)
    first_value, first_pull = jax.vjp(layer_norm, field, ln1_gain, ln1_shift)
    grad_field_part, grad_ln1_gain, grad_ln1_shift = first_pull(grad_normed)
    field_gradient = grad_residual + grad_field_part
    grads = (
        grad_ln1_gain,
        grad_ln1_shift,
        grad_w_qkv,
        grad_b_qv,
        grad_w_out,
        grad_b_out,
        grad_ln2_gain,
        grad_ln2_shift,
        grad_w_up,
        grad_b_up,
        grad_w_down,
        grad_b_down,
    )
    return (field_gradient, grads)


def kept_zeros(microbatch_count, row_count, embedding_width, hidden_width):
    head_size = embedding_width // HEADS
    flat_shape = (microbatch_count, row_count, embedding_width)
    split_shape = (microbatch_count, row_count, HEADS, head_size)
    return (
        jnp.zeros(flat_shape, jnp.float32),
        jnp.zeros(flat_shape, jnp.bfloat16),
        jnp.zeros(split_shape, jnp.bfloat16),
        jnp.zeros(split_shape, jnp.bfloat16),
        jnp.zeros(split_shape, jnp.bfloat16),
        jnp.zeros((microbatch_count, HEADS, row_count, 1), jnp.float32),
        jnp.zeros(flat_shape, jnp.bfloat16),
        jnp.zeros(flat_shape, jnp.float32),
        jnp.zeros(flat_shape, jnp.bfloat16),
        jnp.zeros((microbatch_count, row_count, hidden_width), jnp.float32),
        jnp.zeros((microbatch_count, row_count, hidden_width), jnp.bfloat16),
    )


MESH = pl.DeviceIdType.MESH
BF, F32 = jnp.bfloat16, jnp.float32
ORDERS = ((0, 1, 2), (1, 2, 0), (2, 0, 1))
NMSG = 31

def coords():
    b = lax.axis_index("batch"); y = lax.axis_index("pass")
    core = b % 2
    z = (b // 2) % 4
    x = b // 8
    return (x, y, z), core

def device(pos, core):
    x, y, z = pos
    return ((x * 4 + z) * 2 + core, y)

def along(pos, axis, by):
    return tuple((c + by) % 4 if i == axis else c for i, c in enumerate(pos))

def comm_kernel(w_ref, out_ref, w_buf, relay1, in1, w2, relay2, in2, w3, in3, fin, lsem, ssem, rsem):
    pos, core = coords()
    barrier = pltpu.get_barrier_semaphore()
    for axis in range(3):
        for by in (1, 2, 3):
            pl.semaphore_signal(barrier, inc=1, device_id=device(along(pos, axis, by), core), device_id_type=MESH)
    pl.semaphore_signal(barrier, inc=1, device_id=device(pos, 1 - core), device_id_type=MESH)
    ld = pltpu.make_async_copy(w_ref, w_buf, lsem)
    ld.start()
    pl.semaphore_wait(barrier, 10)
    ld.wait()

    def msg(p, m, src, dst, to):
        return pltpu.make_async_remote_copy(src_ref=src, dst_ref=dst, send_sem=ssem.at[p, m], recv_sem=rsem.at[p, m], device_id=to, device_id_type=MESH)

    sent = []
    def send(p, m, src, dst, to):
        c = msg(p, m, src, dst, to)
        c.start()
        sent.append(c)
    def arrived(p, m, dst):
        msg(p, m, dst, dst, device(pos, 1 - core)).wait_recv()

    A = pl.ds(0, 768); B = pl.ds(768, 768)

    def rs_a(p, phase):
        axis = ORDERS[p][phase]; r = pos[axis]
        w, relay, inn = ((w_buf, relay1, in1), (w2, relay2, in2))[phase]
        b = 6 * phase
        up = device(along(pos, axis, 1), core); dn = device(along(pos, axis, 3), core)
        far = (r + 2) % 4; nx = (r + 1) % 4; pv = (r + 3) % 4
        send(p, b + 0, w.at[p, far, :, A], relay.at[p, 0], up)
        send(p, b + 1, w.at[p, far, :, B], relay.at[p, 1], dn)
        send(p, b + 2, w.at[p, nx, :, B], inn.at[p, 0, :, B], up)
        send(p, b + 3, w.at[p, pv, :, A], inn.at[p, 1, :, A], dn)

    def rs_b(p, phase):
        axis = ORDERS[p][phase]; r = pos[axis]
        w, relay, inn = ((w_buf, relay1, in1), (w2, relay2, in2))[phase]
        b = 6 * phase
        up = device(along(pos, axis, 1), core); dn = device(along(pos, axis, 3), core)
        nx = (r + 1) % 4; pv = (r + 3) % 4
        rows = w.shape[2]
        arrived(p, b + 0, relay.at[p, 0])
        def add(i, _):
            s = pl.ds(pl.multiple_of(i * 16, 16), 16)
            relay[p, 0, s, :] = (relay[p, 0, s, :].astype(F32) + w[p, nx, s, A].astype(F32)).astype(BF)
            return 0
        lax.fori_loop(0, rows // 16, add, 0)
        send(p, b + 4, relay.at[p, 0], inn.at[p, 0, :, A], up)
        arrived(p, b + 1, relay.at[p, 1])
        def add(i, _):
            s = pl.ds(pl.multiple_of(i * 16, 16), 16)
            relay[p, 1, s, :] = (relay[p, 1, s, :].astype(F32) + w[p, pv, s, B].astype(F32)).astype(BF)
            return 0
        lax.fori_loop(0, rows // 16, add, 0)
        send(p, b + 5, relay.at[p, 1], inn.at[p, 1, :, B], dn)

    def rs_c(p, phase):
        axis = ORDERS[p][phase]; r = pos[axis]
        w, relay, inn = ((w_buf, relay1, in1), (w2, relay2, in2))[phase]
        b = 6 * phase
        arrived(p, b + 2, inn.at[p, 0, :, B])
        arrived(p, b + 3, inn.at[p, 1, :, A])
        arrived(p, b + 4, inn.at[p, 0, :, A])
        arrived(p, b + 5, inn.at[p, 1, :, B])
        if phase == 0:
            for k in range(4):
                def add(i, _):
                    s = pl.ds(pl.multiple_of(k * 48 + i * 16, 16), 16)
                    t = pl.ds(pl.multiple_of(i * 16, 16), 16)
                    w2[p, k, t, :] = (w[p, r, s, :].astype(F32) + inn[p, 0, s, :].astype(F32) + inn[p, 1, s, :].astype(F32)).astype(BF)
                    return 0
                lax.fori_loop(0, 3, add, 0)
        else:
            for k in range(4):
                c = pl.ds(384 * k, 384)
                w3[p, k] = (w[p, r, :, c].astype(F32) + inn[p, 0, :, c].astype(F32) + inn[p, 1, :, c].astype(F32)).astype(BF)

    def rs3_a(p):
        axis = ORDERS[p][2]; r = pos[axis]
        for d in (1, 2, 3):
            send(p, 11 + d, w3.at[p, (r + d) % 4], in3.at[p, d - 1], device(along(pos, axis, d), core))

    def spot(p, c1, c2=None, c3=None, cols=None):
        o = out_ref.at[core, p]
        if c2 is None:
            rows = pl.ds(pl.multiple_of(192 * c1, 16), 192)
        else:
            rows = pl.ds(pl.multiple_of(192 * c1 + 48 * c2, 16), 48)
        if c3 is not None:
            cols = pl.ds(pl.multiple_of(384 * c3, 128), 384)
        if cols is None:
            return o.at[rows]
        return o.at[rows, cols]

    def rs3_b(p):
        axis = ORDERS[p][2]; r = pos[axis]
        for d in (1, 2, 3):
            arrived(p, 11 + d, in3.at[p, d - 1])
        fin[p] = (w3[p, r].astype(F32) + in3[p, 0].astype(F32) + in3[p, 1].astype(F32) + in3[p, 2].astype(F32)).astype(BF)
        c1, c2, c3 = (pos[a] for a in ORDERS[p])
        own = pltpu.make_async_copy(fin.at[p], spot(p, c1, c2, c3), lsem)
        own.start()
        for d in (1, 2, 3):
            send(p, 14 + d, fin.at[p], spot(p, c1, c2, c3), device(along(pos, axis, d), core))
        own.wait()

    def ag3(p):
        axis = ORDERS[p][2]
        c1, c2, c3 = (pos[a] for a in ORDERS[p])
        for d in (1, 2, 3):
            arrived(p, 14 + d, spot(p, c1, c2, (c3 + 4 - d) % 4))

    def ag_a(p, phase):
        axis = ORDERS[p][phase]
        c1, c2, _ = (pos[a] for a in ORDERS[p])
        b = 18 if phase == 1 else 22
        mine = spot(p, c1, c2) if phase == 1 else spot(p, c1)
        up = device(along(pos, axis, 1), core); dn = device(along(pos, axis, 3), core)
        send(p, b, mine, mine, up)
        send(p, b + 1, mine, mine, dn)
        if phase == 0:
            send(p, 26, mine, mine, device(pos, 1 - core))

    def ag_b(p, phase):
        axis = ORDERS[p][phase]
        c1, c2, _ = (pos[a] for a in ORDERS[p])
        b = 18 if phase == 1 else 22
        def sp(d, cols=None):
            return spot(p, c1, (c2 + d) % 4, cols=cols) if phase == 1 else spot(p, (c1 + d) % 4, cols=cols)
        up = device(along(pos, axis, 1), core); dn = device(along(pos, axis, 3), core)
        arrived(p, b, sp(3))
        send(p, b + 2, sp(3, A), sp(3, A), up)
        if phase == 0:
            send(p, 27, sp(3), sp(3), device(pos, 1 - core))
        arrived(p, b + 1, sp(1))
        send(p, b + 3, sp(1, B), sp(1, B), dn)
        if phase == 0:
            send(p, 28, sp(1), sp(1), device(pos, 1 - core))

    def ag_c(p, phase):
        axis = ORDERS[p][phase]
        c1, c2, _ = (pos[a] for a in ORDERS[p])
        b = 18 if phase == 1 else 22
        def sp(d, cols=None):
            return spot(p, c1, (c2 + d) % 4, cols=cols) if phase == 1 else spot(p, (c1 + d) % 4, cols=cols)
        arrived(p, b + 2, sp(2, A))
        if phase == 0:
            send(p, 29, sp(2, A), sp(2, A), device(pos, 1 - core))
        arrived(p, b + 3, sp(2, B))
        if phase == 0:
            send(p, 30, sp(2, B), sp(2, B), device(pos, 1 - core))

    def sib(p):
        c1 = pos[ORDERS[p][0]]
        def sp(d, cols=None):
            o = out_ref.at[1 - core, p]
            rows = pl.ds(pl.multiple_of(192 * ((c1 + d) % 4), 16), 192)
            return o.at[rows] if cols is None else o.at[rows, cols]
        arrived(p, 26, sp(0)); arrived(p, 27, sp(3)); arrived(p, 28, sp(1))
        arrived(p, 29, sp(2, A)); arrived(p, 30, sp(2, B))

    T = range(3)
    for p in T: rs_a(p, 0)
    for p in T: rs_b(p, 0)
    for p in T:
        rs_c(p, 0)
        rs_a(p, 1)
    for p in T: rs_b(p, 1)
    for p in T:
        rs_c(p, 1)
        rs3_a(p)
    for p in T: rs3_b(p)
    for p in T:
        ag3(p); ag_a(p, 1)
    for p in T: ag_b(p, 1)
    for p in T:
        ag_c(p, 1); ag_a(p, 0)
    for p in T: ag_b(p, 0)
    for p in T: ag_c(p, 0)
    for p in T: sib(p)
    for c in sent: c.wait_send()

def allreduce(w):
    return pl.pallas_call(
        comm_kernel,
        out_shape=jax.ShapeDtypeStruct((2, 3, 768, 1536), BF),
        in_specs=[pl.BlockSpec(memory_space=pl.ANY)],
        out_specs=pl.BlockSpec(memory_space=pl.ANY),
        scratch_shapes=[
            pltpu.VMEM((3, 4, 192, 1536), BF),
            pltpu.VMEM((3, 2, 192, 768), BF), pltpu.VMEM((3, 2, 192, 1536), BF),
            pltpu.VMEM((3, 4, 48, 1536), BF), pltpu.VMEM((3, 2, 48, 768), BF), pltpu.VMEM((3, 2, 48, 1536), BF),
            pltpu.VMEM((3, 4, 48, 384), BF), pltpu.VMEM((3, 3, 48, 384), BF), pltpu.VMEM((3, 48, 384), BF),
            pltpu.SemaphoreType.DMA, pltpu.SemaphoreType.DMA((3, NMSG)), pltpu.SemaphoreType.DMA((3, NMSG)),
        ],
        compiler_params=pltpu.CompilerParams(collective_id=0, has_side_effects=True, vmem_limit_bytes=50 * 2**20),
        name="comm",
    )(w)


def sum_gradients(grads):
    gq, go, gu, gd = [g.astype(BF) for g in grads]
    def half(c):
        return jnp.stack([
            jnp.concatenate([gq[:, c * 1152:(c + 1) * 1152], go[:, c * 384:(c + 1) * 384]], 1),
            gu[:, c * 1536:(c + 1) * 1536],
            jnp.concatenate([gd[c * 1536:c * 1536 + 768], gd[c * 1536 + 768:(c + 1) * 1536]], 1),
        ])
    halves = jnp.stack([half(0), half(1)])
    core = lax.axis_index("batch") % 2
    keep = lax.dynamic_index_in_dim(halves, core, 0, keepdims=False)
    give = lax.dynamic_index_in_dim(halves, 1 - core, 0, keepdims=False)
    got = lax.ppermute(give, "batch", [(i, i ^ 1) for i in range(lax.axis_size("batch"))])
    mine = (keep.astype(F32) + got.astype(F32)).astype(BF)
    out = allreduce(mine.reshape(3, 4, 192, 1536)).astype(F32)
    return (
        jnp.concatenate([out[0, 0, :, :1152], out[1, 0, :, :1152]], 1),
        jnp.concatenate([out[0, 0, :, 1152:], out[1, 0, :, 1152:]], 1),
        jnp.concatenate([out[0, 1], out[1, 1]], 1),
        jnp.concatenate([out[0, 2, :, :768], out[0, 2, :, 768:], out[1, 2, :, :768], out[1, 2, :, 768:]], 0),
    )


def on_device(
    embedded,
    cotangent,
    lengths,
    starts,
    ln1_gain,
    ln1_shift,
    w_qkv,
    b_qv,
    w_out,
    b_out,
    ln2_gain,
    ln2_shift,
    w_up,
    b_up,
    w_down,
    b_down,
):
    params = (
        ln1_gain,
        ln1_shift,
        w_qkv,
        b_qv,
        w_out,
        b_out,
        ln2_gain,
        ln2_shift,
        w_up,
        b_up,
        w_down,
        b_down,
    )
    section_index = lax.axis_index("pass")
    sections = lax.axis_size("pass")
    not_first = section_index > 0
    base_field = embedded.astype(jnp.float32)
    base_cot = cotangent[0].astype(jnp.float32)
    microbatch_count, row_count, embedding_width = base_field.shape
    hidden_width = w_up.shape[1]
    round_count = sections + microbatch_count - 1

    def forward_turn(turn, loop_state):
        arriving_rows, pass_outs, kept_all = loop_state
        offset = turn - section_index
        in_range = (offset >= 0) & (offset < microbatch_count)
        item_index = jnp.clip(offset, 0, microbatch_count - 1)
        field_item = lax.dynamic_slice_in_dim(base_field, item_index, 1, 0)
        starting_entry = lax.dynamic_slice_in_dim(starts, item_index, 1, 0)
        length_item = lax.dynamic_slice_in_dim(lengths, item_index, 1, 0)
        slot_rows = lax.dynamic_slice_in_dim(arriving_rows, item_index, 1, 0).astype(jnp.float32)
        current = jnp.where(not_first, put_rows(field_item, slot_rows, starting_entry), field_item)
        block_result, kept = forward(current, length_item, params)
        pass_outs = jnp.where(
            in_range,
            lax.dynamic_update_slice_in_dim(pass_outs, block_result, item_index, 0),
            pass_outs,
        )
        kept_all = jax.tree.map(
            lambda whole_buf, piece: jnp.where(
                in_range,
                lax.dynamic_update_slice_in_dim(whole_buf, piece, item_index, 0),
                whole_buf,
            ),
            kept_all,
            kept,
        )
        gathered_rows = forward_sweep(
            select_rows(block_result, starting_entry - 1, THOUGHT_SLOTS).astype(jnp.bfloat16)
        )
        target = turn + 1 - section_index
        target_ok = (target >= 0) & (target < microbatch_count)
        target_index = jnp.clip(target, 0, microbatch_count - 1)
        arriving_rows = jnp.where(
            target_ok,
            lax.dynamic_update_slice_in_dim(arriving_rows, gathered_rows, target_index, 0),
            arriving_rows,
        )
        return (arriving_rows, pass_outs, kept_all)

    arriving_rows = jnp.zeros((microbatch_count, THOUGHT_SLOTS, embedding_width), jnp.bfloat16)
    state = (
        arriving_rows,
        jnp.zeros_like(base_field),
        kept_zeros(microbatch_count, row_count, embedding_width, hidden_width),
    )
    arriving_rows, activations, kept_all = lax.fori_loop(0, round_count, forward_turn, state)

    def backward_turn(turn, loop_state):
        returned, grad_fields, grad_totals = loop_state
        offset = turn - (sections - 1 - section_index)
        in_range = (offset >= 0) & (offset < microbatch_count)
        item_index = jnp.clip(offset, 0, microbatch_count - 1)
        kept = jax.tree.map(
            lambda whole_buf: lax.dynamic_slice_in_dim(whole_buf, item_index, 1, 0), kept_all
        )
        cot_item = lax.dynamic_slice_in_dim(base_cot, item_index, 1, 0)
        starting_entry = lax.dynamic_slice_in_dim(starts, item_index, 1, 0)
        length_item = lax.dynamic_slice_in_dim(lengths, item_index, 1, 0)
        back_rows = lax.dynamic_slice_in_dim(returned, item_index, 1, 0).astype(jnp.float32)
        grad_out = cot_item + put_rows(jnp.zeros_like(cot_item), back_rows, starting_entry - 1)
        field_gradient, grads = backward(kept, grad_out, length_item, params)
        grad_fields = jnp.where(
            in_range,
            lax.dynamic_update_slice_in_dim(grad_fields, field_gradient, item_index, 0),
            grad_fields,
        )
        grad_totals = jax.tree.map(
            lambda running, fresh: running + jnp.where(in_range, fresh, 0.0), grad_totals, grads
        )
        gathered_rows = backward_sweep(
            select_rows(field_gradient, starting_entry, THOUGHT_SLOTS).astype(jnp.bfloat16)
        )
        target = offset + 1
        target_ok = (target >= 0) & (target < microbatch_count)
        target_index = jnp.clip(target, 0, microbatch_count - 1)
        returned = jnp.where(
            target_ok,
            lax.dynamic_update_slice_in_dim(returned, gathered_rows, target_index, 0),
            returned,
        )
        return (returned, grad_fields, grad_totals)

    zero_grads = tuple((jnp.zeros(param.shape, jnp.float32) for param in params))
    state = (
        jnp.zeros((microbatch_count, THOUGHT_SLOTS, embedding_width), jnp.bfloat16),
        jnp.zeros_like(base_field),
        zero_grads,
    )
    returned, field_gradient, grads = lax.fori_loop(0, round_count, backward_turn, state)
    token_position = jnp.arange(row_count, dtype=jnp.int32)
    thought_mask = (
        (token_position[None, :] >= starts[:, None])
        & (token_position[None, :] < starts[:, None] + THOUGHT_SLOTS)
    )[:, :, None]
    own_grad = jnp.where(not_first & thought_mask, 0.0, field_gradient)
    input_grad = lax.psum(own_grad.astype(jnp.bfloat16), "pass")
    big = sum_gradients([grads[2], grads[4], grads[8], grads[10]])
    small = list(lax.psum([g for i, g in enumerate(grads) if i not in (2, 4, 8, 10)], ("batch", "pass")))
    summed = small[:2] + [big[0], small[2], big[1]] + small[3:6] + [big[2], small[6], big[3], small[7]]
    return (activations.astype(jnp.bfloat16)[None], input_grad) + tuple(summed)


def solution(mesh):
    in_specs = (
        P("batch", None, None),
        P("pass", "batch", None, None),
        P("batch"),
        P("batch"),
        P(),
        P(),
        P(),
        P(),
        P(),
        P(),
        P(),
        P(),
        P(),
        P(),
        P(),
        P(),
    )
    out_specs = (
        P("pass", "batch", None, None),
        P("batch", None, None),
        P(),
        P(),
        P(),
        P(),
        P(),
        P(),
        P(),
        P(),
        P(),
        P(),
        P(),
        P(),
    )
    return jax.shard_map(
        on_device, mesh=mesh, in_specs=in_specs, out_specs=out_specs, check_vma=False
    )
```

```python
import functools

import jax
import jax.numpy as jnp
from jax import lax
from jax.experimental import pallas as pl
from jax.experimental.pallas import tpu as pltpu
from jax.sharding import PartitionSpec as P

MESH = pl.DeviceIdType.MESH
BF, F32 = jnp.bfloat16, jnp.float32
HEADS = 12
D = 768
FF = 3072
ROWS = 256
TOP = 48
epsilon = 1e-05
SCALE = 0.125

LN1G, LN1S, BQV, BOUT, LN2G, LN2S, BUP, BDOWN = 0, 1, 2, 4, 5, 6, 7, 11

ORDERS = ((0, 1, 2), (1, 2, 0), (2, 0, 1))
NMSG = 31
A = pl.ds(0, 768)
B = pl.ds(768, 768)


def mm(a, b):
    return jnp.dot(a, b, preferred_element_type=F32)


def mm_nt(a, b):
    return lax.dot_general(a, b, (((1,), (1,)), ((), ())), preferred_element_type=F32)


def mm_tn(a, b):
    return lax.dot_general(a, b, (((0,), (0,)), ((), ())), preferred_element_type=F32)


def normalise(v):
    mu = jnp.sum(v, -1, keepdims=True) * (1.0 / D)
    c = v - mu
    var = jnp.sum(c * c, -1, keepdims=True) * (1.0 / D)
    rs = lax.rsqrt(var + epsilon)
    return c * rs, rs


def normalise_back(grad, gain, xhat, rs):
    gy = grad * gain
    m1 = jnp.sum(gy, -1, keepdims=True) * (1.0 / D)
    m2 = jnp.sum(gy * xhat, -1, keepdims=True) * (1.0 / D)
    return rs * (gy - m1 - xhat * m2)


def gelu_both(u):
    k = 0.7978845608028654
    u2 = u * u
    th = jnp.tanh(k * u * (1.0 + 0.044715 * u2))
    half = 0.5 * (1.0 + th)
    return u * half, half + 0.5 * u * (1.0 - th * th) * (k * (1.0 + 3 * 0.044715 * u2))


def eights(v):
    return jnp.sum(v.reshape(v.shape[0] // 8, 8, v.shape[1]), 0)


def column_sum(v):
    return jnp.sum(eights(v), 0, keepdims=True)


def coords():
    b = lax.axis_index("batch")
    y = lax.axis_index("pass")
    core = b % 2
    z = (b // 2) % 4
    x = b // 8
    return (x, y, z), core


def device(pos, core):
    x, y, z = pos
    return ((x * 4 + z) * 2 + core, y)


def along(pos, axis, by):
    return tuple((c + by) % 4 if i == axis else c for i, c in enumerate(pos))


def iota(shape, dim):
    return lax.broadcasted_iota(jnp.int32, shape, dim)


def lane_heads(v, rows):
    head = iota((rows, D), 1) // 64
    zero = jnp.zeros((rows, D), v.dtype)
    return jnp.concatenate([jnp.where(head == h, v, zero) for h in range(HEADS)], 0)


def join_heads(v, rows):
    head = iota((rows, D), 1) // 64
    total = jnp.zeros((rows, D), F32)
    for h in range(HEADS):
        total = jnp.where(head == h, v[h * rows : (h + 1) * rows], total)
    return total


def pair_rows(v):
    left = iota((128, 128), 1) < 64
    zero = jnp.zeros((128, 128), v.dtype)
    return jnp.concatenate([jnp.where(left, v, zero), jnp.where(left, zero, v)], 0)


def pair_join(v):
    left = iota((128, 128), 1) < 64
    return jnp.where(left, v[:128], v[128:])


SCRATCH = dict(
    x_v=((ROWS, D), BF),
    wq=((D, 3 * D), BF), wo=((D, D), BF), wu=((D, FF), BF), wd=((FF, D), BF),
    par=((16, D), F32),
    xh1=((ROWS, D), F32), rs1=((ROWS, 1), F32), qkv=((ROWS, 3 * D), BF),
    prob=((12, 256, 128), F32), res=((ROWS, D), F32), xh2=((ROWS, D), F32), rs2=((ROWS, 1), F32),
    gp=((ROWS, FF), F32), act=((ROWS, FF), BF),
    tmp=((ROWS, D), F32), dmix=((ROWS, D), BF),
    du=((ROWS, FF), BF), da=((ROWS, D), BF), dqkv=((ROWS, 3 * D), BF), sums=((16, D), F32),
    xm=((4, 16, D), F32), xh1m=((4, 16, D), F32), rs1m=((4, 16, 1), F32), qkvm=((4, 16, 3 * D), BF),
    kall=((3, 128, D), BF), vall=((3, 128, D), BF), pm=((3, 192, 128), F32),
    xh2m=((3, 16, D), F32), rs2m=((3, 16, 1), F32), gpm=((3, 16, FF), F32),
    slots=((4, 16, D), BF), slot_out=((16, D), BF),
    e_own=((16, D), BF), du_own=((16, FF), BF), da_own=((16, D), BF), dqkv_own=((80, 3 * D), BF),
    dx_mini=((16, D), F32), dxm_own=((16, D), BF), dxb_own=((64, D), F32),
    f_n1=((512, D), BF), f_o=((512, D), BF), f_n2=((512, D), BF), f_dh=((512, D), BF),
    f_qo=((512, 1536), BF), f_du=((512, 1536), BF), f_act=((512, 1536), BF),
    w1=((3, 768, 1536), BF), relay1=((3, 2, 192, 768), BF), in1=((3, 2, 192, 1536), BF),
    w2=((3, 192, 1536), BF), relay2=((3, 2, 48, 768), BF), in2=((3, 2, 48, 1536), BF),
    w3=((3, 4, 48, 384), BF), in3=((3, 3, 48, 384), BF), fin=((3, 48, 384), BF),
    own=((4, 64, D), BF), own_in=((3, 64, D), BF), own_sum=((64, D), BF),
    small_in=((10, 16, D), F32),
)
NAMES = list(SCRATCH)


def kernel(start_ref, length_ref, x_hbm, cot_hbm, par_hbm, wq_hbm, wo_hbm, wu_hbm, wd_hbm,
           act_out, own_out, small_out, out_ref, *scratch):
    r = dict(zip(NAMES, scratch))
    lsem, fsem, frem, ssem, rsem, xs_send, xs_recv = scratch[len(NAMES):]
    g = type("Refs", (), r)
    g.dx, g.dres, g.dn1, g.out_act = g.res, g.tmp, g.xh2, g.x_v
    g.cot_v = g.f_dh.at[pl.ds(0, 256)]
    pos, core = coords()
    me = pos[1]
    sibling = device(pos, 1 - core)

    barrier = pltpu.get_barrier_semaphore()
    for axis in range(3):
        for by in (1, 2, 3):
            pl.semaphore_signal(barrier, inc=1, device_id=device(along(pos, axis, by), core), device_id_type=MESH)
    pl.semaphore_signal(barrier, inc=1, device_id=sibling, device_id_type=MESH)

    loads = [
        pltpu.make_async_copy(src, dst, lsem.at[i])
        for i, (src, dst) in enumerate(
            ((x_hbm, g.x_v), (par_hbm, g.par), (wq_hbm, g.wq), (wo_hbm, g.wo), (wu_hbm, g.wu), (wd_hbm, g.wd), (cot_hbm, g.cot_v))
        )
    ]
    for c in loads:
        c.start()

    def row(i, n=1):
        if n == 1:
            return g.par[i : i + 1, :]
        return jnp.concatenate([g.par[i + k : i + k + 1, :] for k in range(n)], 1)

    s0, s1 = start_ref[0], start_ref[1]
    n0, n1 = length_ref[0], length_ref[1]
    r16 = iota((16, 256), 0)
    want = jnp.where(r16 < 8, s0 - 1 + r16, 128 + s1 - 1 + r16 - 8)
    pick = (iota((16, 256), 1) == want).astype(BF)
    col16 = iota((TOP, 16), 1)
    row48 = iota((TOP, 16), 0)
    place = []
    place_slots = []
    for q, s in ((0, s0), (1, s1)):
        i = col16 - 8 * q
        hit = (i >= 0) & (i < 8) & (row48 == s - 1 + i)
        place.append(hit.astype(BF))
        place_slots.append((hit & (i >= 1) & (i <= 6)).astype(BF))

    def is_slot(s, rows):
        j = iota((rows, 1), 0)
        return (j >= s) & (j < s + 6)

    loads[0].wait()
    loads[1].wait()

    def norm_one(i, _):
        rows = pl.ds(pl.multiple_of(i * 32, 32), 32)
        xhat, rs = normalise(g.x_v[rows, :].astype(F32))
        g.xh1[rows, :] = xhat
        g.rs1[rows, :] = rs
        g.f_n1[rows, :] = (xhat * row(LN1G) + row(LN1S)).astype(BF)
        return 0

    lax.fori_loop(0, 8, norm_one, 0)
    loads[2].wait()
    qkv_bias = (row(BQV), jnp.zeros((1, D), F32), row(BQV + 1))
    for k in range(3):
        c = slice(k * D, (k + 1) * D)
        g.qkv[:, c] = (mm(g.f_n1[0:256, :], g.wq[:, c]) + qkv_bias[k]).astype(BF)

    xm = mm(pick, g.x_v[...])
    g.xm[0] = xm
    xhat, rs = normalise(xm)
    g.xh1m[0] = xhat
    g.rs1m[0] = rs
    g.qkvm[0] = mm(pick, g.qkv[...]).astype(BF)
    for t in range(3):
        for buf, lane in ((g.kall, D), (g.vall, 2 * D)):
            buf[t, 0:32, :] = g.qkv[0:32, lane : lane + D]
            buf[t, 32:64, :] = g.qkv[128:160, lane : lane + D]
            buf[t, 80:128, :] = jnp.zeros((48, D), BF)
    for c in loads[3:6]:
        c.wait()

    rr = iota((192, 128), 0) % 16
    cc = iota((192, 128), 1)
    rq, ri = rr // 8, rr % 8
    base_ok = (cc < 64) & (cc // 32 == rq) & (cc % 32 < jnp.where(rq == 0, s0, s1))
    mi = cc - 64
    mini_ok = (mi >= 0) & (mi < 16) & (mi // 8 == rq) & (mi % 8 >= 1) & (mi % 8 <= ri)
    mini_allowed = base_ok | mini_ok
    mini_first = iota((16, D), 0) % 8 == 0

    def thought(t, _):
        g.kall[t, 64:80, :] = g.qkvm[t, :, D : 2 * D]
        g.vall[t, 64:80, :] = g.qkvm[t, :, 2 * D : 3 * D]
        s = mm_nt(lane_heads(g.qkvm[t, :, 0:D], 16), g.kall[t]) * SCALE
        s = jnp.where(mini_allowed, s, -1e30)
        e = jnp.exp(s - jnp.max(s, -1, keepdims=True))
        p = e / jnp.sum(e, -1, keepdims=True)
        g.pm[t] = p
        o = join_heads(mm(p.astype(BF), g.vall[t]), 16).astype(BF)
        res = g.xm[t] + mm(o, g.wo[...]) + row(BOUT)
        xhat, rs = normalise(res)
        g.xh2m[t] = xhat
        g.rs2m[t] = rs
        n2 = (xhat * row(LN2G) + row(LN2S)).astype(BF)
        parts = []
        for k in range(2):
            u = mm(n2, g.wu[:, k * 1536 : (k + 1) * 1536]) + row(BUP + 2 * k, 2)
            m, slope = gelu_both(u)
            g.gpm[t, :, k * 1536 : (k + 1) * 1536] = slope
            parts.append(m.astype(BF))
        h = res + mm(jnp.concatenate(parts, 1), g.wd[...]) + row(BDOWN)
        h = h.astype(BF).astype(F32)
        nxt = jnp.where(mini_first, g.xm[t], pltpu.roll(h, 1, 0))
        g.xm[t + 1] = nxt
        xhat, rs = normalise(nxt)
        g.xh1m[t + 1] = xhat
        g.rs1m[t + 1] = rs
        n1 = (xhat * row(LN1G) + row(LN1S)).astype(BF)
        for k in range(3):
            c = slice(k * D, (k + 1) * D)
            g.qkvm[t + 1, :, c] = (mm(n1, g.wq[:, c]) + qkv_bias[k]).astype(BF)
        return 0

    lax.fori_loop(0, 3, thought, 0)

    for q, s in ((0, s0), (1, s1)):
        rows = slice(128 * q, 128 * q + TOP)
        slot = is_slot(s, TOP)
        x = jnp.where(slot, mm(place_slots[q], g.xm[me].astype(BF)), g.x_v[rows, :].astype(F32))
        g.x_v[rows, :] = x.astype(BF)
        xhat, rs = normalise(x)
        g.xh1[rows, :] = xhat
        g.rs1[rows, :] = rs
        g.f_n1[rows, :] = (xhat * row(LN1G) + row(LN1S)).astype(BF)
        g.qkv[rows, :] = jnp.where(slot, mm(place_slots[q], g.qkvm[me]), g.qkv[rows, :].astype(F32)).astype(BF)

    qi = iota((256, 128), 0) % 128
    kj = iota((256, 128), 1)

    def attend(q, _):
        rows = pl.ds(pl.multiple_of(q * 128, 128), 128)
        ok = (kj <= qi) & (kj < jnp.where(q == 0, n0, n1))
        for hp in range(6):
            lanes = slice(128 * hp, 128 * hp + 128)
            q2 = pair_rows(g.qkv[rows, lanes])
            s = mm_nt(q2, g.qkv[rows, D + 128 * hp : D + 128 * hp + 128]) * SCALE
            s = jnp.where(ok, s, -1e30)
            e = jnp.exp(s - jnp.max(s, -1, keepdims=True))
            p = e / jnp.sum(e, -1, keepdims=True)
            g.prob[q * 6 + hp] = p
            o2 = mm(p.astype(BF), g.qkv[rows, 2 * D + 128 * hp : 2 * D + 128 * hp + 128])
            g.f_o[rows, lanes] = pair_join(o2).astype(BF)
        return 0

    lax.fori_loop(0, 2, attend, 0)

    g.tmp[...] = mm(g.f_o[0:256, :], g.wo[...])

    def norm_two(i, _):
        rows = pl.ds(pl.multiple_of(i * 32, 32), 32)
        res = g.x_v[rows, :].astype(F32) + g.tmp[rows, :] + row(BOUT)
        g.res[rows, :] = res
        xhat, rs = normalise(res)
        g.xh2[rows, :] = xhat
        g.rs2[rows, :] = rs
        g.f_n2[rows, :] = (xhat * row(LN2G) + row(LN2S)).astype(BF)
        return 0

    lax.fori_loop(0, 8, norm_two, 0)
    for k in range(4):
        c = slice(k * D, (k + 1) * D)
        m, slope = gelu_both(mm(g.f_n2[0:256, :], g.wu[:, c]) + row(BUP + k))
        g.gp[:, c] = slope
        g.act[:, c] = m.astype(BF)
    g.out_act[...] = (g.res[...] + mm(g.act[...], g.wd[...]) + row(BDOWN)).astype(BF)
    act_copy = pltpu.make_async_copy(g.out_act, act_out, lsem.at[0])
    act_copy.start()

    pl.semaphore_wait(barrier, 10)
    lo, hi = pl.ds(0, 256), pl.ds(256, 256)
    started = []

    def to_sibling(i, src, dst):
        c = pltpu.make_async_remote_copy(src_ref=src, dst_ref=dst, send_sem=fsem.at[i], recv_sem=frem.at[i],
                                         device_id=sibling, device_id_type=MESH)
        c.start()
        started.append(c)
        return c

    def local(i, src, dst):
        c = pltpu.make_async_copy(src, dst, lsem.at[i])
        c.start()
        return c

    def half(ref, which, width):
        return ref.at[:, pl.ds(pl.multiple_of(which * width, 128), width)]

    n1_go = to_sibling(0, g.f_n1.at[lo], g.f_n1.at[hi])
    o_go = to_sibling(1, g.f_o.at[lo], g.f_o.at[hi])
    n2_go = to_sibling(2, g.f_n2.at[lo], g.f_n2.at[hi])
    act_go = to_sibling(3, half(g.act, 1 - core, 1536), g.f_act.at[hi])
    act_local = local(1, half(g.act, core, 1536), g.f_act.at[lo])

    loads[6].wait()
    for k in range(4):
        c = slice(k * D, (k + 1) * D)
        du = (mm_nt(g.cot_v[...], g.wd[c, :]) * g.gp[:, c]).astype(BF)
        g.du[:, c] = du
        g.sums[BUP + k : BUP + k + 1, :] = column_sum(du.astype(F32))
    g.sums[BDOWN : BDOWN + 1, :] = column_sum(g.cot_v[...].astype(F32))
    g.tmp[...] = mm_nt(g.du[...], g.wu[...])
    zero8 = jnp.zeros((8, D), F32)

    def back_two(i, acc):
        rows = pl.ds(pl.multiple_of(i * 32, 32), 32)
        dn = g.tmp[rows, :]
        xhat = g.xh2[rows, :]
        dres = g.cot_v[rows, :].astype(F32) + normalise_back(dn, row(LN2G), xhat, g.rs2[rows, :])
        g.dres[rows, :] = dres
        da = dres.astype(BF)
        g.da[rows, :] = da
        return acc[0] + eights(dn * xhat), acc[1] + eights(dn), acc[2] + eights(da.astype(F32))

    acc = lax.fori_loop(0, 8, back_two, (zero8, zero8, zero8))
    for i, a in zip((LN2G, LN2S, BOUT), acc):
        g.sums[i : i + 1, :] = jnp.sum(a, 0, keepdims=True)
    g.dmix[...] = mm_nt(g.da[...], g.wo[...]).astype(BF)

    def attend_back(q, _):
        rows = pl.ds(pl.multiple_of(q * 128, 128), 128)
        for hp in range(6):
            lanes = slice(128 * hp, 128 * hp + 128)
            klanes = slice(D + 128 * hp, D + 128 * hp + 128)
            vlanes = slice(2 * D + 128 * hp, 2 * D + 128 * hp + 128)
            do2 = pair_rows(g.dmix[rows, lanes])
            p = g.prob[q * 6 + hp]
            dp = mm_nt(do2, g.qkv[rows, vlanes])
            ds = (p * (dp - jnp.sum(p * dp, -1, keepdims=True))).astype(BF)
            g.dqkv[rows, lanes] = (pair_join(mm(ds, g.qkv[rows, klanes])) * SCALE).astype(BF)
            g.dqkv[rows, klanes] = (mm_tn(ds, pair_rows(g.qkv[rows, lanes])) * SCALE).astype(BF)
            g.dqkv[rows, vlanes] = mm_tn(p.astype(BF), do2).astype(BF)
        return 0

    lax.fori_loop(0, 2, attend_back, 0)
    g.dn1[...] = mm_nt(g.dqkv[...], g.wq[...])

    def back_one(i, acc):
        rows = pl.ds(pl.multiple_of(i * 32, 32), 32)
        dn = g.dn1[rows, :]
        xhat = g.xh1[rows, :]
        g.dx[rows, :] = g.dres[rows, :] + normalise_back(dn, row(LN1G), xhat, g.rs1[rows, :])
        dq = eights(g.dqkv[rows, 0:D].astype(F32))
        dv = eights(g.dqkv[rows, 2 * D : 3 * D].astype(F32))
        return acc[0] + eights(dn * xhat), acc[1] + eights(dn), acc[2] + dq, acc[3] + dv

    acc = lax.fori_loop(0, 8, back_one, (zero8, zero8, zero8, zero8))
    for i, a in zip((LN1G, LN1S, BQV, BQV + 1), acc):
        g.sums[i : i + 1, :] = jnp.sum(a, 0, keepdims=True)

    g.slot_out[...] = mm(pick, g.dx[...].astype(BF)).astype(BF)
    for by in (1, 2, 3):
        c = pltpu.make_async_remote_copy(
            src_ref=g.slot_out, dst_ref=g.slots.at[me], send_sem=xs_send.at[by - 1], recv_sem=xs_recv.at[by - 1],
            device_id=device(along(pos, 1, by), core), device_id_type=MESH)
        c.start()
        started.append(c)
    g.dx_mini[...] = jnp.zeros((16, D), F32)
    g.e_own[...] = jnp.zeros((16, D), BF)
    g.du_own[...] = jnp.zeros((16, FF), BF)
    g.da_own[...] = jnp.zeros((16, D), BF)
    g.dqkv_own[...] = jnp.zeros((80, 3 * D), BF)
    g.dxm_own[...] = jnp.zeros((16, D), BF)
    g.dxb_own[...] = jnp.zeros((64, D), F32)
    for by in (1, 2, 3):
        src = (me + 4 - by) % 4
        pltpu.make_async_remote_copy(
            src_ref=g.slot_out, dst_ref=g.slots.at[src], send_sem=xs_send.at[by - 1], recv_sem=xs_recv.at[by - 1],
            device_id=device(along(pos, 1, by), core), device_id_type=MESH).wait_recv()
    keep = iota((16, D), 0) % 8 <= 5

    def thought_back(i, _):
        t = 2 - i

        @pl.when(t >= me)
        def _():
            e = (g.slots[t + 1].astype(F32) + g.dx_mini[...]).astype(BF).astype(F32)
            e = jnp.where(keep, pltpu.roll(e, 15, 0), 0.0)
            eb = e.astype(BF)
            parts = []
            for k in range(2):
                dm = mm_nt(eb, g.wd[k * 1536 : (k + 1) * 1536, :])
                parts.append((dm * g.gpm[t, :, k * 1536 : (k + 1) * 1536]).astype(BF))
            du = jnp.concatenate(parts, 1)
            dn2 = mm_nt(du, g.wu[...])
            xhat2 = g.xh2m[t]
            dres = e + normalise_back(dn2, row(LN2G), xhat2, g.rs2m[t])
            da = dres.astype(BF)
            dmix = mm_nt(da, g.wo[...]).astype(BF)
            do_s = lane_heads(dmix, 16)
            q_s = lane_heads(g.qkvm[t, :, 0:D], 16)
            p = g.pm[t]
            dp = mm_nt(do_s, g.vall[t])
            ds = (p * (dp - jnp.sum(p * dp, -1, keepdims=True))).astype(BF)
            dq = (join_heads(mm(ds, g.kall[t]), 16) * SCALE).astype(BF)
            dk = (mm_tn(ds, q_s)[0:80] * SCALE).astype(BF)
            dv = mm_tn(p.astype(BF), do_s)[0:80].astype(BF)
            dq = jnp.concatenate([jnp.zeros((64, D), BF), dq], 0)
            dqkv = jnp.concatenate([dq, dk, dv], 1)
            dn1 = mm_nt(dqkv, g.wq[...])
            gain = row(LN1G)
            xhat1 = g.xh1m[t]
            dxm = dres + normalise_back(dn1[64:80], gain, xhat1, g.rs1m[t])
            g.dx_mini[...] = dxm

            @pl.when(t == me)
            def _():
                g.e_own[...] = eb
                g.du_own[...] = du
                g.da_own[...] = da
                g.dqkv_own[...] = dqkv
                g.dxm_own[...] = dxm.astype(BF)
                total = {}
                b0, b1 = g.xh1[0:32, :], g.xh1[128:160, :]
                g.dxb_own[0:32, :] = normalise_back(dn1[0:32], gain, b0, g.rs1[0:32, :])
                g.dxb_own[32:64, :] = normalise_back(dn1[32:64], gain, b1, g.rs1[128:160, :])
                total[LN1G] = column_sum(dn1[0:32] * b0) + column_sum(dn1[32:64] * b1) + column_sum(dn1[64:80] * xhat1)
                total[LN1S] = column_sum(dn1)
                total[BQV] = column_sum(dq.astype(F32))
                total[BQV + 1] = column_sum(dv.astype(F32))
                total[BOUT] = column_sum(da.astype(F32))
                total[LN2G] = column_sum(dn2 * xhat2)
                total[LN2S] = column_sum(dn2)
                total[BDOWN] = column_sum(e)
                for i, v in total.items():
                    g.sums[i : i + 1, :] += v
                for k in range(4):
                    g.sums[BUP + k : BUP + k + 1, :] += column_sum(du[:, k * D : (k + 1) * D].astype(F32))

        return 0

    lax.fori_loop(0, 3, thought_back, 0)

    top = [slice(128 * q, 128 * q + TOP) for q in range(2)]

    def merge(into, own, q):
        into[top[q], :] = (into[top[q], :].astype(F32) + mm(place[q], own[...])).astype(BF)

    for q in range(2):
        merge(g.cot_v, g.e_own, q)
    dh_go = to_sibling(4, g.cot_v, g.f_dh.at[hi])
    for q in range(2):
        merge(g.du, g.du_own, q)
    du_go = to_sibling(5, half(g.du, 1 - core, 1536), g.f_du.at[hi])
    du_local = local(3, half(g.du, core, 1536), g.f_du.at[lo])
    for q in range(2):
        merge(g.da, g.da_own, q)
        base = jnp.concatenate([g.dqkv_own[32 * q : 32 * q + 32, :].astype(F32), jnp.zeros((16, 3 * D), F32)], 0)
        g.dqkv[top[q], :] = (g.dqkv[top[q], :].astype(F32) + mm(place[q], g.dqkv_own[64:80, :]) + base).astype(BF)
    dq_go = to_sibling(6, half(g.dqkv, 1 - core, 1152), g.f_qo.at[hi, pl.ds(0, 1152)])
    dq_local = local(4, half(g.dqkv, core, 1152), g.f_qo.at[lo, pl.ds(0, 1152)])
    da_go = to_sibling(7, half(g.da, 1 - core, 384), g.f_qo.at[hi, pl.ds(1152, 384)])
    da_local = local(5, half(g.da, core, 384), g.f_qo.at[lo, pl.ds(1152, 384)])
    later = (me > 0).astype(F32)
    for q, s in ((0, s0), (1, s1)):
        dx = g.dx[top[q], :] + mm(place[q], g.dxm_own[...])
        dx = dx + jnp.concatenate([g.dxb_own[32 * q : 32 * q + 32, :], jnp.zeros((16, D), F32)], 0)
        dx = dx * (1.0 - later * is_slot(s, TOP).astype(F32))
        g.dx[top[q], :] = dx
    for k in range(4):
        g.own[k] = g.dx[64 * k : 64 * k + 64, :].astype(BF)

    def msg(p, m, src, dst, to):
        return pltpu.make_async_remote_copy(src_ref=src, dst_ref=dst, send_sem=ssem.at[p, m], recv_sem=rsem.at[p, m],
                                            device_id=to, device_id_type=MESH)

    def send(p, m, src, dst, to):
        c = msg(p, m, src, dst, to)
        c.start()
        started.append(c)

    def arrived(p, m, dst):
        msg(p, m, dst, dst, sibling).wait_recv()

    stages = ((g.w1, g.relay1, g.in1, 192), (g.w2, g.relay2, g.in2, 48))

    def ring(p, phase):
        axis = ORDERS[p][phase]
        i = pos[axis]
        return i, device(along(pos, axis, 1), core), device(along(pos, axis, 3), core)

    def rs_a(p, phase):
        i, up, dn = ring(p, phase)
        w, relay, inn, n = stages[phase]
        b = 6 * phase

        def blk(k):
            return pl.ds(pl.multiple_of(((i + k) % 4) * n, 16), n)

        send(p, b + 0, w.at[p, blk(2), A], relay.at[p, 0], up)
        send(p, b + 1, w.at[p, blk(2), B], relay.at[p, 1], dn)
        send(p, b + 2, w.at[p, blk(1), B], inn.at[p, 0, :, B], up)
        send(p, b + 3, w.at[p, blk(3), A], inn.at[p, 1, :, A], dn)

    def rs_b(p, phase):
        i, up, dn = ring(p, phase)
        w, relay, inn, n = stages[phase]
        b = 6 * phase
        for side, by, cols, to in ((0, 1, A, up), (1, 3, B, dn)):
            first = ((i + by) % 4) * n
            arrived(p, b + side, relay.at[p, side])

            def add(j, _):
                s = pl.ds(pl.multiple_of(j * 16, 16), 16)
                t = pl.ds(pl.multiple_of(first + j * 16, 16), 16)
                relay[p, side, s, :] = (relay[p, side, s, :].astype(F32) + w[p, t, cols].astype(F32)).astype(BF)
                return 0

            lax.fori_loop(0, n // 16, add, 0)
            send(p, b + 4 + side, relay.at[p, side], inn.at[p, side, :, cols], to)

    def rs_c(p, phase):
        i, up, dn = ring(p, phase)
        w, relay, inn, n = stages[phase]
        b = 6 * phase
        arrived(p, b + 2, inn.at[p, 0, :, B])
        arrived(p, b + 3, inn.at[p, 1, :, A])
        arrived(p, b + 4, inn.at[p, 0, :, A])
        arrived(p, b + 5, inn.at[p, 1, :, B])

        def add(j, _):
            s = pl.ds(pl.multiple_of(j * 16, 16), 16)
            t = pl.ds(pl.multiple_of(i * n + j * 16, 16), 16)
            v = (w[p, t, :].astype(F32) + inn[p, 0, s, :].astype(F32) + inn[p, 1, s, :].astype(F32)).astype(BF)
            if phase == 0:
                g.w2[p, s, :] = v
            else:
                for k in range(4):
                    g.w3[p, k, s, :] = v[:, 384 * k : 384 * k + 384]
            return 0

        lax.fori_loop(0, n // 16, add, 0)

    def spot(p, c1, c2=None, c3=None, cols=None, c=None):
        o = out_ref.at[core if c is None else c, p]
        if c2 is None:
            rows = pl.ds(pl.multiple_of(192 * c1, 16), 192)
        else:
            rows = pl.ds(pl.multiple_of(192 * c1 + 48 * c2, 16), 48)
        if c3 is not None:
            cols = pl.ds(pl.multiple_of(384 * c3, 128), 384)
        return o.at[rows] if cols is None else o.at[rows, cols]

    def where(p):
        return tuple(pos[a] for a in ORDERS[p])

    def rs3_a(p):
        axis = ORDERS[p][2]
        for d in (1, 2, 3):
            send(p, 11 + d, g.w3.at[p, (pos[axis] + d) % 4], g.in3.at[p, d - 1], device(along(pos, axis, d), core))

    def rs3_b(p):
        axis = ORDERS[p][2]
        for d in (1, 2, 3):
            arrived(p, 11 + d, g.in3.at[p, d - 1])
        total = g.w3[p, pos[axis]].astype(F32)
        for d in range(3):
            total = total + g.in3[p, d].astype(F32)
        g.fin[p] = total.astype(BF)
        mine = spot(p, *where(p))
        own = pltpu.make_async_copy(g.fin.at[p], mine, lsem.at[7])
        own.start()
        for d in (1, 2, 3):
            send(p, 14 + d, g.fin.at[p], mine, device(along(pos, axis, d), core))
        own.wait()

    def ag3(p):
        c1, c2, c3 = where(p)
        for d in (1, 2, 3):
            arrived(p, 14 + d, spot(p, c1, c2, (c3 + 4 - d) % 4))

    def ag_a(p, phase):
        i, up, dn = ring(p, phase)
        c1, c2, _ = where(p)
        b = 18 if phase == 1 else 22
        mine = spot(p, c1, c2) if phase == 1 else spot(p, c1)
        send(p, b, mine, mine, up)
        send(p, b + 1, mine, mine, dn)
        if phase == 0:
            send(p, 26, mine, mine, sibling)

    def turned(p, phase):
        c1, c2, _ = where(p)

        def sp(d, cols=None):
            return spot(p, c1, (c2 + d) % 4, cols=cols) if phase == 1 else spot(p, (c1 + d) % 4, cols=cols)

        return sp

    def ag_b(p, phase):
        i, up, dn = ring(p, phase)
        b = 18 if phase == 1 else 22
        sp = turned(p, phase)
        arrived(p, b, sp(3))
        send(p, b + 2, sp(3, A), sp(3, A), up)
        if phase == 0:
            send(p, 27, sp(3), sp(3), sibling)
        arrived(p, b + 1, sp(1))
        send(p, b + 3, sp(1, B), sp(1, B), dn)
        if phase == 0:
            send(p, 28, sp(1), sp(1), sibling)

    def ag_c(p, phase):
        b = 18 if phase == 1 else 22
        sp = turned(p, phase)
        arrived(p, b + 2, sp(2, A))
        if phase == 0:
            send(p, 29, sp(2, A), sp(2, A), sibling)
        arrived(p, b + 3, sp(2, B))
        if phase == 0:
            send(p, 30, sp(2, B), sp(2, B), sibling)

    def sib(p):
        c1 = where(p)[0]

        def sp(d, cols=None):
            return spot(p, (c1 + d) % 4, cols=cols, c=1 - core)

        arrived(p, 26, sp(0))
        arrived(p, 27, sp(3))
        arrived(p, 28, sp(1))
        arrived(p, 29, sp(2, A))
        arrived(p, 30, sp(2, B))

    def own_a():
        for by in (1, 2, 3):
            c = pltpu.make_async_remote_copy(
                src_ref=g.own.at[(me + by) % 4], dst_ref=g.own_in.at[by - 1], send_sem=xs_send.at[2 + by],
                recv_sem=xs_recv.at[2 + by], device_id=device(along(pos, 1, by), core), device_id_type=MESH)
            c.start()
            started.append(c)

    def own_b():
        total = g.own[me].astype(F32)
        for by in (1, 2, 3):
            pltpu.make_async_remote_copy(
                src_ref=g.own_in.at[by - 1], dst_ref=g.own_in.at[by - 1], send_sem=xs_send.at[2 + by],
                recv_sem=xs_recv.at[2 + by], device_id=sibling, device_id_type=MESH).wait_recv()
            total = total + g.own_in[by - 1].astype(F32)
        g.own_sum[...] = total.astype(BF)
        mine = own_out.at[pl.ds(pl.multiple_of(64 * me, 16), 64)]
        here = pltpu.make_async_copy(g.own_sum, mine, lsem.at[6])
        here.start()
        for by in (1, 2, 3):
            c = pltpu.make_async_remote_copy(
                src_ref=g.own_sum, dst_ref=mine, send_sem=xs_send.at[5 + by],
                recv_sem=xs_recv.at[5 + by], device_id=device(along(pos, 1, by), core), device_id_type=MESH)
            c.start()
            started.append(c)
        return here

    def own_c(here):
        here.wait()
        for by in (1, 2, 3):
            src = own_out.at[pl.ds(pl.multiple_of(64 * ((me + 4 - by) % 4), 16), 64)]
            pltpu.make_async_remote_copy(
                src_ref=src, dst_ref=src, send_sem=xs_send.at[5 + by],
                recv_sem=xs_recv.at[5 + by], device_id=sibling, device_id_type=MESH).wait_recv()

    def small_send(stage):
        n = 1 if stage == 0 else 3
        first = 0 if stage == 0 else 3 * stage - 2
        for k in range(n):
            to = sibling if stage == 0 else device(along(pos, stage - 1, k + 1), core)
            c = pltpu.make_async_remote_copy(
                src_ref=g.small_out_v.at[stage], dst_ref=g.small_in.at[first + k], send_sem=xs_send.at[9 + first + k],
                recv_sem=xs_recv.at[9 + first + k], device_id=to, device_id_type=MESH)
            c.start()
            started.append(c)

    def small_take(stage):
        n = 1 if stage == 0 else 3
        first = 0 if stage == 0 else 3 * stage - 2
        total = g.small_out_v[stage]
        for k in range(n):
            ref = g.small_in.at[first + k]
            pltpu.make_async_remote_copy(
                src_ref=ref, dst_ref=ref, send_sem=xs_send.at[9 + first + k],
                recv_sem=xs_recv.at[9 + first + k], device_id=sibling, device_id_type=MESH).wait_recv()
            total = total + g.small_in[first + k]
        g.small_out_v[stage + 1] = total

    g.small_out_v[0] = g.sums[...]
    small_send(0)
    act_local.wait()
    act_go.wait_recv()
    dh_go.wait_recv()
    for k in range(2):
        g.w1[2, :, 768 * k : 768 * k + 768] = mm_tn(g.f_act[:, 768 * k : 768 * k + 768], g.f_dh[...]).astype(BF)
    rs_a(2, 0)
    du_local.wait()
    du_go.wait_recv()
    n2_go.wait_recv()
    for k in range(2):
        g.w1[1, :, 768 * k : 768 * k + 768] = mm_tn(g.f_n2[...], g.f_du[:, 768 * k : 768 * k + 768]).astype(BF)
    rs_a(1, 0)
    for c in (dq_local, da_local):
        c.wait()
    for c in (dq_go, da_go, n1_go, o_go):
        c.wait_recv()
    g.w1[0, :, 1152:1536] = mm_tn(g.f_o[...], g.f_qo[:, 1152:1536]).astype(BF)
    g.w1[0, :, 0:768] = mm_tn(g.f_n1[...], g.f_qo[:, 0:768]).astype(BF)
    g.w1[0, :, 768:1152] = mm_tn(g.f_n1[...], g.f_qo[:, 768:1152]).astype(BF)
    rs_a(0, 0)
    own_a()
    small_take(0)
    small_send(1)
    T = (2, 1, 0)
    for p in T:
        rs_b(p, 0)
    small_take(1)
    small_send(2)
    for p in T:
        rs_c(p, 0)
        rs_a(p, 1)
    small_take(2)
    small_send(3)
    here = own_b()
    for p in T:
        rs_b(p, 1)
    for p in T:
        rs_c(p, 1)
        rs3_a(p)
    small_take(3)
    small_copy = pltpu.make_async_copy(g.small_out_v.at[4], small_out, lsem.at[8])
    small_copy.start()
    for p in T:
        rs3_b(p)
    own_c(here)
    for p in T:
        ag3(p)
        ag_a(p, 1)
    for p in T:
        ag_b(p, 1)
    for p in T:
        ag_c(p, 1)
        ag_a(p, 0)
    for p in T:
        ag_b(p, 0)
    for p in T:
        ag_c(p, 0)
    for p in T:
        sib(p)
    act_copy.wait()
    small_copy.wait()
    for c in started:
        c.wait_send()


SCRATCH["small_out_v"] = ((5, 16, D), F32)
NAMES.append("small_out_v")


def passes(starts, lengths, x, cot, par, wq, wo, wu, wd):
    smem = pl.BlockSpec(memory_space=pltpu.SMEM)
    hbm = pl.BlockSpec(memory_space=pl.ANY)
    dma = pltpu.SemaphoreType.DMA
    return pl.pallas_call(
        kernel,
        out_shape=[
            jax.ShapeDtypeStruct((ROWS, D), BF),
            jax.ShapeDtypeStruct((ROWS, D), BF),
            jax.ShapeDtypeStruct((16, D), F32),
            jax.ShapeDtypeStruct((2, 3, 768, 1536), BF),
        ],
        in_specs=[smem, smem] + [hbm] * 7,
        out_specs=[hbm] * 4,
        scratch_shapes=[pltpu.VMEM(s, t) for s, t in SCRATCH.values()]
        + [dma((9,)), dma((8,)), dma((8,)), dma((3, NMSG)), dma((3, NMSG)), dma((19,)), dma((19,))],
        compiler_params=pltpu.CompilerParams(
            collective_id=0, has_side_effects=True, vmem_limit_bytes=60 * 2**20
        ),
        name="passes",
    )(starts, lengths, x, cot, par, wq, wo, wu, wd)


def widen_kernel(all_ref, gq, go, gu, gd):
    for c in range(2):
        gq[:, 1152 * c : 1152 * c + 1152] = all_ref[c, 0, :, 0:1152].astype(F32)
        go[:, 384 * c : 384 * c + 384] = all_ref[c, 0, :, 1152:1536].astype(F32)
        gu[:, 1536 * c : 1536 * c + 1536] = all_ref[c, 1].astype(F32)
        for k in range(2):
            gd[2 * c + k] = all_ref[c, 2, :, 768 * k : 768 * k + 768].astype(F32)


def widen(gathered):
    n = 96
    return pl.pallas_call(
        widen_kernel,
        grid=(768 // n,),
        in_specs=[pl.BlockSpec((2, 3, n, 1536), lambda i: (0, 0, i, 0))],
        out_specs=[
            pl.BlockSpec((n, 2304), lambda i: (i, 0)),
            pl.BlockSpec((n, 768), lambda i: (i, 0)),
            pl.BlockSpec((n, 3072), lambda i: (i, 0)),
            pl.BlockSpec((4, n, 768), lambda i: (0, i, 0)),
        ],
        out_shape=[
            jax.ShapeDtypeStruct((768, 2304), F32),
            jax.ShapeDtypeStruct((768, 768), F32),
            jax.ShapeDtypeStruct((768, 3072), F32),
            jax.ShapeDtypeStruct((4, 768, 768), F32),
        ],
        compiler_params=pltpu.CompilerParams(vmem_limit_bytes=40 * 2**20),
        name="widen",
    )(gathered)


def on_device(embedded, cotangent, lengths, starts, ln1_gain, ln1_shift, w_qkv, b_qv, w_out, b_out,
              ln2_gain, ln2_shift, w_up, b_up, w_down, b_down):
    par = jnp.concatenate(
        [ln1_gain, ln1_shift, b_qv, b_out, ln2_gain, ln2_shift, b_up, b_down, jnp.zeros((4 * D,), F32)]
    ).reshape(16, D)
    act, own, small, gathered = passes(
        starts, lengths, embedded.reshape(ROWS, D), cotangent.reshape(ROWS, D), par, w_qkv, w_out, w_up, w_down
    )
    gq, go, gu, gd = widen(gathered)
    return (
        act.reshape(1, 2, 128, D),
        own.reshape(2, 128, D),
        small[LN1G],
        small[LN1S],
        gq,
        small[BQV : BQV + 2].reshape(2 * D),
        go,
        small[BOUT],
        small[LN2G],
        small[LN2S],
        gu,
        small[BUP : BUP + 4].reshape(FF),
        gd.reshape(FF, D),
        small[BDOWN],
    )


def solution(mesh):
    rows = P("batch", None, None)
    passes_rows = P("pass", "batch", None, None)
    return jax.shard_map(
        on_device,
        mesh=mesh,
        in_specs=(rows, passes_rows, P("batch"), P("batch")) + (P(),) * 12,
        out_specs=(passes_rows, rows) + (P(),) * 12,
        check_vma=False,
    )
```

```python
import functools

import jax
import jax.numpy as jnp
from jax import lax
from jax.experimental import pallas as pl
from jax.experimental.pallas import tpu as pltpu
from jax.sharding import PartitionSpec as P

MESH = pl.DeviceIdType.MESH
BF, F32 = jnp.bfloat16, jnp.float32
HEADS = 12
D = 768
FF = 3072
ROWS = 256
TOP = 48
epsilon = 1e-05
SCALE = 0.125

LN1G, LN1S, BQV, BOUT, LN2G, LN2S, BUP, BDOWN = 0, 1, 2, 4, 5, 6, 7, 11

ORDERS = ((0, 1, 2), (1, 2, 0), (2, 0, 1))
NMSG = 30
WAVES = 3
SHAPES = ((512, 768), (768, 512), (768, 512))
SUBS = ((16, 384), (48, 128), (48, 128))


def mm(a, b):
    return jnp.dot(a, b, preferred_element_type=F32)


def mm_nt(a, b):
    return lax.dot_general(a, b, (((1,), (1,)), ((), ())), preferred_element_type=F32)


def mm_tn(a, b):
    return lax.dot_general(a, b, (((0,), (0,)), ((), ())), preferred_element_type=F32)


def normalise(v):
    mu = jnp.sum(v, -1, keepdims=True) * (1.0 / D)
    c = v - mu
    var = jnp.sum(c * c, -1, keepdims=True) * (1.0 / D)
    rs = lax.rsqrt(var + epsilon)
    return c * rs, rs


def normalise_back(grad, gain, xhat, rs):
    gy = grad * gain
    m1 = jnp.sum(gy, -1, keepdims=True) * (1.0 / D)
    m2 = jnp.sum(gy * xhat, -1, keepdims=True) * (1.0 / D)
    return rs * (gy - m1 - xhat * m2)


def gelu_both(u):
    k = 0.7978845608028654
    u2 = u * u
    th = jnp.tanh(k * u * (1.0 + 0.044715 * u2))
    half = 0.5 * (1.0 + th)
    return u * half, half + 0.5 * u * (1.0 - th * th) * (k * (1.0 + 3 * 0.044715 * u2))


def eights(v):
    return jnp.sum(v.reshape(v.shape[0] // 8, 8, v.shape[1]), 0)


def column_sum(v):
    return jnp.sum(eights(v), 0, keepdims=True)


def coords():
    b = lax.axis_index("batch")
    y = lax.axis_index("pass")
    core = b % 2
    z = (b // 2) % 4
    x = b // 8
    return (x, y, z), core


def device(pos, core):
    x, y, z = pos
    return ((x * 4 + z) * 2 + core, y)


def along(pos, axis, by):
    return tuple((c + by) % 4 if i == axis else c for i, c in enumerate(pos))


def iota(shape, dim):
    return lax.broadcasted_iota(jnp.int32, shape, dim)


def lane_heads(v, rows):
    head = iota((rows, D), 1) // 64
    zero = jnp.zeros((rows, D), v.dtype)
    return jnp.concatenate([jnp.where(head == h, v, zero) for h in range(HEADS)], 0)


def join_heads(v, rows):
    head = iota((rows, D), 1) // 64
    total = jnp.zeros((rows, D), F32)
    for h in range(HEADS):
        total = jnp.where(head == h, v[h * rows : (h + 1) * rows], total)
    return total


def pair_rows(v):
    left = iota((128, 128), 1) < 64
    zero = jnp.zeros((128, 128), v.dtype)
    return jnp.concatenate([jnp.where(left, v, zero), jnp.where(left, zero, v)], 0)


def pair_join(v):
    left = iota((128, 128), 1) < 64
    return jnp.where(left, v[:128], v[128:])


SCRATCH = dict(
        par=((16, D), F32),
    xh1=((ROWS, D), F32), rs1=((ROWS, 1), F32), qkv=((ROWS, 3 * D), BF),
    prob=((12, 256, 128), F32), res=((ROWS, D), F32), xh2=((ROWS, D), F32), rs2=((ROWS, 1), F32),
    gp=((ROWS, FF), F32), act=((ROWS, FF), BF),
    tmp=((ROWS, D), F32), dmix=((ROWS, D), BF),
    du=((ROWS, FF), BF), dqo=((ROWS, FF), BF), sums=((16, D), F32),
    xm=((4, 16, D), F32), xh1m=((4, 16, D), F32), rs1m=((4, 16, 1), F32), qkvm=((4, 16, 3 * D), BF),
    kall=((3, 128, D), BF), vall=((3, 128, D), BF), pm=((3, 192, 128), F32),
    xh2m=((3, 16, D), F32), rs2m=((3, 16, 1), F32), gpm=((3, 16, FF), F32),
    slots=((4, 16, D), BF), slot_out=((16, D), BF),
    e_own=((16, D), BF), du_own=((16, FF), BF), da_own=((16, D), BF), dqkv_own=((80, 3 * D), BF),
    dx_mini=((16, D), F32), dxm_own=((16, D), BF), dxb_own=((64, D), F32),
    f_n1=((512, D), BF), f_o=((512, D), BF), f_n2=((512, D), BF), f_dh=((512, D), BF),
    f_qo=((512, 1536), BF), f_du=((512, 1536), BF), f_act=((512, 1536), BF),
    w1_0=((3, 512, 768), BF), w1_1=((3, 768, 512), BF), w1_2=((3, 768, 512), BF),
    relay_0=((3, 2, 128, 384), BF), relay_1=((3, 2, 192, 256), BF), relay_2=((3, 2, 192, 256), BF),
    in1_0=((3, 2, 128, 768), BF), in1_1=((3, 2, 192, 512), BF), in1_2=((3, 2, 192, 512), BF),
    w2_0=((3, 128, 768), BF), w2_1=((3, 192, 512), BF), w2_2=((3, 192, 512), BF),
    in2_0=((3, 3, 32, 768), BF), in2_1=((3, 3, 48, 512), BF), in2_2=((3, 3, 48, 512), BF),
    w3_0=((3, 32, 768), BF), w3_1=((3, 48, 512), BF), w3_2=((3, 48, 512), BF),
    in3_0=((3, 3, 16, 384), BF), in3_1=((3, 3, 48, 128), BF), in3_2=((3, 3, 48, 128), BF),
    own=((4, 64, D), BF), own_in=((3, 64, D), BF),
    small_in=((10, 16, D), F32),
)
NAMES = list(SCRATCH)


def kernel(start_ref, length_ref, x_hbm, cot_hbm, ln1g_hbm, ln1s_hbm, wq_hbm, bqv_hbm, wo_hbm, bout_hbm, ln2g_hbm, ln2s_hbm,
           wu_hbm, bup_hbm, wd_hbm, bdown_hbm, x_v, own_out, small_out, w_qo, w_u, w_d, *scratch):
    r = dict(zip(NAMES, scratch))
    lsem, fsem, frem, ssem, rsem, xs_send, xs_recv = scratch[len(NAMES):]
    g = type("Refs", (), r)
    g.x_v, g.wu, g.wd = x_v, w_u, w_d
    g.wq, g.wo = w_qo.at[:, pl.ds(0, 3 * D)], w_qo.at[:, pl.ds(3 * D, D)]
    g.dqkv, g.da = g.dqo.at[:, pl.ds(0, 3 * D)], g.dqo.at[:, pl.ds(3 * D, D)]
    g.dx, g.dres, g.dn1, g.out_act = g.res, g.tmp, g.xh2, g.x_v
    g.cot_v = g.f_dh.at[pl.ds(0, 256)]
    pos, core = coords()
    me = pos[1]
    sibling = device(pos, 1 - core)

    barrier = pltpu.get_barrier_semaphore()
    for axis in range(3):
        for by in (1, 2, 3):
            pl.semaphore_signal(barrier, inc=1, device_id=device(along(pos, axis, by), core), device_id_type=MESH)
    pl.semaphore_signal(barrier, inc=1, device_id=sibling, device_id_type=MESH)

    def load(i, src, dst):
        c = pltpu.make_async_copy(src, dst, lsem.at[i])
        c.start()
        return c

    vectors = ((ln1g_hbm, LN1G), (ln1s_hbm, LN1S), (bqv_hbm, BQV), (bout_hbm, BOUT), (ln2g_hbm, LN2G), (ln2s_hbm, LN2S),
               (bup_hbm, BUP), (bdown_hbm, BDOWN))
    x_load = load(0, x_hbm, g.x_v)
    par_loads = []
    for src, first in vectors:
        for k in range(src.shape[0] // D):
            par_loads.append(load(9 + first + k, src.at[pl.ds(k * D, D)], g.par.at[first + k]))
    wq_load = load(2, wq_hbm, g.wq)

    def row(i, n=1):
        if n == 1:
            return g.par[i : i + 1, :]
        return jnp.concatenate([g.par[i + k : i + k + 1, :] for k in range(n)], 1)

    s0, s1 = start_ref[0], start_ref[1]
    n0, n1 = length_ref[0], length_ref[1]
    r16 = iota((16, 256), 0)
    want = jnp.where(r16 < 8, s0 - 1 + r16, 128 + s1 - 1 + r16 - 8)
    pick = (iota((16, 256), 1) == want).astype(BF)
    col16 = iota((TOP, 16), 1)
    row48 = iota((TOP, 16), 0)
    place = []
    place_slots = []
    for q, s in ((0, s0), (1, s1)):
        i = col16 - 8 * q
        hit = (i >= 0) & (i < 8) & (row48 == s - 1 + i)
        place.append(hit.astype(BF))
        place_slots.append((hit & (i >= 1) & (i <= 6)).astype(BF))

    def is_slot(s, rows):
        j = iota((rows, 1), 0)
        return (j >= s) & (j < s + 6)

    x_load.wait()
    for c in par_loads:
        c.wait()

    def norm_one(i, _):
        rows = pl.ds(pl.multiple_of(i * 32, 32), 32)
        xhat, rs = normalise(g.x_v[rows, :].astype(F32))
        g.xh1[rows, :] = xhat
        g.rs1[rows, :] = rs
        g.f_n1[rows, :] = (xhat * row(LN1G) + row(LN1S)).astype(BF)
        return 0

    w_loads = [load(3, wo_hbm, g.wo), load(4, wu_hbm, g.wu), load(5, wd_hbm, g.wd)]
    cot_load = load(6, cot_hbm, g.cot_v)
    lax.fori_loop(0, 8, norm_one, 0)
    wq_load.wait()
    qkv_bias = (row(BQV), jnp.zeros((1, D), F32), row(BQV + 1))
    for k in range(3):
        c = slice(k * D, (k + 1) * D)
        g.qkv[:, c] = (mm(g.f_n1[0:256, :], g.wq[:, c]) + qkv_bias[k]).astype(BF)

    xm = mm(pick, g.x_v[...])
    g.xm[0] = xm
    xhat, rs = normalise(xm)
    g.xh1m[0] = xhat
    g.rs1m[0] = rs
    g.qkvm[0] = mm(pick, g.qkv[...]).astype(BF)
    for t in range(3):
        for buf, lane in ((g.kall, D), (g.vall, 2 * D)):
            buf[t, 0:32, :] = g.qkv[0:32, lane : lane + D]
            buf[t, 32:64, :] = g.qkv[128:160, lane : lane + D]
            buf[t, 80:128, :] = jnp.zeros((48, D), BF)
    for c in w_loads:
        c.wait()

    rr = iota((192, 128), 0) % 16
    cc = iota((192, 128), 1)
    rq, ri = rr // 8, rr % 8
    base_ok = (cc < 64) & (cc // 32 == rq) & (cc % 32 < jnp.where(rq == 0, s0, s1))
    mi = cc - 64
    mini_ok = (mi >= 0) & (mi < 16) & (mi // 8 == rq) & (mi % 8 >= 1) & (mi % 8 <= ri)
    mini_allowed = base_ok | mini_ok
    mini_first = iota((16, D), 0) % 8 == 0

    def thought(t, _):
        g.kall[t, 64:80, :] = g.qkvm[t, :, D : 2 * D]
        g.vall[t, 64:80, :] = g.qkvm[t, :, 2 * D : 3 * D]
        s = mm_nt(lane_heads(g.qkvm[t, :, 0:D], 16), g.kall[t]) * SCALE
        s = jnp.where(mini_allowed, s, -1e30)
        e = jnp.exp(s - jnp.max(s, -1, keepdims=True))
        p = e / jnp.sum(e, -1, keepdims=True)
        g.pm[t] = p
        o = join_heads(mm(p.astype(BF), g.vall[t]), 16).astype(BF)
        res = g.xm[t] + mm(o, g.wo[...]) + row(BOUT)
        xhat, rs = normalise(res)
        g.xh2m[t] = xhat
        g.rs2m[t] = rs
        n2 = (xhat * row(LN2G) + row(LN2S)).astype(BF)
        parts = []
        for k in range(2):
            u = mm(n2, g.wu[:, k * 1536 : (k + 1) * 1536]) + row(BUP + 2 * k, 2)
            m, slope = gelu_both(u)
            g.gpm[t, :, k * 1536 : (k + 1) * 1536] = slope
            parts.append(m.astype(BF))
        h = res + mm(jnp.concatenate(parts, 1), g.wd[...]) + row(BDOWN)
        h = h.astype(BF).astype(F32)
        nxt = jnp.where(mini_first, g.xm[t], pltpu.roll(h, 1, 0))
        g.xm[t + 1] = nxt
        xhat, rs = normalise(nxt)
        g.xh1m[t + 1] = xhat
        g.rs1m[t + 1] = rs
        n1 = (xhat * row(LN1G) + row(LN1S)).astype(BF)
        for k in range(3):
            c = slice(k * D, (k + 1) * D)
            g.qkvm[t + 1, :, c] = (mm(n1, g.wq[:, c]) + qkv_bias[k]).astype(BF)
        return 0

    lax.fori_loop(0, 3, thought, 0)

    for q, s in ((0, s0), (1, s1)):
        rows = slice(128 * q, 128 * q + TOP)
        slot = is_slot(s, TOP)
        x = jnp.where(slot, mm(place_slots[q], g.xm[me].astype(BF)), g.x_v[rows, :].astype(F32))
        g.x_v[rows, :] = x.astype(BF)
        xhat, rs = normalise(x)
        g.xh1[rows, :] = xhat
        g.rs1[rows, :] = rs
        g.f_n1[rows, :] = (xhat * row(LN1G) + row(LN1S)).astype(BF)
        g.qkv[rows, :] = jnp.where(slot, mm(place_slots[q], g.qkvm[me]), g.qkv[rows, :].astype(F32)).astype(BF)

    qi = iota((256, 128), 0) % 128
    kj = iota((256, 128), 1)

    def attend(q, _):
        rows = pl.ds(pl.multiple_of(q * 128, 128), 128)
        ok = (kj <= qi) & (kj < jnp.where(q == 0, n0, n1))
        for hp in range(6):
            lanes = slice(128 * hp, 128 * hp + 128)
            q2 = pair_rows(g.qkv[rows, lanes])
            s = mm_nt(q2, g.qkv[rows, D + 128 * hp : D + 128 * hp + 128]) * SCALE
            s = jnp.where(ok, s, -1e30)
            e = jnp.exp(s - jnp.max(s, -1, keepdims=True))
            p = e / jnp.sum(e, -1, keepdims=True)
            g.prob[q * 6 + hp] = p
            o2 = mm(p.astype(BF), g.qkv[rows, 2 * D + 128 * hp : 2 * D + 128 * hp + 128])
            g.f_o[rows, lanes] = pair_join(o2).astype(BF)
        return 0

    lax.fori_loop(0, 2, attend, 0)

    g.tmp[...] = mm(g.f_o[0:256, :], g.wo[...])

    def norm_two(i, _):
        rows = pl.ds(pl.multiple_of(i * 32, 32), 32)
        res = g.x_v[rows, :].astype(F32) + g.tmp[rows, :] + row(BOUT)
        g.res[rows, :] = res
        xhat, rs = normalise(res)
        g.xh2[rows, :] = xhat
        g.rs2[rows, :] = rs
        g.f_n2[rows, :] = (xhat * row(LN2G) + row(LN2S)).astype(BF)
        return 0

    lax.fori_loop(0, 8, norm_two, 0)
    for k in range(4):
        c = slice(k * D, (k + 1) * D)
        m, slope = gelu_both(mm(g.f_n2[0:256, :], g.wu[:, c]) + row(BUP + k))
        g.gp[:, c] = slope
        g.act[:, c] = m.astype(BF)
    g.out_act[...] = (g.res[...] + mm(g.act[...], g.wd[...]) + row(BDOWN)).astype(BF)

    pl.semaphore_wait(barrier, 10)
    lo, hi = pl.ds(0, 256), pl.ds(256, 256)
    started = []

    def to_sibling(i, src, dst):
        c = pltpu.make_async_remote_copy(src_ref=src, dst_ref=dst, send_sem=fsem.at[i], recv_sem=frem.at[i],
                                         device_id=sibling, device_id_type=MESH)
        c.start()
        started.append(c)
        return c

    def local(i, src, dst):
        c = pltpu.make_async_copy(src, dst, lsem.at[i])
        c.start()
        return c

    def half(ref, which, width):
        return ref.at[:, pl.ds(pl.multiple_of(which * width, 128), width)]

    n1_go = to_sibling(0, g.f_n1.at[lo], g.f_n1.at[hi])
    o_go = to_sibling(1, g.f_o.at[lo], g.f_o.at[hi])
    n2_go = to_sibling(2, g.f_n2.at[lo], g.f_n2.at[hi])
    act_go = to_sibling(3, half(g.act, 1 - core, 1536), g.f_act.at[hi])
    act_local = local(1, half(g.act, core, 1536), g.f_act.at[lo])

    cot_load.wait()
    for k in range(4):
        c = slice(k * D, (k + 1) * D)
        du = (mm_nt(g.cot_v[...], g.wd[c, :]) * g.gp[:, c]).astype(BF)
        g.du[:, c] = du
        g.sums[BUP + k : BUP + k + 1, :] = column_sum(du.astype(F32))
    g.sums[BDOWN : BDOWN + 1, :] = column_sum(g.cot_v[...].astype(F32))
    g.tmp[...] = mm_nt(g.du[...], g.wu[...])
    zero8 = jnp.zeros((8, D), F32)

    def back_two(i, acc):
        rows = pl.ds(pl.multiple_of(i * 32, 32), 32)
        dn = g.tmp[rows, :]
        xhat = g.xh2[rows, :]
        dres = g.cot_v[rows, :].astype(F32) + normalise_back(dn, row(LN2G), xhat, g.rs2[rows, :])
        g.dres[rows, :] = dres
        da = dres.astype(BF)
        g.da[rows, :] = da
        return acc[0] + eights(dn * xhat), acc[1] + eights(dn), acc[2] + eights(da.astype(F32))

    acc = lax.fori_loop(0, 8, back_two, (zero8, zero8, zero8))
    for i, a in zip((LN2G, LN2S, BOUT), acc):
        g.sums[i : i + 1, :] = jnp.sum(a, 0, keepdims=True)
    g.dmix[...] = mm_nt(g.da[...], g.wo[...]).astype(BF)

    def attend_back(q, _):
        rows = pl.ds(pl.multiple_of(q * 128, 128), 128)
        for hp in range(6):
            lanes = slice(128 * hp, 128 * hp + 128)
            klanes = slice(D + 128 * hp, D + 128 * hp + 128)
            vlanes = slice(2 * D + 128 * hp, 2 * D + 128 * hp + 128)
            do2 = pair_rows(g.dmix[rows, lanes])
            p = g.prob[q * 6 + hp]
            dp = mm_nt(do2, g.qkv[rows, vlanes])
            ds = (p * (dp - jnp.sum(p * dp, -1, keepdims=True))).astype(BF)
            g.dqkv[rows, lanes] = (pair_join(mm(ds, g.qkv[rows, klanes])) * SCALE).astype(BF)
            g.dqkv[rows, klanes] = (mm_tn(ds, pair_rows(g.qkv[rows, lanes])) * SCALE).astype(BF)
            g.dqkv[rows, vlanes] = mm_tn(p.astype(BF), do2).astype(BF)
        return 0

    lax.fori_loop(0, 2, attend_back, 0)
    g.dn1[...] = mm_nt(g.dqkv[...], g.wq[...])

    def back_one(i, acc):
        rows = pl.ds(pl.multiple_of(i * 32, 32), 32)
        dn = g.dn1[rows, :]
        xhat = g.xh1[rows, :]
        g.dx[rows, :] = g.dres[rows, :] + normalise_back(dn, row(LN1G), xhat, g.rs1[rows, :])
        dq = eights(g.dqkv[rows, 0:D].astype(F32))
        dv = eights(g.dqkv[rows, 2 * D : 3 * D].astype(F32))
        return acc[0] + eights(dn * xhat), acc[1] + eights(dn), acc[2] + dq, acc[3] + dv

    acc = lax.fori_loop(0, 8, back_one, (zero8, zero8, zero8, zero8))
    for i, a in zip((LN1G, LN1S, BQV, BQV + 1), acc):
        g.sums[i : i + 1, :] = jnp.sum(a, 0, keepdims=True)

    g.slot_out[...] = mm(pick, g.dx[...].astype(BF)).astype(BF)
    for by in (1, 2, 3):
        c = pltpu.make_async_remote_copy(
            src_ref=g.slot_out, dst_ref=g.slots.at[me], send_sem=xs_send.at[by - 1], recv_sem=xs_recv.at[by - 1],
            device_id=device(along(pos, 1, by), core), device_id_type=MESH)
        c.start()
        started.append(c)
    g.dx_mini[...] = jnp.zeros((16, D), F32)
    g.e_own[...] = jnp.zeros((16, D), BF)
    g.du_own[...] = jnp.zeros((16, FF), BF)
    g.da_own[...] = jnp.zeros((16, D), BF)
    g.dqkv_own[...] = jnp.zeros((80, 3 * D), BF)
    g.dxm_own[...] = jnp.zeros((16, D), BF)
    g.dxb_own[...] = jnp.zeros((64, D), F32)
    for by in (1, 2, 3):
        src = (me + 4 - by) % 4
        pltpu.make_async_remote_copy(
            src_ref=g.slot_out, dst_ref=g.slots.at[src], send_sem=xs_send.at[by - 1], recv_sem=xs_recv.at[by - 1],
            device_id=device(along(pos, 1, by), core), device_id_type=MESH).wait_recv()
    keep = iota((16, D), 0) % 8 <= 5

    def thought_back(i, _):
        t = 2 - i

        @pl.when(t >= me)
        def _():
            e = (g.slots[t + 1].astype(F32) + g.dx_mini[...]).astype(BF).astype(F32)
            e = jnp.where(keep, pltpu.roll(e, 15, 0), 0.0)
            eb = e.astype(BF)
            parts = []
            for k in range(2):
                dm = mm_nt(eb, g.wd[k * 1536 : (k + 1) * 1536, :])
                parts.append((dm * g.gpm[t, :, k * 1536 : (k + 1) * 1536]).astype(BF))
            du = jnp.concatenate(parts, 1)
            dn2 = mm_nt(du, g.wu[...])
            xhat2 = g.xh2m[t]
            dres = e + normalise_back(dn2, row(LN2G), xhat2, g.rs2m[t])
            da = dres.astype(BF)
            dmix = mm_nt(da, g.wo[...]).astype(BF)
            do_s = lane_heads(dmix, 16)
            q_s = lane_heads(g.qkvm[t, :, 0:D], 16)
            p = g.pm[t]
            dp = mm_nt(do_s, g.vall[t])
            ds = (p * (dp - jnp.sum(p * dp, -1, keepdims=True))).astype(BF)
            dq = (join_heads(mm(ds, g.kall[t]), 16) * SCALE).astype(BF)
            dk = (mm_tn(ds, q_s)[0:80] * SCALE).astype(BF)
            dv = mm_tn(p.astype(BF), do_s)[0:80].astype(BF)
            dq = jnp.concatenate([jnp.zeros((64, D), BF), dq], 0)
            dqkv = jnp.concatenate([dq, dk, dv], 1)
            dn1 = mm_nt(dqkv, g.wq[...])
            gain = row(LN1G)
            xhat1 = g.xh1m[t]
            dxm = dres + normalise_back(dn1[64:80], gain, xhat1, g.rs1m[t])
            g.dx_mini[...] = dxm

            @pl.when(t == me)
            def _():
                g.e_own[...] = eb
                g.du_own[...] = du
                g.da_own[...] = da
                g.dqkv_own[...] = dqkv
                g.dxm_own[...] = dxm.astype(BF)
                total = {}
                b0, b1 = g.xh1[0:32, :], g.xh1[128:160, :]
                g.dxb_own[0:32, :] = normalise_back(dn1[0:32], gain, b0, g.rs1[0:32, :])
                g.dxb_own[32:64, :] = normalise_back(dn1[32:64], gain, b1, g.rs1[128:160, :])
                total[LN1G] = column_sum(dn1[0:32] * b0) + column_sum(dn1[32:64] * b1) + column_sum(dn1[64:80] * xhat1)
                total[LN1S] = column_sum(dn1)
                total[BQV] = column_sum(dq.astype(F32))
                total[BQV + 1] = column_sum(dv.astype(F32))
                total[BOUT] = column_sum(da.astype(F32))
                total[LN2G] = column_sum(dn2 * xhat2)
                total[LN2S] = column_sum(dn2)
                total[BDOWN] = column_sum(e)
                for i, v in total.items():
                    g.sums[i : i + 1, :] += v
                for k in range(4):
                    g.sums[BUP + k : BUP + k + 1, :] += column_sum(du[:, k * D : (k + 1) * D].astype(F32))

        return 0

    lax.fori_loop(0, 3, thought_back, 0)

    top = [slice(128 * q, 128 * q + TOP) for q in range(2)]

    def merge(into, own, q):
        into[top[q], :] = (into[top[q], :].astype(F32) + mm(place[q], own[...])).astype(BF)

    for q in range(2):
        merge(g.cot_v, g.e_own, q)
    dh_go = to_sibling(4, g.cot_v, g.f_dh.at[hi])
    for q in range(2):
        merge(g.du, g.du_own, q)
    du_go = to_sibling(5, half(g.du, 1 - core, 1536), g.f_du.at[hi])
    du_local = local(3, half(g.du, core, 1536), g.f_du.at[lo])
    for q in range(2):
        merge(g.da, g.da_own, q)
        base = jnp.concatenate([g.dqkv_own[32 * q : 32 * q + 32, :].astype(F32), jnp.zeros((16, 3 * D), F32)], 0)
        g.dqkv[top[q], :] = (g.dqkv[top[q], :].astype(F32) + mm(place[q], g.dqkv_own[64:80, :]) + base).astype(BF)
    dq_go = to_sibling(6, half(g.dqo, 1 - core, 1536), g.f_qo.at[hi])
    dq_local = local(4, half(g.dqo, core, 1536), g.f_qo.at[lo])
    later = (me > 0).astype(F32)
    for q, s in ((0, s0), (1, s1)):
        dx = g.dx[top[q], :] + mm(place[q], g.dxm_own[...])
        dx = dx + jnp.concatenate([g.dxb_own[32 * q : 32 * q + 32, :], jnp.zeros((16, D), F32)], 0)
        dx = dx * (1.0 - later * is_slot(s, TOP).astype(F32))
        g.dx[top[q], :] = dx
    for k in range(4):
        g.own[k] = g.dx[64 * k : 64 * k + 64, :].astype(BF)

    def msg(w, k, m, src, dst, to):
        i = 3 * w + k
        return pltpu.make_async_remote_copy(src_ref=src, dst_ref=dst, send_sem=ssem.at[i, m], recv_sem=rsem.at[i, m],
                                            device_id=to, device_id_type=MESH)

    def send(w, k, m, src, dst, to):
        c = msg(w, k, m, src, dst, to)
        c.start()
        started.append(c)

    def arrived(w, k, m, dst):
        msg(w, k, m, dst, dst, sibling).wait_recv()

    w1s, relays, in1s = (g.w1_0, g.w1_1, g.w1_2), (g.relay_0, g.relay_1, g.relay_2), (g.in1_0, g.in1_1, g.in1_2)
    w2s, in2s = (g.w2_0, g.w2_1, g.w2_2), (g.in2_0, g.in2_1, g.in2_2)
    w3s, in3s = (g.w3_0, g.w3_1, g.w3_2), (g.in3_0, g.in3_1, g.in3_2)
    outs = (w_d, w_u, w_qo)

    def ds(i, n, m):
        return pl.ds(pl.multiple_of(i, m), n)

    def place_of(k, phase):
        axis = ORDERS[k][phase]
        return pos[axis], lambda by: device(along(pos, axis, by), core)

    def dims(w):
        n, c = SHAPES[w]
        return n // 4, n // 16, c, ds(0, c // 2, 128), ds(c // 2, c // 2, 128)

    def rs1a(w, k):
        i, to = place_of(k, 0)
        n, _, _, A, B = dims(w)
        w1, relay, inn = w1s[w].at[k], relays[w].at[k], in1s[w].at[k]

        def blk(by):
            return ds(((i + by) % 4) * n, n, 16)

        send(w, k, 0, w1.at[blk(2), A], relay.at[0], to(1))
        send(w, k, 1, w1.at[blk(2), B], relay.at[1], to(3))
        send(w, k, 2, w1.at[blk(1), B], inn.at[0, :, B], to(1))
        send(w, k, 3, w1.at[blk(3), A], inn.at[1, :, A], to(3))

    def rs1b(w, k):
        i, to = place_of(k, 0)
        n, _, _, A, B = dims(w)
        w1, relay, inn = w1s[w], relays[w], in1s[w]
        for side, by, cols in ((0, 1, A), (1, 3, B)):
            first = ((i + by) % 4) * n
            arrived(w, k, side, relay.at[k, side])

            def add(j, _):
                s = ds(j * 16, 16, 16)
                t = ds(first + j * 16, 16, 16)
                relay[k, side, s, :] = (relay[k, side, s, :].astype(F32) + w1[k, t, cols].astype(F32)).astype(BF)
                return 0

            lax.fori_loop(0, n // 16, add, 0)
            send(w, k, 4 + side, relay.at[k, side], inn.at[k, side, :, cols], to(by))

    def rs1c(w, k):
        i, _ = place_of(k, 0)
        n, _, _, A, B = dims(w)
        w1, inn, w2 = w1s[w], in1s[w], w2s[w]
        arrived(w, k, 2, inn.at[k, 0, :, B])
        arrived(w, k, 3, inn.at[k, 1, :, A])
        arrived(w, k, 4, inn.at[k, 0, :, A])
        arrived(w, k, 5, inn.at[k, 1, :, B])

        def add(j, _):
            s = ds(j * 16, 16, 16)
            t = ds(i * n + j * 16, 16, 16)
            w2[k, s, :] = (w1[k, t, :].astype(F32) + inn[k, 0, s, :].astype(F32) + inn[k, 1, s, :].astype(F32)).astype(BF)
            return 0

        lax.fori_loop(0, n // 16, add, 0)

    def rs2a(w, k):
        i, to = place_of(k, 1)
        _, n, _, _, _ = dims(w)
        for d in (1, 2, 3):
            send(w, k, 5 + d, w2s[w].at[k, ds(((i + d) % 4) * n, n, 16)], in2s[w].at[k, d - 1], to(d))

    def rs2b(w, k):
        i, _ = place_of(k, 1)
        _, n, _, _, _ = dims(w)
        for d in (1, 2, 3):
            arrived(w, k, 5 + d, in2s[w].at[k, d - 1])
        total = w2s[w][k, ds(i * n, n, 16), :].astype(F32)
        for d in range(3):
            total = total + in2s[w][k, d].astype(F32)
        w3s[w][k] = total.astype(BF)

    def sub(w, j):
        n, c = SUBS[w]
        if w == 0:
            return ds((j // 2) * n, n, 16), ds((j % 2) * c, c, 128)
        return slice(None), ds(j * c, c, 128)

    def rs3a(w, k):
        i, to = place_of(k, 2)
        for d in (1, 2, 3):
            rows, cols = sub(w, (i + d) % 4)
            send(w, k, 8 + d, w3s[w].at[k, rows, cols], in3s[w].at[k, d - 1], to(d))

    def spot(w, k, c1, c2=None, c3=None, cols=None, c=None):
        c = core if c is None else c
        n1, n2, width, _, _ = dims(w)
        r0, l0 = (c * 1536 + 512 * k, 0) if w == 0 else (0, c * 1536 + 512 * k)
        r0 = r0 + n1 * c1
        n = n1
        if c2 is not None:
            r0 = r0 + n2 * c2
            n = n2
        if c3 is not None:
            n, width = SUBS[w]
            if w == 0:
                r0, l0 = r0 + n * (c3 // 2), l0 + width * (c3 % 2)
            else:
                l0 = l0 + width * c3
        elif cols is not None:
            width = width // 2
            l0 = l0 + width * cols
        return outs[w].at[ds(r0, n, 16), ds(l0, width, 128)]

    def at(k):
        return tuple(pos[a] for a in ORDERS[k])

    def rs3b(w, k):
        i, to = place_of(k, 2)
        for d in (1, 2, 3):
            arrived(w, k, 8 + d, in3s[w].at[k, d - 1])
        rows, cols = sub(w, i)
        total = w3s[w][k, rows, cols].astype(F32)
        for d in range(3):
            total = total + in3s[w][k, d].astype(F32)
        mine = spot(w, k, *at(k))
        mine[...] = total.astype(BF)
        for d in (1, 2, 3):
            send(w, k, 11 + d, mine, mine, to(d))

    def ag3b(w, k):
        c1, c2, c3 = at(k)
        for d in (1, 2, 3):
            arrived(w, k, 11 + d, spot(w, k, c1, c2, (c3 + 4 - d) % 4))

    def ag2a(w, k):
        c1, c2, _ = at(k)
        _, to = place_of(k, 1)
        mine = spot(w, k, c1, c2)
        for d in (1, 2, 3):
            send(w, k, 14 + d, mine, mine, to(d))

    def ag2b(w, k):
        c1, c2, _ = at(k)
        for d in (1, 2, 3):
            arrived(w, k, 14 + d, spot(w, k, c1, (c2 + 4 - d) % 4))

    def ag1a(w, k):
        c1, _, _ = at(k)
        _, to = place_of(k, 0)
        for cols, m in ((0, 18), (1, 20)):
            up = spot(w, k, c1, cols=cols)
            send(w, k, m, up, up, to(1))
            dn = spot(w, k, c1, cols=1 - cols)
            send(w, k, m + 1, dn, dn, to(3))
        mine = spot(w, k, c1)
        send(w, k, 24, mine, mine, sibling)

    def ag1b(w, k):
        c1, _, _ = at(k)
        _, to = place_of(k, 0)
        left, right = (c1 + 3) % 4, (c1 + 1) % 4
        a = spot(w, k, left, cols=0)
        arrived(w, k, 18, a)
        send(w, k, 22, a, a, to(1))
        b = spot(w, k, right, cols=1)
        arrived(w, k, 19, b)
        send(w, k, 23, b, b, to(3))
        arrived(w, k, 20, spot(w, k, left, cols=1))
        send(w, k, 25, spot(w, k, left), spot(w, k, left), sibling)
        arrived(w, k, 21, spot(w, k, right, cols=0))
        send(w, k, 26, spot(w, k, right), spot(w, k, right), sibling)

    def ag1c(w, k):
        c1, _, _ = at(k)
        for cols in range(2):
            far = spot(w, k, (c1 + 2) % 4, cols=cols)
            arrived(w, k, 22 + cols, far)
            send(w, k, 27 + cols, far, far, sibling)

    def sib(w, k):
        c1, _, _ = at(k)
        for by, m in ((0, 24), (3, 25), (1, 26)):
            arrived(w, k, m, spot(w, k, (c1 + by) % 4, c=1 - core))
        for cols in range(2):
            arrived(w, k, 27 + cols, spot(w, k, (c1 + 2) % 4, cols=cols, c=1 - core))

    STEPS = ((rs1a,), (rs1b,), (rs1c, rs2a), (rs2b, rs3a), (rs3b,), (ag3b, ag2a), (ag2b, ag1a), (ag1b,), (ag1c,), (sib,))

    def step(w, n):
        for k in range(3):
            for f in STEPS[n]:
                f(w, k)

    def own_a():
        for by in (1, 2, 3):
            c = pltpu.make_async_remote_copy(
                src_ref=g.own.at[(me + by) % 4], dst_ref=g.own_in.at[by - 1], send_sem=xs_send.at[2 + by],
                recv_sem=xs_recv.at[2 + by], device_id=device(along(pos, 1, by), core), device_id_type=MESH)
            c.start()
            started.append(c)

    def own_b():
        total = g.own[me].astype(F32)
        for by in (1, 2, 3):
            pltpu.make_async_remote_copy(
                src_ref=g.own_in.at[by - 1], dst_ref=g.own_in.at[by - 1], send_sem=xs_send.at[2 + by],
                recv_sem=xs_recv.at[2 + by], device_id=sibling, device_id_type=MESH).wait_recv()
            total = total + g.own_in[by - 1].astype(F32)
        mine = own_out.at[pl.ds(pl.multiple_of(64 * me, 16), 64)]
        mine[...] = total.astype(BF)
        for by in (1, 2, 3):
            c = pltpu.make_async_remote_copy(
                src_ref=mine, dst_ref=mine, send_sem=xs_send.at[5 + by],
                recv_sem=xs_recv.at[5 + by], device_id=device(along(pos, 1, by), core), device_id_type=MESH)
            c.start()
            started.append(c)

    def own_c():
        for by in (1, 2, 3):
            src = own_out.at[pl.ds(pl.multiple_of(64 * ((me + 4 - by) % 4), 16), 64)]
            pltpu.make_async_remote_copy(
                src_ref=src, dst_ref=src, send_sem=xs_send.at[5 + by],
                recv_sem=xs_recv.at[5 + by], device_id=sibling, device_id_type=MESH).wait_recv()

    def small_send(stage):
        n = 1 if stage == 0 else 3
        first = 0 if stage == 0 else 3 * stage - 2
        for k in range(n):
            to = sibling if stage == 0 else device(along(pos, stage - 1, k + 1), core)
            c = pltpu.make_async_remote_copy(
                src_ref=g.small_out_v.at[stage], dst_ref=g.small_in.at[first + k], send_sem=xs_send.at[9 + first + k],
                recv_sem=xs_recv.at[9 + first + k], device_id=to, device_id_type=MESH)
            c.start()
            started.append(c)

    def small_take(stage):
        n = 1 if stage == 0 else 3
        first = 0 if stage == 0 else 3 * stage - 2
        total = g.small_out_v[stage]
        for k in range(n):
            ref = g.small_in.at[first + k]
            pltpu.make_async_remote_copy(
                src_ref=ref, dst_ref=ref, send_sem=xs_send.at[9 + first + k],
                recv_sem=xs_recv.at[9 + first + k], device_id=sibling, device_id_type=MESH).wait_recv()
            total = total + g.small_in[first + k]
        g.small_out_v[stage + 1] = total

    g.small_out_v[0] = g.sums[...]
    small_send(0)
    act_local.wait()
    act_go.wait_recv()
    dh_go.wait_recv()
    for k in range(3):
        g.w1_0[k] = mm_tn(g.f_act[:, 512 * k : 512 * k + 512], g.f_dh[...]).astype(BF)
    step(0, 0)
    du_local.wait()
    du_go.wait_recv()
    n2_go.wait_recv()
    for k in range(3):
        g.w1_1[k] = mm_tn(g.f_n2[...], g.f_du[:, 512 * k : 512 * k + 512]).astype(BF)
    dq_local.wait()
    for c in (dq_go, n1_go, o_go):
        c.wait_recv()
    left = mm_tn(g.f_n1[...], g.f_qo[:, 0:768]).astype(BF)
    g.w1_2[0] = left[:, 0:512]
    g.w1_2[1, :, 0:256] = left[:, 512:768]
    step(0, 1)
    step(1, 0)

    def right(factor):
        v = mm_tn(factor[...], g.f_qo[:, 768:1536]).astype(BF)
        g.w1_2[1, :, 256:512] = v[:, 0:256]
        g.w1_2[2] = v[:, 256:768]

    @pl.when(core == 0)
    def _():
        right(g.f_n1)

    @pl.when(core == 1)
    def _():
        right(g.f_o)

    step(0, 2)
    step(1, 1)
    step(2, 0)
    own_a()
    small_take(0)
    small_send(1)
    step(0, 3)
    step(1, 2)
    step(2, 1)
    small_take(1)
    small_send(2)
    step(0, 4)
    step(1, 3)
    step(2, 2)
    own_b()
    small_take(2)
    small_send(3)
    step(0, 5)
    step(1, 4)
    step(2, 3)
    small_take(3)
    small_out[...] = g.small_out_v[4]
    step(0, 6)
    step(1, 5)
    step(2, 4)
    own_c()
    step(0, 7)
    step(1, 6)
    step(2, 5)
    step(0, 8)
    step(1, 7)
    step(2, 6)
    step(1, 8)
    step(2, 7)
    step(2, 8)
    for w in range(3):
        step(w, 9)
    for c in started:
        c.wait_send()


SCRATCH["small_out_v"] = ((5, 16, D), F32)
NAMES.append("small_out_v")


def passes(*args):
    smem = pl.BlockSpec(memory_space=pltpu.SMEM)
    hbm = pl.BlockSpec(memory_space=pl.ANY)
    vmem = pl.BlockSpec(memory_space=pltpu.VMEM)
    dma = pltpu.SemaphoreType.DMA
    return pl.pallas_call(
        kernel,
        out_shape=[
            pltpu.VMEM((ROWS, D), BF),
            pltpu.VMEM((ROWS, D), BF),
            pltpu.VMEM((16, D), F32),
            pltpu.VMEM((D, FF), BF),
            pltpu.VMEM((D, FF), BF),
            pltpu.VMEM((FF, D), BF),
        ],
        in_specs=[smem, smem] + [hbm] * (len(args) - 2),
        out_specs=[vmem] * 6,
        scratch_shapes=[pltpu.VMEM(s, t) for s, t in SCRATCH.values()]
        + [dma((21,)), dma((8,)), dma((8,)), dma((9, NMSG)), dma((9, NMSG)), dma((19,)), dma((19,))],
        compiler_params=pltpu.CompilerParams(
            collective_id=0, has_side_effects=True, vmem_limit_bytes=VMEM_LIMIT
        ),
        name="passes",
    )(*args)


VMEM_LIMIT = 46 * 2**20
SMALL = ((LN1G, 1), (LN1S, 1), (BQV, 2), (BOUT, 1), (LN2G, 1), (LN2S, 1), (BUP, 4), (BDOWN, 1))


def widen_kernel(act, own, small, qo, u, d, act_out, own_out, gq, go, gu, gd, *rest):
    small_outs, (wide, tall, sem, wide_sem, tall_sem) = rest[:8], rest[8:]
    pending = []

    def copy(src, dst, s):
        c = pltpu.make_async_copy(src, dst, s)
        c.start()
        return c

    pending.append(copy(act, act_out, sem.at[0]))
    pending.append(copy(own, own_out, sem.at[1]))
    n = 2
    for (first, count), ref in zip(SMALL, small_outs):
        for k in range(count):
            pending.append(copy(small.at[first + k], ref.at[pl.ds(k * D, D)], sem.at[n]))
            n += 1
    slots = {}

    def chunk(buf, sems, i, value, parts):
        slot = i % buf.shape[0]
        key = (buf is wide, slot)
        for c in slots.get(key, ()):
            c.wait()
        buf[slot] = value.astype(F32)
        slots[key] = [copy(buf.at[slot, :, pl.ds(l0, n)], dst, sems.at[slot, j]) for j, (l0, n, dst) in enumerate(parts)]

    for i in range(12):
        rows = pl.ds(64 * i, 64)
        chunk(wide, wide_sem, 2 * i, qo[64 * i : 64 * i + 64, :], ((0, 3 * D, gq.at[rows]), (3 * D, D, go.at[rows])))
        chunk(tall, tall_sem, i, d[256 * i : 256 * i + 256, :], ((0, D, gd.at[pl.ds(256 * i, 256)]),))
        chunk(wide, wide_sem, 2 * i + 1, u[64 * i : 64 * i + 64, :], ((0, FF, gu.at[rows]),))
    for cs in list(slots.values()) + [pending]:
        for c in cs:
            c.wait()


def widen(*arrays):
    hbm = pl.BlockSpec(memory_space=pl.ANY)
    vmem = pl.BlockSpec(memory_space=pltpu.VMEM)
    dma = pltpu.SemaphoreType.DMA
    shape = jax.ShapeDtypeStruct
    return pl.pallas_call(
        widen_kernel,
        in_specs=[vmem] * 6,
        out_specs=[hbm] * 14,
        out_shape=[shape((ROWS, D), BF), shape((ROWS, D), BF), shape((D, 3 * D), F32), shape((D, D), F32), shape((D, FF), F32),
                   shape((FF, D), F32)] + [shape((n * D,), F32) for _, n in SMALL],
        scratch_shapes=[pltpu.VMEM((6, 64, FF), F32), pltpu.VMEM((3, 256, D), F32), dma((14,)), dma((6, 2)), dma((3, 1))],
        compiler_params=pltpu.CompilerParams(vmem_limit_bytes=24 * 2**20),
        name="widen",
    )(*arrays)


def on_device(embedded, cotangent, lengths, starts, *params):
    gathered = passes(starts, lengths, embedded.reshape(ROWS, D), cotangent.reshape(ROWS, D), *params)
    act, own, gq, go, gu, gd, ln1g, ln1s, bqv, bout, ln2g, ln2s, bup, bdown = widen(*gathered)
    return (act.reshape(1, 2, 128, D), own.reshape(2, 128, D), ln1g, ln1s, gq, bqv, go, bout, ln2g, ln2s, gu, bup, gd, bdown)


def solution(mesh):
    rows = P("batch", None, None)
    passes_rows = P("pass", "batch", None, None)
    return jax.shard_map(
        on_device,
        mesh=mesh,
        in_specs=(rows, passes_rows, P("batch"), P("batch")) + (P(),) * 12,
        out_specs=(passes_rows, rows) + (P(),) * 12,
        check_vma=False,
    )
```

```python
import functools

import jax
import jax.numpy as jnp
from jax import lax
from jax.experimental import pallas as pl
from jax.experimental.pallas import tpu as pltpu
from jax.sharding import PartitionSpec as P

MESH = pl.DeviceIdType.MESH
BF, F32 = jnp.bfloat16, jnp.float32
HEADS = 12
D = 768
FF = 3072
ROWS = 256
TOP = 48
epsilon = 1e-05
SCALE = 0.125

LN1G, LN1S, BQV, BOUT, LN2G, LN2S, BUP, BDOWN = 0, 1, 2, 4, 5, 6, 7, 11

ORDERS = ((0, 1, 2), (1, 2, 0), (2, 0, 1))
NMSG = 32
WAVES = 3
SHAPES = ((1536, 256), (768, 512), (768, 512))
BLOCKS = ((384, 256), (768, 128), (192, 512))
PIECES = ((96, 256), (192, 128), (48, 512))
SUB = (48, 128)


def mm(a, b):
    return jnp.dot(a, b, preferred_element_type=F32)


def mm_nt(a, b):
    return lax.dot_general(a, b, (((1,), (1,)), ((), ())), preferred_element_type=F32)


def mm_tn(a, b):
    return lax.dot_general(a, b, (((0,), (0,)), ((), ())), preferred_element_type=F32)


def normalise(v):
    mu = jnp.sum(v, -1, keepdims=True) * (1.0 / D)
    c = v - mu
    var = jnp.sum(c * c, -1, keepdims=True) * (1.0 / D)
    rs = lax.rsqrt(var + epsilon)
    return c * rs, rs


def normalise_back(grad, gain, xhat, rs):
    gy = grad * gain
    m1 = jnp.sum(gy, -1, keepdims=True) * (1.0 / D)
    m2 = jnp.sum(gy * xhat, -1, keepdims=True) * (1.0 / D)
    return rs * (gy - m1 - xhat * m2)


def gelu_both(u):
    k = 0.7978845608028654
    u2 = u * u
    th = jnp.tanh(k * u * (1.0 + 0.044715 * u2))
    half = 0.5 * (1.0 + th)
    return u * half, half + 0.5 * u * (1.0 - th * th) * (k * (1.0 + 3 * 0.044715 * u2))


def eights(v):
    return jnp.sum(v.reshape(v.shape[0] // 8, 8, v.shape[1]), 0)


def column_sum(v):
    return jnp.sum(eights(v), 0, keepdims=True)


def coords():
    b = lax.axis_index("batch")
    y = lax.axis_index("pass")
    return (lax.div(b, 8), y, lax.rem(lax.div(b, 2), 4)), lax.rem(b, 2)


def device(pos, core):
    x, y, z = pos
    return ((x * 4 + z) * 2 + core, y)


def along(pos, axis, by):
    return tuple(lax.rem(c + by, 4) if i == axis else c for i, c in enumerate(pos))


def iota(shape, dim):
    return lax.broadcasted_iota(jnp.int32, shape, dim)


def lane_heads(v, rows):
    head = iota((rows, D), 1) // 64
    zero = jnp.zeros((rows, D), v.dtype)
    return jnp.concatenate([jnp.where(head == h, v, zero) for h in range(HEADS)], 0)


def join_heads(v, rows):
    head = iota((rows, D), 1) // 64
    total = jnp.zeros((rows, D), F32)
    for h in range(HEADS):
        total = jnp.where(head == h, v[h * rows : (h + 1) * rows], total)
    return total


def pair_rows(v):
    left = iota((128, 128), 1) < 64
    zero = jnp.zeros((128, 128), v.dtype)
    return jnp.concatenate([jnp.where(left, v, zero), jnp.where(left, zero, v)], 0)


def pair_join(v):
    left = iota((128, 128), 1) < 64
    return jnp.where(left, v[:128], v[128:])


SCRATCH = dict(
        par=((16, D), F32),
    xh1=((ROWS, D), F32), rs1=((ROWS, 1), F32), qkv=((ROWS, 3 * D), BF),
    prob=((12, 256, 128), F32), res=((ROWS, D), F32), xh2=((ROWS, D), F32), rs2=((ROWS, 1), F32),
    gp=((ROWS, FF), F32), act=((ROWS, FF), BF),
    tmp=((ROWS, D), F32), dmix=((ROWS, D), BF),
    du=((ROWS, FF), BF), dqo=((ROWS, FF), BF), sums=((16, D), F32),
    xm=((4, 16, D), F32), xh1m=((4, 16, D), F32), rs1m=((4, 16, 1), F32), qkvm=((4, 16, 3 * D), BF),
    kall=((3, 128, D), BF), vall=((3, 128, D), BF), pm=((3, 192, 128), F32),
    xh2m=((3, 16, D), F32), rs2m=((3, 16, 1), F32), gpm=((3, 16, FF), F32),
    slots=((4, 16, D), BF), slot_out=((16, D), BF),
    e_own=((16, D), BF), du_own=((16, FF), BF), da_own=((16, D), BF), dqkv_own=((80, 3 * D), BF),
    dx_mini=((16, D), F32), dxm_own=((16, D), BF), dxb_own=((64, D), F32),
    f_n1=((512, D), BF), f_o=((512, D), BF), f_n2=((512, D), BF), f_dh=((512, D), BF),
    f_qo=((512, 1536), BF), f_du=((512, 1536), BF), f_act=((512, 1536), BF),
    w1_0=((3, 1536, 256), BF), w1_1=((3, 768, 512), BF), w1_2=((3, 768, 512), BF),
    relay=((3, 2, 192, 256), BF),
    in1_0=((3, 3, 384, 256), BF), in1_1=((3, 3, 768, 128), BF), in1_2=((3, 2, 192, 512), BF),
    w2_0=((3, 384, 256), BF), w2_1=((3, 768, 128), BF), w2_2=((3, 192, 512), BF),
    in2_0=((3, 3, 96, 256), BF), in2_1=((3, 3, 192, 128), BF), in2_2=((3, 3, 48, 512), BF),
    w3_0=((3, 96, 256), BF), w3_1=((3, 192, 128), BF), w3_2=((3, 48, 512), BF),
    in3_0=((3, 3, 48, 128), BF), in3_1=((3, 3, 48, 128), BF), in3_2=((3, 3, 48, 128), BF),
    act_mini=((16, FF), BF), c_act=((32, 1536), BF), c_n2=((32, D), BF), c_e=((32, D), BF), c_du=((32, 1536), BF),
    ca_0=((3, 4, 32, 384), BF), cg_0=((3, 4, 32, 256), BF), ca_1=((3, 4, 32, D), BF), cg_1=((3, 4, 32, 128), BF),
    own=((2, 4, 32, D), BF), own_in=((2, 3, 32, D), BF),
    small_in=((10, 16, D), F32),
)
NAMES = list(SCRATCH)


def kernel(start_ref, length_ref, x_hbm, cot_hbm, ln1g_hbm, ln1s_hbm, wq_hbm, bqv_hbm, wo_hbm, bout_hbm, ln2g_hbm, ln2s_hbm,
           wu_hbm, bup_hbm, wd_hbm, bdown_hbm, x_v, own_out, small_out, w_qo, w_u, w_d, *scratch):
    r = dict(zip(NAMES, scratch))
    lsem, fsem, frem, ssem, rsem, xs_send, xs_recv = scratch[len(NAMES):]
    g = type("Refs", (), r)
    g.x_v, g.wu, g.wd = x_v, w_u, w_d
    g.wq, g.wo = w_qo.at[:, pl.ds(0, 3 * D)], w_qo.at[:, pl.ds(3 * D, D)]
    g.dqkv, g.da = g.dqo.at[:, pl.ds(0, 3 * D)], g.dqo.at[:, pl.ds(3 * D, D)]
    g.dx, g.dres, g.dn1, g.out_act = g.res, g.tmp, g.xh2, g.x_v
    g.cot_v = g.f_dh.at[pl.ds(0, 256)]
    pos, core = coords()
    me = pos[1]
    sibling = device(pos, 1 - core)

    barrier = pltpu.get_barrier_semaphore()
    for axis in range(3):
        for by in (1, 2, 3):
            pl.semaphore_signal(barrier, inc=1, device_id=device(along(pos, axis, by), core), device_id_type=MESH)
    pl.semaphore_signal(barrier, inc=1, device_id=sibling, device_id_type=MESH)

    def load(i, src, dst):
        c = pltpu.make_async_copy(src, dst, lsem.at[i])
        c.start()
        return c

    vectors = ((ln1g_hbm, LN1G), (ln1s_hbm, LN1S), (bqv_hbm, BQV), (bout_hbm, BOUT), (ln2g_hbm, LN2G), (ln2s_hbm, LN2S),
               (bup_hbm, BUP), (bdown_hbm, BDOWN))
    x_load = load(0, x_hbm, g.x_v)
    par_loads = []
    for src, first in vectors:
        for k in range(src.shape[0] // D):
            par_loads.append(load(9 + first + k, src.at[pl.ds(k * D, D)], g.par.at[first + k]))
    wq_load = load(2, wq_hbm, g.wq)

    def row(i, n=1):
        if n == 1:
            return g.par[i : i + 1, :]
        return jnp.concatenate([g.par[i + k : i + k + 1, :] for k in range(n)], 1)

    s0, s1 = start_ref[0], start_ref[1]
    n0, n1 = length_ref[0], length_ref[1]
    r16 = iota((16, 256), 0)
    want = jnp.where(r16 < 8, s0 - 1 + r16, 128 + s1 - 1 + r16 - 8)
    pick = (iota((16, 256), 1) == want).astype(BF)
    col16 = iota((TOP, 16), 1)
    row48 = iota((TOP, 16), 0)
    place = []
    place_slots = []
    for q, s in ((0, s0), (1, s1)):
        i = col16 - 8 * q
        hit = (i >= 0) & (i < 8) & (row48 == s - 1 + i)
        place.append(hit.astype(BF))
        place_slots.append((hit & (i >= 1) & (i <= 6)).astype(BF))

    def is_slot(s, rows):
        j = iota((rows, 1), 0)
        return (j >= s) & (j < s + 6)

    x_load.wait()
    for c in par_loads:
        c.wait()

    def norm_one(i, _):
        rows = pl.ds(pl.multiple_of(i * 32, 32), 32)
        xhat, rs = normalise(g.x_v[rows, :].astype(F32))
        g.xh1[rows, :] = xhat
        g.rs1[rows, :] = rs
        g.f_n1[rows, :] = (xhat * row(LN1G) + row(LN1S)).astype(BF)
        return 0

    w_loads = [load(3, wo_hbm, g.wo), load(4, wu_hbm, g.wu), load(5, wd_hbm, g.wd)]
    cot_load = load(6, cot_hbm, g.cot_v)
    lax.fori_loop(0, 8, norm_one, 0)
    wq_load.wait()
    qkv_bias = (row(BQV), jnp.zeros((1, D), F32), row(BQV + 1))
    for k in range(3):
        c = slice(k * D, (k + 1) * D)
        g.qkv[:, c] = (mm(g.f_n1[0:256, :], g.wq[:, c]) + qkv_bias[k]).astype(BF)

    xm = mm(pick, g.x_v[...])
    g.xm[0] = xm
    xhat, rs = normalise(xm)
    g.xh1m[0] = xhat
    g.rs1m[0] = rs
    g.qkvm[0] = mm(pick, g.qkv[...]).astype(BF)
    for t in range(3):
        for buf, lane in ((g.kall, D), (g.vall, 2 * D)):
            buf[t, 0:32, :] = g.qkv[0:32, lane : lane + D]
            buf[t, 32:64, :] = g.qkv[128:160, lane : lane + D]
            buf[t, 80:128, :] = jnp.zeros((48, D), BF)
    for c in w_loads:
        c.wait()

    rr = iota((192, 128), 0) % 16
    cc = iota((192, 128), 1)
    rq, ri = rr // 8, rr % 8
    base_ok = (cc < 64) & (cc // 32 == rq) & (cc % 32 < jnp.where(rq == 0, s0, s1))
    mi = cc - 64
    mini_ok = (mi >= 0) & (mi < 16) & (mi // 8 == rq) & (mi % 8 >= 1) & (mi % 8 <= ri)
    mini_allowed = base_ok | mini_ok
    mini_first = iota((16, D), 0) % 8 == 0

    def thought(t, _):
        g.kall[t, 64:80, :] = g.qkvm[t, :, D : 2 * D]
        g.vall[t, 64:80, :] = g.qkvm[t, :, 2 * D : 3 * D]
        s = mm_nt(lane_heads(g.qkvm[t, :, 0:D], 16), g.kall[t]) * SCALE
        s = jnp.where(mini_allowed, s, -1e30)
        e = jnp.exp(s - jnp.max(s, -1, keepdims=True))
        p = e / jnp.sum(e, -1, keepdims=True)
        g.pm[t] = p
        o = join_heads(mm(p.astype(BF), g.vall[t]), 16).astype(BF)
        res = g.xm[t] + mm(o, g.wo[...]) + row(BOUT)
        xhat, rs = normalise(res)
        g.xh2m[t] = xhat
        g.rs2m[t] = rs
        n2 = (xhat * row(LN2G) + row(LN2S)).astype(BF)
        parts = []
        for k in range(2):
            u = mm(n2, g.wu[:, k * 1536 : (k + 1) * 1536]) + row(BUP + 2 * k, 2)
            m, slope = gelu_both(u)
            g.gpm[t, :, k * 1536 : (k + 1) * 1536] = slope
            parts.append(m.astype(BF))
        h = res + mm(jnp.concatenate(parts, 1), g.wd[...]) + row(BDOWN)
        h = h.astype(BF).astype(F32)
        nxt = jnp.where(mini_first, g.xm[t], pltpu.roll(h, 1, 0))
        g.xm[t + 1] = nxt
        xhat, rs = normalise(nxt)
        g.xh1m[t + 1] = xhat
        g.rs1m[t + 1] = rs
        n1 = (xhat * row(LN1G) + row(LN1S)).astype(BF)
        for k in range(3):
            c = slice(k * D, (k + 1) * D)
            g.qkvm[t + 1, :, c] = (mm(n1, g.wq[:, c]) + qkv_bias[k]).astype(BF)
        return 0

    lax.fori_loop(0, 3, thought, 0)

    for q, s in ((0, s0), (1, s1)):
        rows = slice(128 * q, 128 * q + TOP)
        slot = is_slot(s, TOP)
        x = jnp.where(slot, mm(place_slots[q], g.xm[me].astype(BF)), g.x_v[rows, :].astype(F32))
        g.x_v[rows, :] = x.astype(BF)
        xhat, rs = normalise(x)
        g.xh1[rows, :] = xhat
        g.rs1[rows, :] = rs
        g.f_n1[rows, :] = (xhat * row(LN1G) + row(LN1S)).astype(BF)
        g.qkv[rows, :] = jnp.where(slot, mm(place_slots[q], g.qkvm[me]), g.qkv[rows, :].astype(F32)).astype(BF)

    qi = iota((256, 128), 0) % 128
    kj = iota((256, 128), 1)

    def attend(q, _):
        rows = pl.ds(pl.multiple_of(q * 128, 128), 128)
        ok = (kj <= qi) & (kj < jnp.where(q == 0, n0, n1))
        for hp in range(6):
            lanes = slice(128 * hp, 128 * hp + 128)
            q2 = pair_rows(g.qkv[rows, lanes])
            s = mm_nt(q2, g.qkv[rows, D + 128 * hp : D + 128 * hp + 128]) * SCALE
            s = jnp.where(ok, s, -1e30)
            e = jnp.exp(s - jnp.max(s, -1, keepdims=True))
            p = e / jnp.sum(e, -1, keepdims=True)
            g.prob[q * 6 + hp] = p
            o2 = mm(p.astype(BF), g.qkv[rows, 2 * D + 128 * hp : 2 * D + 128 * hp + 128])
            g.f_o[rows, lanes] = pair_join(o2).astype(BF)
        return 0

    lax.fori_loop(0, 2, attend, 0)

    g.tmp[...] = mm(g.f_o[0:256, :], g.wo[...])

    def norm_two(i, _):
        rows = pl.ds(pl.multiple_of(i * 32, 32), 32)
        res = g.x_v[rows, :].astype(F32) + g.tmp[rows, :] + row(BOUT)
        g.res[rows, :] = res
        xhat, rs = normalise(res)
        g.xh2[rows, :] = xhat
        g.rs2[rows, :] = rs
        g.f_n2[rows, :] = (xhat * row(LN2G) + row(LN2S)).astype(BF)
        return 0

    lax.fori_loop(0, 8, norm_two, 0)
    for k in range(4):
        c = slice(k * D, (k + 1) * D)
        m, slope = gelu_both(mm(g.f_n2[0:256, :], g.wu[:, c]) + row(BUP + k))
        g.gp[:, c] = slope
        g.act[:, c] = m.astype(BF)
    g.out_act[...] = (g.res[...] + mm(g.act[...], g.wd[...]) + row(BDOWN)).astype(BF)

    pl.semaphore_wait(barrier, 10)
    lo, hi = pl.ds(0, 256), pl.ds(256, 256)
    started = []

    def to_sibling(i, src, dst):
        c = pltpu.make_async_remote_copy(src_ref=src, dst_ref=dst, send_sem=fsem.at[i], recv_sem=frem.at[i],
                                         device_id=sibling, device_id_type=MESH)
        c.start()
        started.append(c)
        return c

    def local(i, src, dst):
        c = pltpu.make_async_copy(src, dst, lsem.at[i])
        c.start()
        return c

    def half(ref, which, width):
        return ref.at[:, pl.ds(pl.multiple_of(which * width, 128), width)]

    cot_load.wait()
    dh_go = to_sibling(4, g.f_dh.at[lo], g.f_dh.at[hi])
    act_go = to_sibling(3, half(g.act, 1 - core, 1536), g.f_act.at[hi])
    act_local = local(1, half(g.act, core, 1536), g.f_act.at[lo])
    n2_go = to_sibling(2, g.f_n2.at[lo], g.f_n2.at[hi])
    n1_go = to_sibling(0, g.f_n1.at[lo], g.f_n1.at[hi])
    o_go = to_sibling(1, g.f_o.at[lo], g.f_o.at[hi])
    mini_lo, mini_hi = pl.ds(0, 16), pl.ds(16, 16)
    g.act_mini[...] = mm(pick, g.act[...]).astype(BF)
    g.c_act[0:16, :] = g.act_mini[:, pl.ds(pl.multiple_of(core * 1536, 128), 1536)]
    g.c_n2[0:16, :] = mm(pick, g.f_n2[0:256, :]).astype(BF)
    c_act_go = to_sibling(7, half(g.act_mini, 1 - core, 1536), g.c_act.at[mini_hi])
    c_n2_go = to_sibling(8, g.c_n2.at[mini_lo], g.c_n2.at[mini_hi])

    for k in range(4):
        c = slice(k * D, (k + 1) * D)
        du = (mm_nt(g.cot_v[...], g.wd[c, :]) * g.gp[:, c]).astype(BF)
        g.du[:, c] = du
        g.sums[BUP + k : BUP + k + 1, :] = column_sum(du.astype(F32))
    du_go = to_sibling(5, half(g.du, 1 - core, 1536), g.f_du.at[hi])
    du_local = local(3, half(g.du, core, 1536), g.f_du.at[lo])
    g.sums[BDOWN : BDOWN + 1, :] = column_sum(g.cot_v[...].astype(F32))
    g.tmp[...] = mm_nt(g.du[...], g.wu[...])
    zero8 = jnp.zeros((8, D), F32)

    def back_two(i, acc):
        rows = pl.ds(pl.multiple_of(i * 32, 32), 32)
        dn = g.tmp[rows, :]
        xhat = g.xh2[rows, :]
        dres = g.cot_v[rows, :].astype(F32) + normalise_back(dn, row(LN2G), xhat, g.rs2[rows, :])
        g.dres[rows, :] = dres
        da = dres.astype(BF)
        g.da[rows, :] = da
        return acc[0] + eights(dn * xhat), acc[1] + eights(dn), acc[2] + eights(da.astype(F32))

    acc = lax.fori_loop(0, 8, back_two, (zero8, zero8, zero8))
    for i, a in zip((LN2G, LN2S, BOUT), acc):
        g.sums[i : i + 1, :] = jnp.sum(a, 0, keepdims=True)
    g.dmix[...] = mm_nt(g.da[...], g.wo[...]).astype(BF)

    def attend_back(q, _):
        rows = pl.ds(pl.multiple_of(q * 128, 128), 128)
        for hp in range(6):
            lanes = slice(128 * hp, 128 * hp + 128)
            klanes = slice(D + 128 * hp, D + 128 * hp + 128)
            vlanes = slice(2 * D + 128 * hp, 2 * D + 128 * hp + 128)
            do2 = pair_rows(g.dmix[rows, lanes])
            p = g.prob[q * 6 + hp]
            dp = mm_nt(do2, g.qkv[rows, vlanes])
            ds = (p * (dp - jnp.sum(p * dp, -1, keepdims=True))).astype(BF)
            g.dqkv[rows, lanes] = (pair_join(mm(ds, g.qkv[rows, klanes])) * SCALE).astype(BF)
            g.dqkv[rows, klanes] = (mm_tn(ds, pair_rows(g.qkv[rows, lanes])) * SCALE).astype(BF)
            g.dqkv[rows, vlanes] = mm_tn(p.astype(BF), do2).astype(BF)
        return 0

    lax.fori_loop(0, 2, attend_back, 0)
    g.dn1[...] = mm_nt(g.dqkv[...], g.wq[...])

    def back_one(i, acc):
        rows = pl.ds(pl.multiple_of(i * 32, 32), 32)
        dn = g.dn1[rows, :]
        xhat = g.xh1[rows, :]
        g.dx[rows, :] = g.dres[rows, :] + normalise_back(dn, row(LN1G), xhat, g.rs1[rows, :])
        dq = eights(g.dqkv[rows, 0:D].astype(F32))
        dv = eights(g.dqkv[rows, 2 * D : 3 * D].astype(F32))
        return acc[0] + eights(dn * xhat), acc[1] + eights(dn), acc[2] + dq, acc[3] + dv

    acc = lax.fori_loop(0, 8, back_one, (zero8, zero8, zero8, zero8))
    for i, a in zip((LN1G, LN1S, BQV, BQV + 1), acc):
        g.sums[i : i + 1, :] = jnp.sum(a, 0, keepdims=True)

    def msg(w, k, m, src, dst, to):
        i = 3 * w + k
        return pltpu.make_async_remote_copy(src_ref=src, dst_ref=dst, send_sem=ssem.at[i, m], recv_sem=rsem.at[i, m],
                                            device_id=to, device_id_type=MESH)

    def send(w, k, m, src, dst, to):
        c = msg(w, k, m, src, dst, to)
        c.start()
        started.append(c)

    def arrived(w, k, m, dst):
        msg(w, k, m, dst, dst, sibling).wait_recv()

    w1s, in1s = (g.w1_0, g.w1_1, g.w1_2), (g.in1_0, g.in1_1, g.in1_2)
    w2s, in2s = (g.w2_0, g.w2_1, g.w2_2), (g.in2_0, g.in2_1, g.in2_2)
    w3s, in3s = (g.w3_0, g.w3_1, g.w3_2), (g.in3_0, g.in3_1, g.in3_2)
    cas, cgs = (g.ca_0, g.ca_1), (g.cg_0, g.cg_1)
    outs = (w_d, w_u, w_qo)
    memo = {}

    def near(axis, by):
        if (axis, by) not in memo:
            there = along(pos, axis, by)
            memo[axis, by] = (device(there, core), there[axis])
        return memo[axis, by]

    def ds(i, n, m):
        return pl.ds(i if isinstance(i, int) else pl.multiple_of(i, m), n)

    def window(ref, r0, l0, shape):
        return ref.at[ds(r0, shape[0], 16), ds(l0, shape[1], 128)]

    def block(w, c1):
        return ((384 * c1, 0), (0, 128 * c1), (192 * c1, 0))[w]

    def piece(w, c1, c2):
        r, l = block(w, c1)
        return r + PIECES[w][0] * c2, l

    def inner(w, c3):
        return ((48 * lax.div(c3, 2), 128 * lax.rem(c3, 2)), (48 * c3, 0), (0, 128 * c3))[w]

    HALVES = ((384, 128), (384, 128), (192, 256))

    def half_of(w, cols):
        return ((0, 128 * cols), (384 * cols, 0), (0, 256 * cols))[w]

    def send_first(w, k):
        axis = ORDERS[k][0]
        for d in (1, 2, 3):
            to, c = near(axis, d)
            send(w, k, d - 1, window(w1s[w].at[k], *block(w, c), BLOCKS[w]), in1s[w].at[k, d - 1], to)

    def send_left(k):
        axis = ORDERS[k][0]
        mine = near(axis, 0)[1]
        g.ca_0[k, 0] = g.c_act[:, ds(384 * mine, 384, 128)]
        g.ca_1[k, 0] = g.c_n2[...]
        for d in (1, 2, 3):
            to, c = near(axis, d)
            send(0, k, 2 + d, window(g.c_act, 0, 384 * c, (32, 384)), g.ca_0.at[k, d], to)
            send(1, k, 2 + d, g.c_n2, g.ca_1.at[k, d], to)

    def send_right(k):
        axis = ORDERS[k][0]
        mine = near(axis, 0)[1]
        g.cg_0[k, 0] = g.c_e[:, 256 * k : 256 * k + 256]
        g.cg_1[k, 0] = g.c_du[:, ds(512 * k + 128 * mine, 128, 128)]
        for d in (1, 2, 3):
            to, c = near(axis, d)
            send(0, k, 28 + d, window(g.c_e, 0, 256 * k, (32, 256)), g.cg_0.at[k, d], to)
            send(1, k, 28 + d, window(g.c_du, 0, 512 * k + 128 * c, (32, 128)), g.cg_1.at[k, d], to)

    def sum_first(w, k):
        mine = near(ORDERS[k][0], 0)[1]
        for d in (1, 2, 3):
            arrived(w, k, 2 + d, cas[w].at[k, d])
            arrived(w, k, 28 + d, cgs[w].at[k, d])
            arrived(w, k, d - 1, in1s[w].at[k, d - 1])
        n = BLOCKS[w][0]
        total = mm_tn(cas[w][k].reshape(128, n), cgs[w][k].reshape(128, BLOCKS[w][1]))
        total = total + window(w1s[w].at[k], *block(w, mine), BLOCKS[w])[...].astype(F32)
        for d in range(3):
            total = total + in1s[w][k, d].astype(F32)
        w2s[w][k] = total.astype(BF)

    A, B = pl.ds(0, 256), pl.ds(256, 256)

    def ring_a(k):
        axis = ORDERS[k][0]
        w1, inn = g.w1_2.at[k], g.in1_2.at[k]
        (up, c_up), (dn, c_dn), (_, far) = near(axis, 1), near(axis, 3), near(axis, 2)

        def blk(c):
            return ds(c * 192, 192, 16)

        send(2, k, 0, w1.at[blk(far), A], g.relay.at[k, 0], up)
        send(2, k, 1, w1.at[blk(far), B], g.relay.at[k, 1], dn)
        send(2, k, 2, w1.at[blk(c_up), B], inn.at[0, :, B], up)
        send(2, k, 3, w1.at[blk(c_dn), A], inn.at[1, :, A], dn)

    def ring_b(k):
        axis = ORDERS[k][0]
        for side, by, cols in ((0, 1, A), (1, 3, B)):
            to, c = near(axis, by)
            arrived(2, k, side, g.relay.at[k, side])
            g.relay[k, side] = (g.relay[k, side].astype(F32) + g.w1_2[k, ds(c * 192, 192, 16), cols].astype(F32)).astype(BF)
            send(2, k, 4 + side, g.relay.at[k, side], g.in1_2.at[k, side, :, cols], to)

    def ring_c(k):
        inn = g.in1_2
        arrived(2, k, 2, inn.at[k, 0, :, B])
        arrived(2, k, 3, inn.at[k, 1, :, A])
        arrived(2, k, 4, inn.at[k, 0, :, A])
        arrived(2, k, 5, inn.at[k, 1, :, B])
        mine = near(ORDERS[k][0], 0)[1]
        total = g.w1_2[k, ds(mine * 192, 192, 16), :].astype(F32) + inn[k, 0].astype(F32) + inn[k, 1].astype(F32)
        g.w2_2[k] = total.astype(BF)

    def rs2a(w, k):
        axis = ORDERS[k][1]
        for d in (1, 2, 3):
            to, c = near(axis, d)
            send(w, k, 5 + d, window(w2s[w].at[k], PIECES[w][0] * c, 0, PIECES[w]), in2s[w].at[k, d - 1], to)

    def rs2b(w, k):
        mine = near(ORDERS[k][1], 0)[1]
        for d in (1, 2, 3):
            arrived(w, k, 5 + d, in2s[w].at[k, d - 1])
        total = window(w2s[w].at[k], PIECES[w][0] * mine, 0, PIECES[w])[...].astype(F32)
        for d in range(3):
            total = total + in2s[w][k, d].astype(F32)
        w3s[w][k] = total.astype(BF)

    def rs3a(w, k):
        axis = ORDERS[k][2]
        for d in (1, 2, 3):
            to, c = near(axis, d)
            send(w, k, 8 + d, window(w3s[w].at[k], *inner(w, c), SUB), in3s[w].at[k, d - 1], to)

    def out_window(w, k, r, l, shape, c=None):
        c = core if c is None else c
        r0, l0 = (c * 1536, 256 * k) if w == 0 else (0, c * 1536 + 512 * k)
        return window(outs[w], r0 + r, l0 + l, shape)

    def out_block(w, k, c1, cols=None, c=None):
        r, l = block(w, c1)
        if cols is None:
            return out_window(w, k, r, l, BLOCKS[w], c)
        r1, l1 = half_of(w, cols)
        return out_window(w, k, r + r1, l + l1, HALVES[w], c)

    def out_piece(w, k, c1, c2):
        return out_window(w, k, *piece(w, c1, c2), PIECES[w])

    def out_sub(w, k, c1, c2, c3):
        (r, l), (r1, l1) = piece(w, c1, c2), inner(w, c3)
        return out_window(w, k, r + r1, l + l1, SUB)

    def at(k):
        return tuple(near(a, 0)[1] for a in ORDERS[k])

    def rs3b(w, k):
        axis = ORDERS[k][2]
        for d in (1, 2, 3):
            arrived(w, k, 8 + d, in3s[w].at[k, d - 1])
        total = window(w3s[w].at[k], *inner(w, near(axis, 0)[1]), SUB)[...].astype(F32)
        for d in range(3):
            total = total + in3s[w][k, d].astype(F32)
        mine = out_sub(w, k, *at(k))
        mine[...] = total.astype(BF)
        for d in (1, 2, 3):
            send(w, k, 11 + d, mine, mine, near(axis, d)[0])

    def ag3b(w, k):
        c1, c2, _ = at(k)
        for d in (1, 2, 3):
            arrived(w, k, 11 + d, out_sub(w, k, c1, c2, near(ORDERS[k][2], 4 - d)[1]))

    def ag2a(w, k):
        c1, c2, _ = at(k)
        mine = out_piece(w, k, c1, c2)
        for d in (1, 2, 3):
            send(w, k, 14 + d, mine, mine, near(ORDERS[k][1], d)[0])

    def ag2b(w, k):
        c1 = at(k)[0]
        for d in (1, 2, 3):
            arrived(w, k, 14 + d, out_piece(w, k, c1, near(ORDERS[k][1], 4 - d)[1]))

    def ag1a(w, k):
        axis = ORDERS[k][0]
        c1 = at(k)[0]
        for cols, m in ((0, 18), (1, 20)):
            up = out_block(w, k, c1, cols)
            send(w, k, m, up, up, near(axis, 1)[0])
            dn = out_block(w, k, c1, 1 - cols)
            send(w, k, m + 1, dn, dn, near(axis, 3)[0])
        mine = out_block(w, k, c1)
        send(w, k, 24, mine, mine, sibling)

    def ag1b(w, k):
        axis = ORDERS[k][0]
        left, right = near(axis, 3)[1], near(axis, 1)[1]
        a = out_block(w, k, left, 0)
        arrived(w, k, 18, a)
        send(w, k, 22, a, a, near(axis, 1)[0])
        b = out_block(w, k, right, 1)
        arrived(w, k, 19, b)
        send(w, k, 23, b, b, near(axis, 3)[0])
        arrived(w, k, 20, out_block(w, k, left, 1))
        send(w, k, 25, out_block(w, k, left), out_block(w, k, left), sibling)
        arrived(w, k, 21, out_block(w, k, right, 0))
        send(w, k, 26, out_block(w, k, right), out_block(w, k, right), sibling)

    def ag1c(w, k):
        far = near(ORDERS[k][0], 2)[1]
        for cols in range(2):
            v = out_block(w, k, far, cols)
            arrived(w, k, 22 + cols, v)
            send(w, k, 27 + cols, v, v, sibling)

    def sib(w, k):
        axis = ORDERS[k][0]
        for by, m in ((0, 24), (3, 25), (1, 26)):
            arrived(w, k, m, out_block(w, k, near(axis, by)[1], c=1 - core))
        for cols in range(2):
            arrived(w, k, 27 + cols, out_block(w, k, near(axis, 2)[1], cols, c=1 - core))

    def step(w, *fs):
        for f in fs:
            for k in range(3):
                f(w, k)

    def each(f):
        for k in range(3):
            f(k)

    def own_msg(i, src, dst, to):
        return pltpu.make_async_remote_copy(src_ref=src, dst_ref=dst, send_sem=xs_send.at[i], recv_sem=xs_recv.at[i],
                                            device_id=to, device_id_type=MESH)

    def own_rows(part, b):
        return ds(128 * lax.div(b, 2) + 64 * (1 - part) + 32 * lax.rem(b, 2), 32, 16)

    def own_a(part):
        for b in range(4):
            first = 128 * (b // 2) + 64 * (1 - part) + 32 * (b % 2)
            g.own[part, b] = g.dx[first : first + 32, :].astype(BF)
        for by in (1, 2, 3):
            to, c = near(1, by)
            m = own_msg(3 + 6 * part + by - 1, g.own.at[part, c], g.own_in.at[part, by - 1], to)
            m.start()
            started.append(m)

    def own_b(part):
        total = g.own[part, me].astype(F32)
        for by in (1, 2, 3):
            ref = g.own_in.at[part, by - 1]
            own_msg(3 + 6 * part + by - 1, ref, ref, sibling).wait_recv()
            total = total + g.own_in[part, by - 1].astype(F32)
        mine = own_out.at[own_rows(part, me)]
        mine[...] = total.astype(BF)
        for by in (1, 2, 3):
            m = own_msg(6 + 6 * part + by - 1, mine, mine, near(1, by)[0])
            m.start()
            started.append(m)

    def own_c(part):
        for by in (1, 2, 3):
            ref = own_out.at[own_rows(part, near(1, 4 - by)[1])]
            own_msg(6 + 6 * part + by - 1, ref, ref, sibling).wait_recv()

    def small_send(stage):
        n = 1 if stage == 0 else 3
        first = 0 if stage == 0 else 3 * stage - 2
        for k in range(n):
            to = sibling if stage == 0 else near(stage - 1, k + 1)[0]
            c = pltpu.make_async_remote_copy(
                src_ref=g.small_out_v.at[stage], dst_ref=g.small_in.at[first + k], send_sem=xs_send.at[15 + first + k],
                recv_sem=xs_recv.at[15 + first + k], device_id=to, device_id_type=MESH)
            c.start()
            started.append(c)

    def small_take(stage):
        n = 1 if stage == 0 else 3
        first = 0 if stage == 0 else 3 * stage - 2
        total = g.small_out_v[stage]
        for k in range(n):
            ref = g.small_in.at[first + k]
            pltpu.make_async_remote_copy(
                src_ref=ref, dst_ref=ref, send_sem=xs_send.at[15 + first + k],
                recv_sem=xs_recv.at[15 + first + k], device_id=sibling, device_id_type=MESH).wait_recv()
            total = total + g.small_in[first + k]
        g.small_out_v[stage + 1] = total

    g.slot_out[...] = mm(pick, g.dx[...].astype(BF)).astype(BF)
    for by in (1, 2, 3):
        c = pltpu.make_async_remote_copy(
            src_ref=g.slot_out, dst_ref=g.slots.at[me], send_sem=xs_send.at[by - 1], recv_sem=xs_recv.at[by - 1],
            device_id=device(along(pos, 1, by), core), device_id_type=MESH)
        c.start()
        started.append(c)
    g.dx_mini[...] = jnp.zeros((16, D), F32)
    g.e_own[...] = jnp.zeros((16, D), BF)
    g.du_own[...] = jnp.zeros((16, FF), BF)
    g.da_own[...] = jnp.zeros((16, D), BF)
    g.dqkv_own[...] = jnp.zeros((80, 3 * D), BF)
    g.dxm_own[...] = jnp.zeros((16, D), BF)
    g.dxb_own[...] = jnp.zeros((64, D), F32)
    dh_go.wait_recv()
    act_go.wait_recv()
    act_local.wait()
    for k in range(2):
        v = mm_tn(g.f_act[:, 768 * k : 768 * k + 768], g.f_dh[...]).astype(BF)
        for j in range(3):
            g.w1_0[j, 768 * k : 768 * k + 768, :] = v[:, 256 * j : 256 * j + 256]
    each(lambda k: send_first(0, k))
    own_a(0)
    du_go.wait_recv()
    du_local.wait()
    n2_go.wait_recv()
    for k in range(3):
        g.w1_1[k] = mm_tn(g.f_n2[...], g.f_du[:, 512 * k : 512 * k + 512]).astype(BF)
    each(lambda k: send_first(1, k))
    c_act_go.wait_recv()
    c_n2_go.wait_recv()
    each(send_left)
    for by in (1, 2, 3):
        src = near(1, 4 - by)[1]
        pltpu.make_async_remote_copy(
            src_ref=g.slot_out, dst_ref=g.slots.at[src], send_sem=xs_send.at[by - 1], recv_sem=xs_recv.at[by - 1],
            device_id=device(along(pos, 1, by), core), device_id_type=MESH).wait_recv()
    keep = iota((16, D), 0) % 8 <= 5

    def thought_back(i, _):
        t = 2 - i

        @pl.when(t >= me)
        def _():
            e = (g.slots[t + 1].astype(F32) + g.dx_mini[...]).astype(BF).astype(F32)
            e = jnp.where(keep, pltpu.roll(e, 15, 0), 0.0)
            eb = e.astype(BF)
            parts = []
            for k in range(2):
                dm = mm_nt(eb, g.wd[k * 1536 : (k + 1) * 1536, :])
                parts.append((dm * g.gpm[t, :, k * 1536 : (k + 1) * 1536]).astype(BF))
            du = jnp.concatenate(parts, 1)
            dn2 = mm_nt(du, g.wu[...])
            xhat2 = g.xh2m[t]
            dres = e + normalise_back(dn2, row(LN2G), xhat2, g.rs2m[t])
            da = dres.astype(BF)
            dmix = mm_nt(da, g.wo[...]).astype(BF)
            do_s = lane_heads(dmix, 16)
            q_s = lane_heads(g.qkvm[t, :, 0:D], 16)
            p = g.pm[t]
            dp = mm_nt(do_s, g.vall[t])
            ds = (p * (dp - jnp.sum(p * dp, -1, keepdims=True))).astype(BF)
            dq = (join_heads(mm(ds, g.kall[t]), 16) * SCALE).astype(BF)
            dk = (mm_tn(ds, q_s)[0:80] * SCALE).astype(BF)
            dv = mm_tn(p.astype(BF), do_s)[0:80].astype(BF)
            dq = jnp.concatenate([jnp.zeros((64, D), BF), dq], 0)
            dqkv = jnp.concatenate([dq, dk, dv], 1)
            dn1 = mm_nt(dqkv, g.wq[...])
            gain = row(LN1G)
            xhat1 = g.xh1m[t]
            dxm = dres + normalise_back(dn1[64:80], gain, xhat1, g.rs1m[t])
            g.dx_mini[...] = dxm

            @pl.when(t == me)
            def _():
                g.e_own[...] = eb
                g.du_own[...] = du
                g.da_own[...] = da
                g.dqkv_own[...] = dqkv
                g.dxm_own[...] = dxm.astype(BF)
                total = {}
                b0, b1 = g.xh1[0:32, :], g.xh1[128:160, :]
                g.dxb_own[0:32, :] = normalise_back(dn1[0:32], gain, b0, g.rs1[0:32, :])
                g.dxb_own[32:64, :] = normalise_back(dn1[32:64], gain, b1, g.rs1[128:160, :])
                total[LN1G] = column_sum(dn1[0:32] * b0) + column_sum(dn1[32:64] * b1) + column_sum(dn1[64:80] * xhat1)
                total[LN1S] = column_sum(dn1)
                total[BQV] = column_sum(dq.astype(F32))
                total[BQV + 1] = column_sum(dv.astype(F32))
                total[BOUT] = column_sum(da.astype(F32))
                total[LN2G] = column_sum(dn2 * xhat2)
                total[LN2S] = column_sum(dn2)
                total[BDOWN] = column_sum(e)
                for i, v in total.items():
                    g.sums[i : i + 1, :] += v
                for k in range(4):
                    g.sums[BUP + k : BUP + k + 1, :] += column_sum(du[:, k * D : (k + 1) * D].astype(F32))

        return 0

    lax.fori_loop(0, 3, thought_back, 0)

    g.c_e[0:16, :] = g.e_own[...]
    g.c_du[0:16, :] = g.du_own[:, pl.ds(pl.multiple_of(core * 1536, 128), 1536)]
    c_e_go = to_sibling(9, g.c_e.at[mini_lo], g.c_e.at[mini_hi])
    c_du_go = to_sibling(10, half(g.du_own, 1 - core, 1536), g.c_du.at[mini_hi])
    top = [slice(128 * q, 128 * q + TOP) for q in range(2)]
    for q in range(2):
        g.da[top[q], :] = (g.da[top[q], :].astype(F32) + mm(place[q], g.da_own[...])).astype(BF)
        base = jnp.concatenate([g.dqkv_own[32 * q : 32 * q + 32, :].astype(F32), jnp.zeros((16, 3 * D), F32)], 0)
        g.dqkv[top[q], :] = (g.dqkv[top[q], :].astype(F32) + mm(place[q], g.dqkv_own[64:80, :]) + base).astype(BF)
    dq_go = to_sibling(6, half(g.dqo, 1 - core, 1536), g.f_qo.at[hi])
    dq_local = local(4, half(g.dqo, core, 1536), g.f_qo.at[lo])
    c_e_go.wait_recv()
    c_du_go.wait_recv()
    each(send_right)
    g.small_out_v[0] = g.sums[...]
    small_send(0)
    own_b(0)
    later = (me > 0).astype(F32)
    for q, s in ((0, s0), (1, s1)):
        dx = g.dx[top[q], :] + mm(place[q], g.dxm_own[...])
        dx = dx + jnp.concatenate([g.dxb_own[32 * q : 32 * q + 32, :], jnp.zeros((16, D), F32)], 0)
        dx = dx * (1.0 - later * is_slot(s, TOP).astype(F32))
        g.dx[top[q], :] = dx
    dq_local.wait()
    for c in (dq_go, n1_go, o_go):
        c.wait_recv()
    left = mm_tn(g.f_n1[...], g.f_qo[:, 0:768]).astype(BF)
    g.w1_2[0] = left[:, 0:512]
    g.w1_2[1, :, 0:256] = left[:, 512:768]

    def right(factor):
        v = mm_tn(factor[...], g.f_qo[:, 768:1536]).astype(BF)
        g.w1_2[1, :, 256:512] = v[:, 0:256]
        g.w1_2[2] = v[:, 256:768]

    @pl.when(core == 0)
    def _():
        right(g.f_n1)

    @pl.when(core == 1)
    def _():
        right(g.f_o)

    each(ring_a)
    small_take(0)
    small_send(1)
    step(0, sum_first, rs2a)
    step(1, sum_first, rs2a)
    own_a(1)
    each(ring_b)
    step(0, rs2b, rs3a)
    step(1, rs2b, rs3a)
    small_take(1)
    small_send(2)
    each(ring_c)
    step(2, rs2a)
    step(0, rs3b)
    step(1, rs3b)
    own_b(1)
    step(0, ag3b, ag2a)
    step(2, rs2b, rs3a)
    step(1, ag3b, ag2a)
    small_take(2)
    small_send(3)
    step(2, rs3b)
    step(0, ag2b, ag1a)
    step(2, ag3b, ag2a)
    step(1, ag2b, ag1a)
    small_take(3)
    small_out[...] = g.small_out_v[4]
    own_c(0)
    own_c(1)
    step(0, ag1b)
    step(2, ag2b, ag1a)
    step(1, ag1b)
    step(0, ag1c)
    step(1, ag1c)
    step(2, ag1b)
    step(2, ag1c)
    for w in range(3):
        step(w, sib)
    for c in started:
        c.wait_send()


SCRATCH["small_out_v"] = ((5, 16, D), F32)
NAMES.append("small_out_v")


def passes(*args):
    smem = pl.BlockSpec(memory_space=pltpu.SMEM)
    hbm = pl.BlockSpec(memory_space=pl.ANY)
    vmem = pl.BlockSpec(memory_space=pltpu.VMEM)
    dma = pltpu.SemaphoreType.DMA
    return pl.pallas_call(
        kernel,
        out_shape=[
            pltpu.VMEM((ROWS, D), BF),
            pltpu.VMEM((ROWS, D), BF),
            pltpu.VMEM((16, D), F32),
            pltpu.VMEM((D, FF), BF),
            pltpu.VMEM((D, FF), BF),
            pltpu.VMEM((FF, D), BF),
        ],
        in_specs=[smem, smem] + [hbm] * (len(args) - 2),
        out_specs=[vmem] * 6,
        scratch_shapes=[pltpu.VMEM(s, t) for s, t in SCRATCH.values()]
        + [dma((21,)), dma((11,)), dma((11,)), dma((9, NMSG)), dma((9, NMSG)), dma((25,)), dma((25,))],
        compiler_params=pltpu.CompilerParams(
            collective_id=0, has_side_effects=True, vmem_limit_bytes=VMEM_LIMIT
        ),
        name="passes",
    )(*args)


VMEM_LIMIT = 48 * 2**20
SMALL = ((LN1G, 1), (LN1S, 1), (BQV, 2), (BOUT, 1), (LN2G, 1), (LN2S, 1), (BUP, 4), (BDOWN, 1))


def widen_kernel(act, own, small, qo, u, d, act_out, own_out, gq, go, gu, gd, *rest):
    small_outs, (wide, tall, sem, wide_sem, tall_sem) = rest[:8], rest[8:]
    pending = []

    def copy(src, dst, s):
        c = pltpu.make_async_copy(src, dst, s)
        c.start()
        return c

    pending.append(copy(act, act_out, sem.at[0]))
    pending.append(copy(own, own_out, sem.at[1]))
    n = 2
    for (first, count), ref in zip(SMALL, small_outs):
        for k in range(count):
            pending.append(copy(small.at[first + k], ref.at[pl.ds(k * D, D)], sem.at[n]))
            n += 1
    slots = {}

    def chunk(buf, sems, i, value, parts):
        slot = i % buf.shape[0]
        key = (buf is wide, slot)
        for c in slots.get(key, ()):
            c.wait()
        buf[slot] = value.astype(F32)
        slots[key] = [copy(buf.at[slot, :, pl.ds(l0, n)], dst, sems.at[slot, j]) for j, (l0, n, dst) in enumerate(parts)]

    for i in range(12):
        rows = pl.ds(64 * i, 64)
        chunk(wide, wide_sem, 2 * i, qo[64 * i : 64 * i + 64, :], ((0, 3 * D, gq.at[rows]), (3 * D, D, go.at[rows])))
        chunk(tall, tall_sem, i, d[256 * i : 256 * i + 256, :], ((0, D, gd.at[pl.ds(256 * i, 256)]),))
        chunk(wide, wide_sem, 2 * i + 1, u[64 * i : 64 * i + 64, :], ((0, FF, gu.at[rows]),))
    for cs in list(slots.values()) + [pending]:
        for c in cs:
            c.wait()


def widen(*arrays):
    hbm = pl.BlockSpec(memory_space=pl.ANY)
    vmem = pl.BlockSpec(memory_space=pltpu.VMEM)
    dma = pltpu.SemaphoreType.DMA
    shape = jax.ShapeDtypeStruct
    return pl.pallas_call(
        widen_kernel,
        in_specs=[vmem] * 6,
        out_specs=[hbm] * 14,
        out_shape=[shape((ROWS, D), BF), shape((ROWS, D), BF), shape((D, 3 * D), F32), shape((D, D), F32), shape((D, FF), F32),
                   shape((FF, D), F32)] + [shape((n * D,), F32) for _, n in SMALL],
        scratch_shapes=[pltpu.VMEM((6, 64, FF), F32), pltpu.VMEM((3, 256, D), F32), dma((14,)), dma((6, 2)), dma((3, 1))],
        compiler_params=pltpu.CompilerParams(vmem_limit_bytes=24 * 2**20),
        name="widen",
    )(*arrays)


def on_device(embedded, cotangent, lengths, starts, *params):
    gathered = passes(starts, lengths, embedded.reshape(ROWS, D), cotangent.reshape(ROWS, D), *params)
    act, own, gq, go, gu, gd, ln1g, ln1s, bqv, bout, ln2g, ln2s, bup, bdown = widen(*gathered)
    return (act.reshape(1, 2, 128, D), own.reshape(2, 128, D), ln1g, ln1s, gq, bqv, go, bout, ln2g, ln2s, gu, bup, gd, bdown)


def solution(mesh):
    rows = P("batch", None, None)
    passes_rows = P("pass", "batch", None, None)
    return jax.shard_map(
        on_device,
        mesh=mesh,
        in_specs=(rows, passes_rows, P("batch"), P("batch")) + (P(),) * 12,
        out_specs=(passes_rows, rows) + (P(),) * 12,
        check_vma=False,
    )
```

```python
import functools

import jax
import jax.numpy as jnp
from jax import lax
from jax.experimental import pallas as pl
from jax.experimental.pallas import tpu as pltpu
from jax.sharding import PartitionSpec as P

MESH = pl.DeviceIdType.MESH
BF, F32 = jnp.bfloat16, jnp.float32
HEADS = 12
D = 768
FF = 3072
ROWS = 256
TOP = 48
epsilon = 1e-05
SCALE = 0.125

LN1G, LN1S, BQV, BOUT, LN2G, LN2S, BUP, BDOWN = 0, 1, 2, 4, 5, 6, 7, 11

ORDERS = ((0, 1, 2), (1, 2, 0), (2, 0, 1))
NMSG = 32
WAVES = 3
SHAPES = ((1536, 256), (768, 512), (768, 512))
BLOCKS = ((384, 256), (768, 128), (192, 512))
PIECES = ((96, 256), (192, 128), (48, 512))
SUB = (48, 128)


def mm(a, b):
    return jnp.dot(a, b, preferred_element_type=F32)


def mm_nt(a, b):
    return lax.dot_general(a, b, (((1,), (1,)), ((), ())), preferred_element_type=F32)


def mm_tn(a, b):
    return lax.dot_general(a, b, (((0,), (0,)), ((), ())), preferred_element_type=F32)


def normalise(v):
    mu = jnp.sum(v, -1, keepdims=True) * (1.0 / D)
    c = v - mu
    var = jnp.sum(c * c, -1, keepdims=True) * (1.0 / D)
    rs = lax.rsqrt(var + epsilon)
    return c * rs, rs


def normalise_back(grad, gain, xhat, rs):
    gy = grad * gain
    m1 = jnp.sum(gy, -1, keepdims=True) * (1.0 / D)
    m2 = jnp.sum(gy * xhat, -1, keepdims=True) * (1.0 / D)
    return rs * (gy - m1 - xhat * m2)


def gelu_both(u):
    k = 0.7978845608028654
    u2 = u * u
    th = jnp.tanh(k * u * (1.0 + 0.044715 * u2))
    half = 0.5 * (1.0 + th)
    return u * half, half + 0.5 * u * (1.0 - th * th) * (k * (1.0 + 3 * 0.044715 * u2))


def eights(v):
    return jnp.sum(v.reshape(v.shape[0] // 8, 8, v.shape[1]), 0)


def column_sum(v):
    return jnp.sum(eights(v), 0, keepdims=True)


def coords():
    b = lax.axis_index("batch")
    y = lax.axis_index("pass")
    return (lax.div(b, 8), y, lax.rem(lax.div(b, 2), 4)), lax.rem(b, 2)


def device(pos, core):
    x, y, z = pos
    return ((x * 4 + z) * 2 + core, y)


def along(pos, axis, by):
    return tuple(lax.rem(c + by, 4) if i == axis else c for i, c in enumerate(pos))


def iota(shape, dim):
    return lax.broadcasted_iota(jnp.int32, shape, dim)


def lane_heads(v, rows):
    head = iota((rows, D), 1) // 64
    zero = jnp.zeros((rows, D), v.dtype)
    return jnp.concatenate([jnp.where(head == h, v, zero) for h in range(HEADS)], 0)


def join_heads(v, rows):
    head = iota((rows, D), 1) // 64
    total = jnp.zeros((rows, D), F32)
    for h in range(HEADS):
        total = jnp.where(head == h, v[h * rows : (h + 1) * rows], total)
    return total


def pair_rows(v):
    left = iota((128, 128), 1) < 64
    zero = jnp.zeros((128, 128), v.dtype)
    return jnp.concatenate([jnp.where(left, v, zero), jnp.where(left, zero, v)], 0)


def pair_join(v):
    left = iota((128, 128), 1) < 64
    return jnp.where(left, v[:128], v[128:])


SCRATCH = dict(
        par=((16, D), F32),
    xh1=((ROWS, D), F32), rs1=((ROWS, 1), F32), qkv=((ROWS, 3 * D), BF),
    prob=((12, 256, 128), F32), res=((ROWS, D), F32), xh2=((ROWS, D), F32), rs2=((ROWS, 1), F32),
    gp=((ROWS, FF), F32), act=((ROWS, FF), BF),
    tmp=((ROWS, D), F32), dmix=((ROWS, D), BF),
    du=((ROWS, FF), BF), dqo=((ROWS, FF), BF), sums=((16, D), F32),
    xm=((4, 16, D), F32), xh1m=((4, 16, D), F32), rs1m=((4, 16, 1), F32), qkvm=((4, 16, 3 * D), BF),
    kall=((3, 128, D), BF), vall=((3, 128, D), BF), pm=((3, 192, 128), F32),
    xh2m=((3, 16, D), F32), rs2m=((3, 16, 1), F32), gpm=((3, 16, FF), F32),
    slots=((4, 16, D), BF), slot_out=((16, D), BF),
    e_own=((16, D), BF), du_own=((16, FF), BF), dqo_own=((80, FF), BF), c_qo=((80, 1536), BF),
    dx_mini=((16, D), F32), dxm_own=((16, D), BF), dxb_own=((64, D), F32),
    f_n1=((512, D), BF), f_o=((512, D), BF), f_n2=((512, D), BF), f_dh=((512, D), BF),
    f_qo=((512, 1536), BF), f_du=((512, 1536), BF), f_act=((512, 1536), BF),
    w1_0=((3, 1536, 256), BF), w1_1=((3, 768, 512), BF), w1_2=((3, 768, 512), BF),
    relay=((3, 2, 192, 256), BF),
    in1_0=((3, 3, 384, 256), BF), in1_1=((3, 3, 768, 128), BF), in1_2=((3, 2, 192, 512), BF),
    w2_0=((3, 384, 256), BF), w2_1=((3, 768, 128), BF), w2_2=((3, 192, 512), BF),
    in2_0=((3, 3, 96, 256), BF), in2_1=((3, 3, 192, 128), BF), in2_2=((3, 3, 48, 512), BF),
    w3_0=((3, 96, 256), BF), w3_1=((3, 192, 128), BF), w3_2=((3, 48, 512), BF),
    in3_0=((3, 3, 48, 128), BF), in3_1=((3, 3, 48, 128), BF), in3_2=((3, 3, 48, 128), BF),
    spread=((2, 2, TOP, 16), BF), act_mini=((16, FF), BF), c_act=((32, 1536), BF), c_n2=((32, D), BF), c_e=((32, D), BF), c_du=((32, 1536), BF),
    ca_0=((3, 4, 32, 384), BF), cg_0=((3, 4, 32, 256), BF), ca_1=((3, 4, 32, D), BF), cg_1=((3, 4, 32, 128), BF),
    own=((2, 4, 32, D), BF), own_in=((2, 3, 32, D), BF),
    small_in=((10, 16, D), F32),
)
NAMES = list(SCRATCH)


def kernel(start_ref, length_ref, x_hbm, cot_hbm, ln1g_hbm, ln1s_hbm, wq_hbm, bqv_hbm, wo_hbm, bout_hbm, ln2g_hbm, ln2s_hbm,
           wu_hbm, bup_hbm, wd_hbm, bdown_hbm, x_v, own_out, small_out, w_qo, w_u, w_d, *scratch):
    r = dict(zip(NAMES, scratch))
    lsem, fsem, frem, ssem, rsem, xs_send, xs_recv = scratch[len(NAMES):]
    g = type("Refs", (), r)
    g.x_v, g.wu, g.wd = x_v, w_u, w_d
    g.wq, g.wo = w_qo.at[:, pl.ds(0, 3 * D)], w_qo.at[:, pl.ds(3 * D, D)]
    g.dqkv, g.da = g.dqo.at[:, pl.ds(0, 3 * D)], g.dqo.at[:, pl.ds(3 * D, D)]
    g.dx, g.dres, g.dn1, g.out_act = g.res, g.tmp, g.xh2, g.x_v
    g.cot_v = g.f_dh.at[pl.ds(0, 256)]
    pos, core = coords()
    me = pos[1]
    sibling = device(pos, 1 - core)

    barrier = pltpu.get_barrier_semaphore()
    for axis in range(3):
        for by in (1, 2, 3):
            pl.semaphore_signal(barrier, inc=1, device_id=device(along(pos, axis, by), core), device_id_type=MESH)
    pl.semaphore_signal(barrier, inc=1, device_id=sibling, device_id_type=MESH)

    def load(i, src, dst):
        c = pltpu.make_async_copy(src, dst, lsem.at[i])
        c.start()
        return c

    vectors = ((ln1g_hbm, LN1G), (ln1s_hbm, LN1S), (bqv_hbm, BQV), (bout_hbm, BOUT), (ln2g_hbm, LN2G), (ln2s_hbm, LN2S),
               (bup_hbm, BUP), (bdown_hbm, BDOWN))
    x_load = load(0, x_hbm, g.x_v)
    par_loads = []
    for src, first in vectors:
        for k in range(src.shape[0] // D):
            par_loads.append(load(9 + first + k, src.at[pl.ds(k * D, D)], g.par.at[first + k]))
    wq_load = load(2, wq_hbm, g.wq)
    w_loads = [load(3, wo_hbm, g.wo), load(4, wu_hbm, g.wu), load(5, wd_hbm, g.wd)]
    cot_load = load(6, cot_hbm, g.cot_v)

    def row(i, n=1):
        if n == 1:
            return g.par[i : i + 1, :]
        return jnp.concatenate([g.par[i + k : i + k + 1, :] for k in range(n)], 1)

    s0, s1 = start_ref[0], start_ref[1]
    n0, n1 = length_ref[0], length_ref[1]
    r16 = iota((16, 256), 0)
    want = jnp.where(r16 < 8, s0 - 1 + r16, 128 + s1 - 1 + r16 - 8)
    pick = (iota((16, 256), 1) == want).astype(BF)
    col16 = iota((TOP, 16), 1)
    row48 = iota((TOP, 16), 0)
    place = []
    place_slots = []
    for q, s in ((0, s0), (1, s1)):
        i = col16 - 8 * q
        hit = (i >= 0) & (i < 8) & (row48 == s - 1 + i)
        place.append(hit.astype(BF))
        place_slots.append((hit & (i >= 1) & (i <= 6)).astype(BF))

    def is_slot(s, rows):
        j = iota((rows, 1), 0)
        return (j >= s) & (j < s + 6)

    x_load.wait()
    for c in par_loads:
        c.wait()

    def norm_one(i, _):
        rows = pl.ds(pl.multiple_of(i * 32, 32), 32)
        xhat, rs = normalise(g.x_v[rows, :].astype(F32))
        g.xh1[rows, :] = xhat
        g.rs1[rows, :] = rs
        g.f_n1[rows, :] = (xhat * row(LN1G) + row(LN1S)).astype(BF)
        return 0

    lax.fori_loop(0, 8, norm_one, 0)
    wq_load.wait()
    qkv_bias = (row(BQV), jnp.zeros((1, D), F32), row(BQV + 1))
    for k in range(3):
        c = slice(k * D, (k + 1) * D)
        g.qkv[:, c] = (mm(g.f_n1[0:256, :], g.wq[:, c]) + qkv_bias[k]).astype(BF)

    xm = mm(pick, g.x_v[...])
    g.xm[0] = xm
    xhat, rs = normalise(xm)
    g.xh1m[0] = xhat
    g.rs1m[0] = rs
    g.qkvm[0] = mm(pick, g.qkv[...]).astype(BF)
    for t in range(3):
        for buf, lane in ((g.kall, D), (g.vall, 2 * D)):
            buf[t, 0:32, :] = g.qkv[0:32, lane : lane + D]
            buf[t, 32:64, :] = g.qkv[128:160, lane : lane + D]
            buf[t, 80:128, :] = jnp.zeros((48, D), BF)
    for c in w_loads:
        c.wait()

    rr = iota((192, 128), 0) % 16
    cc = iota((192, 128), 1)
    rq, ri = rr // 8, rr % 8
    base_ok = (cc < 64) & (cc // 32 == rq) & (cc % 32 < jnp.where(rq == 0, s0, s1))
    mi = cc - 64
    mini_ok = (mi >= 0) & (mi < 16) & (mi // 8 == rq) & (mi % 8 >= 1) & (mi % 8 <= ri)
    mini_allowed = base_ok | mini_ok
    mini_first = iota((16, D), 0) % 8 == 0

    def thought(t, _):
        g.kall[t, 64:80, :] = g.qkvm[t, :, D : 2 * D]
        g.vall[t, 64:80, :] = g.qkvm[t, :, 2 * D : 3 * D]
        s = mm_nt(lane_heads(g.qkvm[t, :, 0:D], 16), g.kall[t]) * SCALE
        s = jnp.where(mini_allowed, s, -1e30)
        e = jnp.exp(s - jnp.max(s, -1, keepdims=True))
        p = e / jnp.sum(e, -1, keepdims=True)
        g.pm[t] = p
        o = join_heads(mm(p.astype(BF), g.vall[t]), 16).astype(BF)
        res = g.xm[t] + mm(o, g.wo[...]) + row(BOUT)
        xhat, rs = normalise(res)
        g.xh2m[t] = xhat
        g.rs2m[t] = rs
        n2 = (xhat * row(LN2G) + row(LN2S)).astype(BF)
        parts = []
        for k in range(2):
            u = mm(n2, g.wu[:, k * 1536 : (k + 1) * 1536]) + row(BUP + 2 * k, 2)
            m, slope = gelu_both(u)
            g.gpm[t, :, k * 1536 : (k + 1) * 1536] = slope
            parts.append(m.astype(BF))
        h = res + mm(jnp.concatenate(parts, 1), g.wd[...]) + row(BDOWN)
        h = h.astype(BF).astype(F32)
        nxt = jnp.where(mini_first, g.xm[t], pltpu.roll(h, 1, 0))
        g.xm[t + 1] = nxt
        xhat, rs = normalise(nxt)
        g.xh1m[t + 1] = xhat
        g.rs1m[t + 1] = rs
        n1 = (xhat * row(LN1G) + row(LN1S)).astype(BF)
        for k in range(3):
            c = slice(k * D, (k + 1) * D)
            g.qkvm[t + 1, :, c] = (mm(n1, g.wq[:, c]) + qkv_bias[k]).astype(BF)
        return 0

    lax.fori_loop(0, 3, thought, 0)

    for q, s in ((0, s0), (1, s1)):
        rows = slice(128 * q, 128 * q + TOP)
        slot = is_slot(s, TOP)
        x = jnp.where(slot, mm(place_slots[q], g.xm[me].astype(BF)), g.x_v[rows, :].astype(F32))
        g.x_v[rows, :] = x.astype(BF)
        xhat, rs = normalise(x)
        g.xh1[rows, :] = xhat
        g.rs1[rows, :] = rs
        g.f_n1[rows, :] = (xhat * row(LN1G) + row(LN1S)).astype(BF)
        g.qkv[rows, :] = jnp.where(slot, mm(place_slots[q], g.qkvm[me]), g.qkv[rows, :].astype(F32)).astype(BF)

    qi = iota((256, 128), 0) % 128
    kj = iota((256, 128), 1)

    def attend(q, _):
        rows = pl.ds(pl.multiple_of(q * 128, 128), 128)
        ok = (kj <= qi) & (kj < jnp.where(q == 0, n0, n1))
        for hp in range(6):
            lanes = slice(128 * hp, 128 * hp + 128)
            q2 = pair_rows(g.qkv[rows, lanes])
            s = mm_nt(q2, g.qkv[rows, D + 128 * hp : D + 128 * hp + 128]) * SCALE
            s = jnp.where(ok, s, -1e30)
            e = jnp.exp(s - jnp.max(s, -1, keepdims=True))
            p = e / jnp.sum(e, -1, keepdims=True)
            g.prob[q * 6 + hp] = p
            o2 = mm(p.astype(BF), g.qkv[rows, 2 * D + 128 * hp : 2 * D + 128 * hp + 128])
            g.f_o[rows, lanes] = pair_join(o2).astype(BF)
        return 0

    lax.fori_loop(0, 2, attend, 0)

    g.tmp[...] = mm(g.f_o[0:256, :], g.wo[...])

    def norm_two(i, _):
        rows = pl.ds(pl.multiple_of(i * 32, 32), 32)
        res = g.x_v[rows, :].astype(F32) + g.tmp[rows, :] + row(BOUT)
        g.res[rows, :] = res
        xhat, rs = normalise(res)
        g.xh2[rows, :] = xhat
        g.rs2[rows, :] = rs
        g.f_n2[rows, :] = (xhat * row(LN2G) + row(LN2S)).astype(BF)
        return 0

    lax.fori_loop(0, 8, norm_two, 0)
    for k in range(4):
        c = slice(k * D, (k + 1) * D)
        m, slope = gelu_both(mm(g.f_n2[0:256, :], g.wu[:, c]) + row(BUP + k))
        g.gp[:, c] = slope
        g.act[:, c] = m.astype(BF)
    g.out_act[...] = (g.res[...] + mm(g.act[...], g.wd[...]) + row(BDOWN)).astype(BF)

    pl.semaphore_wait(barrier, 10)
    lo, hi = pl.ds(0, 256), pl.ds(256, 256)
    started = []

    def to_sibling(i, src, dst):
        c = pltpu.make_async_remote_copy(src_ref=src, dst_ref=dst, send_sem=fsem.at[i], recv_sem=frem.at[i],
                                         device_id=sibling, device_id_type=MESH)
        c.start()
        started.append(c)
        return c

    def local(i, src, dst):
        c = pltpu.make_async_copy(src, dst, lsem.at[i])
        c.start()
        return c

    def half(ref, which, width):
        return ref.at[:, pl.ds(pl.multiple_of(which * width, 128), width)]

    mini_lo, mini_hi = pl.ds(0, 16), pl.ds(16, 16)
    g.act_mini[...] = mm(pick, g.act[...]).astype(BF)
    g.c_act[0:16, :] = g.act_mini[:, pl.ds(pl.multiple_of(core * 1536, 128), 1536)]
    g.c_n2[0:16, :] = mm(pick, g.f_n2[0:256, :]).astype(BF)
    for q in range(2):
        g.spread[0, q] = place[q]
    spread_go = to_sibling(11, g.spread.at[0], g.spread.at[1])
    c_act_go = to_sibling(7, half(g.act_mini, 1 - core, 1536), g.c_act.at[mini_hi])
    c_n2_go = to_sibling(12, g.c_n2.at[mini_lo], g.c_n2.at[mini_hi])
    cot_load.wait()
    dh_go = to_sibling(4, g.f_dh.at[lo], g.f_dh.at[hi])
    act_go = to_sibling(3, half(g.act, 1 - core, 1536), g.f_act.at[hi])
    act_local = local(1, half(g.act, core, 1536), g.f_act.at[lo])
    n2_go = to_sibling(2, g.f_n2.at[lo], g.f_n2.at[hi])
    n1_go = to_sibling(0, g.f_n1.at[lo], g.f_n1.at[hi])
    o_go = to_sibling(1, g.f_o.at[lo], g.f_o.at[hi])

    def msg(w, k, m, src, dst, to):
        i = 3 * w + k
        return pltpu.make_async_remote_copy(src_ref=src, dst_ref=dst, send_sem=ssem.at[i, m], recv_sem=rsem.at[i, m],
                                            device_id=to, device_id_type=MESH)

    def send(w, k, m, src, dst, to):
        c = msg(w, k, m, src, dst, to)
        c.start()
        started.append(c)

    def arrived(w, k, m, dst):
        msg(w, k, m, dst, dst, sibling).wait_recv()

    w1s, in1s = (g.w1_0, g.w1_1, g.w1_2), (g.in1_0, g.in1_1, g.in1_2)
    w2s, in2s = (g.w2_0, g.w2_1, g.w2_2), (g.in2_0, g.in2_1, g.in2_2)
    w3s, in3s = (g.w3_0, g.w3_1, g.w3_2), (g.in3_0, g.in3_1, g.in3_2)
    cas, cgs = (g.ca_0, g.ca_1), (g.cg_0, g.cg_1)
    outs = (w_d, w_u, w_qo)
    memo = {}

    def near(axis, by):
        if (axis, by) not in memo:
            there = along(pos, axis, by)
            memo[axis, by] = (device(there, core), there[axis])
        return memo[axis, by]

    def ds(i, n, m):
        return pl.ds(i if isinstance(i, int) else pl.multiple_of(i, m), n)

    def window(ref, r0, l0, shape):
        return ref.at[ds(r0, shape[0], 16), ds(l0, shape[1], 128)]

    def block(w, c1):
        return ((384 * c1, 0), (0, 128 * c1), (192 * c1, 0))[w]

    def piece(w, c1, c2):
        r, l = block(w, c1)
        return r + PIECES[w][0] * c2, l

    def inner(w, c3):
        return ((48 * lax.div(c3, 2), 128 * lax.rem(c3, 2)), (48 * c3, 0), (0, 128 * c3))[w]

    HALVES = ((384, 128), (384, 128), (192, 256))

    def half_of(w, cols):
        return ((0, 128 * cols), (384 * cols, 0), (0, 256 * cols))[w]

    def send_first(w, k):
        axis = ORDERS[k][0]
        for d in (1, 2, 3):
            to, c = near(axis, d)
            send(w, k, d - 1, window(w1s[w].at[k], *block(w, c), BLOCKS[w]), in1s[w].at[k, d - 1], to)

    def send_left(k):
        axis = ORDERS[k][0]
        mine = near(axis, 0)[1]
        g.ca_0[k, 0] = g.c_act[:, ds(384 * mine, 384, 128)]
        g.ca_1[k, 0] = g.c_n2[...]
        for d in (1, 2, 3):
            to, c = near(axis, d)
            send(0, k, 2 + d, window(g.c_act, 0, 384 * c, (32, 384)), g.ca_0.at[k, d], to)
            send(1, k, 2 + d, g.c_n2, g.ca_1.at[k, d], to)

    def send_right(k):
        axis = ORDERS[k][0]
        mine = near(axis, 0)[1]
        g.cg_0[k, 0] = g.c_e[:, 256 * k : 256 * k + 256]
        g.cg_1[k, 0] = g.c_du[:, ds(512 * k + 128 * mine, 128, 128)]
        for d in (1, 2, 3):
            to, c = near(axis, d)
            send(0, k, 28 + d, window(g.c_e, 0, 256 * k, (32, 256)), g.cg_0.at[k, d], to)
            send(1, k, 28 + d, window(g.c_du, 0, 512 * k + 128 * c, (32, 128)), g.cg_1.at[k, d], to)

    def sum_first(w, k):
        mine = near(ORDERS[k][0], 0)[1]
        for d in (1, 2, 3):
            arrived(w, k, 2 + d, cas[w].at[k, d])
            arrived(w, k, 28 + d, cgs[w].at[k, d])
            arrived(w, k, d - 1, in1s[w].at[k, d - 1])
        n = BLOCKS[w][0]
        total = mm_tn(cas[w][k].reshape(128, n), cgs[w][k].reshape(128, BLOCKS[w][1]))
        total = total + window(w1s[w].at[k], *block(w, mine), BLOCKS[w])[...].astype(F32)
        for d in range(3):
            total = total + in1s[w][k, d].astype(F32)
        w2s[w][k] = total.astype(BF)

    A, B = pl.ds(0, 256), pl.ds(256, 256)

    def ring_a(k):
        axis = ORDERS[k][0]
        w1, inn = g.w1_2.at[k], g.in1_2.at[k]
        (up, c_up), (dn, c_dn), (_, far) = near(axis, 1), near(axis, 3), near(axis, 2)

        def blk(c):
            return ds(c * 192, 192, 16)

        send(2, k, 0, w1.at[blk(far), A], g.relay.at[k, 0], up)
        send(2, k, 1, w1.at[blk(far), B], g.relay.at[k, 1], dn)
        send(2, k, 2, w1.at[blk(c_up), B], inn.at[0, :, B], up)
        send(2, k, 3, w1.at[blk(c_dn), A], inn.at[1, :, A], dn)

    def ring_b(k):
        axis = ORDERS[k][0]
        for side, by, cols in ((0, 1, A), (1, 3, B)):
            to, c = near(axis, by)
            arrived(2, k, side, g.relay.at[k, side])
            g.relay[k, side] = (g.relay[k, side].astype(F32) + g.w1_2[k, ds(c * 192, 192, 16), cols].astype(F32)).astype(BF)
            send(2, k, 4 + side, g.relay.at[k, side], g.in1_2.at[k, side, :, cols], to)

    def ring_c(k):
        inn = g.in1_2
        arrived(2, k, 2, inn.at[k, 0, :, B])
        arrived(2, k, 3, inn.at[k, 1, :, A])
        arrived(2, k, 4, inn.at[k, 0, :, A])
        arrived(2, k, 5, inn.at[k, 1, :, B])
        mine = near(ORDERS[k][0], 0)[1]
        total = g.w1_2[k, ds(mine * 192, 192, 16), :].astype(F32) + inn[k, 0].astype(F32) + inn[k, 1].astype(F32)
        g.w2_2[k] = total.astype(BF)

    def rs2a(w, k):
        axis = ORDERS[k][1]
        for d in (1, 2, 3):
            to, c = near(axis, d)
            send(w, k, 5 + d, window(w2s[w].at[k], PIECES[w][0] * c, 0, PIECES[w]), in2s[w].at[k, d - 1], to)

    def rs2b(w, k):
        mine = near(ORDERS[k][1], 0)[1]
        for d in (1, 2, 3):
            arrived(w, k, 5 + d, in2s[w].at[k, d - 1])
        total = window(w2s[w].at[k], PIECES[w][0] * mine, 0, PIECES[w])[...].astype(F32)
        for d in range(3):
            total = total + in2s[w][k, d].astype(F32)
        w3s[w][k] = total.astype(BF)

    def rs3a(w, k):
        axis = ORDERS[k][2]
        for d in (1, 2, 3):
            to, c = near(axis, d)
            send(w, k, 8 + d, window(w3s[w].at[k], *inner(w, c), SUB), in3s[w].at[k, d - 1], to)

    def out_window(w, k, r, l, shape, c=None):
        c = core if c is None else c
        r0, l0 = (c * 1536, 256 * k) if w == 0 else (0, c * 1536 + 512 * k)
        return window(outs[w], r0 + r, l0 + l, shape)

    def out_block(w, k, c1, cols=None, c=None):
        r, l = block(w, c1)
        if cols is None:
            return out_window(w, k, r, l, BLOCKS[w], c)
        r1, l1 = half_of(w, cols)
        return out_window(w, k, r + r1, l + l1, HALVES[w], c)

    def out_piece(w, k, c1, c2):
        return out_window(w, k, *piece(w, c1, c2), PIECES[w])

    def out_sub(w, k, c1, c2, c3):
        (r, l), (r1, l1) = piece(w, c1, c2), inner(w, c3)
        return out_window(w, k, r + r1, l + l1, SUB)

    def at(k):
        return tuple(near(a, 0)[1] for a in ORDERS[k])

    def rs3b(w, k):
        axis = ORDERS[k][2]
        for d in (1, 2, 3):
            arrived(w, k, 8 + d, in3s[w].at[k, d - 1])
        total = window(w3s[w].at[k], *inner(w, near(axis, 0)[1]), SUB)[...].astype(F32)
        for d in range(3):
            total = total + in3s[w][k, d].astype(F32)
        mine = out_sub(w, k, *at(k))
        mine[...] = total.astype(BF)
        for d in (1, 2, 3):
            send(w, k, 11 + d, mine, mine, near(axis, d)[0])

    def ag3b(w, k):
        c1, c2, _ = at(k)
        for d in (1, 2, 3):
            arrived(w, k, 11 + d, out_sub(w, k, c1, c2, near(ORDERS[k][2], 4 - d)[1]))

    def ag2a(w, k):
        c1, c2, _ = at(k)
        mine = out_piece(w, k, c1, c2)
        for d in (1, 2, 3):
            send(w, k, 14 + d, mine, mine, near(ORDERS[k][1], d)[0])

    def ag2b(w, k):
        c1 = at(k)[0]
        for d in (1, 2, 3):
            arrived(w, k, 14 + d, out_piece(w, k, c1, near(ORDERS[k][1], 4 - d)[1]))

    def ag1a(w, k):
        axis = ORDERS[k][0]
        c1 = at(k)[0]
        for cols, m in ((0, 18), (1, 20)):
            up = out_block(w, k, c1, cols)
            send(w, k, m, up, up, near(axis, 1)[0])
            dn = out_block(w, k, c1, 1 - cols)
            send(w, k, m + 1, dn, dn, near(axis, 3)[0])
        mine = out_block(w, k, c1)
        send(w, k, 24, mine, mine, sibling)

    def ag1b(w, k):
        axis = ORDERS[k][0]
        left, right = near(axis, 3)[1], near(axis, 1)[1]
        a = out_block(w, k, left, 0)
        arrived(w, k, 18, a)
        send(w, k, 22, a, a, near(axis, 1)[0])
        b = out_block(w, k, right, 1)
        arrived(w, k, 19, b)
        send(w, k, 23, b, b, near(axis, 3)[0])
        arrived(w, k, 20, out_block(w, k, left, 1))
        send(w, k, 25, out_block(w, k, left), out_block(w, k, left), sibling)
        arrived(w, k, 21, out_block(w, k, right, 0))
        send(w, k, 26, out_block(w, k, right), out_block(w, k, right), sibling)

    def ag1c(w, k):
        far = near(ORDERS[k][0], 2)[1]
        for cols in range(2):
            v = out_block(w, k, far, cols)
            arrived(w, k, 22 + cols, v)
            send(w, k, 27 + cols, v, v, sibling)

    def sib(w, k):
        axis = ORDERS[k][0]
        for by, m in ((0, 24), (3, 25), (1, 26)):
            arrived(w, k, m, out_block(w, k, near(axis, by)[1], c=1 - core))
        for cols in range(2):
            arrived(w, k, 27 + cols, out_block(w, k, near(axis, 2)[1], cols, c=1 - core))

    def step(w, *fs):
        for f in fs:
            for k in range(3):
                f(w, k)

    def each(f):
        for k in range(3):
            f(k)

    def own_msg(i, src, dst, to):
        return pltpu.make_async_remote_copy(src_ref=src, dst_ref=dst, send_sem=xs_send.at[i], recv_sem=xs_recv.at[i],
                                            device_id=to, device_id_type=MESH)

    def own_rows(part, b):
        return ds(128 * lax.div(b, 2) + 64 * (1 - part) + 32 * lax.rem(b, 2), 32, 16)

    def own_a(part):
        for b in range(4):
            first = 128 * (b // 2) + 64 * (1 - part) + 32 * (b % 2)
            g.own[part, b] = g.dx[first : first + 32, :].astype(BF)
        for by in (1, 2, 3):
            to, c = near(1, by)
            m = own_msg(3 + 6 * part + by - 1, g.own.at[part, c], g.own_in.at[part, by - 1], to)
            m.start()
            started.append(m)

    def own_b(part):
        total = g.own[part, me].astype(F32)
        for by in (1, 2, 3):
            ref = g.own_in.at[part, by - 1]
            own_msg(3 + 6 * part + by - 1, ref, ref, sibling).wait_recv()
            total = total + g.own_in[part, by - 1].astype(F32)
        mine = own_out.at[own_rows(part, me)]
        mine[...] = total.astype(BF)
        for by in (1, 2, 3):
            m = own_msg(6 + 6 * part + by - 1, mine, mine, near(1, by)[0])
            m.start()
            started.append(m)

    def own_c(part):
        for by in (1, 2, 3):
            ref = own_out.at[own_rows(part, near(1, 4 - by)[1])]
            own_msg(6 + 6 * part + by - 1, ref, ref, sibling).wait_recv()

    def small_send(stage):
        n = 1 if stage == 0 else 3
        first = 0 if stage == 0 else 3 * stage - 2
        for k in range(n):
            to = sibling if stage == 0 else near(stage - 1, k + 1)[0]
            c = pltpu.make_async_remote_copy(
                src_ref=g.small_out_v.at[stage], dst_ref=g.small_in.at[first + k], send_sem=xs_send.at[15 + first + k],
                recv_sem=xs_recv.at[15 + first + k], device_id=to, device_id_type=MESH)
            c.start()
            started.append(c)

    def small_take(stage):
        n = 1 if stage == 0 else 3
        first = 0 if stage == 0 else 3 * stage - 2
        total = g.small_out_v[stage]
        for k in range(n):
            ref = g.small_in.at[first + k]
            pltpu.make_async_remote_copy(
                src_ref=ref, dst_ref=ref, send_sem=xs_send.at[15 + first + k],
                recv_sem=xs_recv.at[15 + first + k], device_id=sibling, device_id_type=MESH).wait_recv()
            total = total + g.small_in[first + k]
        g.small_out_v[stage + 1] = total

    for k in range(4):
        c = slice(k * D, (k + 1) * D)
        du = (mm_nt(g.cot_v[...], g.wd[c, :]) * g.gp[:, c]).astype(BF)
        g.du[:, c] = du
        g.sums[BUP + k : BUP + k + 1, :] = column_sum(du.astype(F32))
    du_go = to_sibling(5, half(g.du, 1 - core, 1536), g.f_du.at[hi])
    du_local = local(3, half(g.du, core, 1536), g.f_du.at[lo])
    g.sums[BDOWN : BDOWN + 1, :] = column_sum(g.cot_v[...].astype(F32))
    c_act_go.wait_recv()
    c_n2_go.wait_recv()
    each(send_left)
    g.tmp[...] = mm_nt(g.du[...], g.wu[...])
    zero8 = jnp.zeros((8, D), F32)

    def back_two(i, acc):
        rows = pl.ds(pl.multiple_of(i * 32, 32), 32)
        dn = g.tmp[rows, :]
        xhat = g.xh2[rows, :]
        dres = g.cot_v[rows, :].astype(F32) + normalise_back(dn, row(LN2G), xhat, g.rs2[rows, :])
        g.dres[rows, :] = dres
        da = dres.astype(BF)
        g.da[rows, :] = da
        return acc[0] + eights(dn * xhat), acc[1] + eights(dn), acc[2] + eights(da.astype(F32))

    acc = lax.fori_loop(0, 8, back_two, (zero8, zero8, zero8))
    for i, a in zip((LN2G, LN2S, BOUT), acc):
        g.sums[i : i + 1, :] = jnp.sum(a, 0, keepdims=True)
    g.dmix[...] = mm_nt(g.da[...], g.wo[...]).astype(BF)

    def attend_back(q, _):
        rows = pl.ds(pl.multiple_of(q * 128, 128), 128)
        for hp in range(6):
            lanes = slice(128 * hp, 128 * hp + 128)
            klanes = slice(D + 128 * hp, D + 128 * hp + 128)
            vlanes = slice(2 * D + 128 * hp, 2 * D + 128 * hp + 128)
            do2 = pair_rows(g.dmix[rows, lanes])
            p = g.prob[q * 6 + hp]
            dp = mm_nt(do2, g.qkv[rows, vlanes])
            ds = (p * (dp - jnp.sum(p * dp, -1, keepdims=True))).astype(BF)
            g.dqkv[rows, lanes] = (pair_join(mm(ds, g.qkv[rows, klanes])) * SCALE).astype(BF)
            g.dqkv[rows, klanes] = (mm_tn(ds, pair_rows(g.qkv[rows, lanes])) * SCALE).astype(BF)
            g.dqkv[rows, vlanes] = mm_tn(p.astype(BF), do2).astype(BF)
        return 0

    lax.fori_loop(0, 2, attend_back, 0)
    g.dn1[...] = mm_nt(g.dqkv[...], g.wq[...])

    def back_one(i, acc):
        rows = pl.ds(pl.multiple_of(i * 32, 32), 32)
        dn = g.dn1[rows, :]
        xhat = g.xh1[rows, :]
        g.dx[rows, :] = g.dres[rows, :] + normalise_back(dn, row(LN1G), xhat, g.rs1[rows, :])
        dq = eights(g.dqkv[rows, 0:D].astype(F32))
        dv = eights(g.dqkv[rows, 2 * D : 3 * D].astype(F32))
        return acc[0] + eights(dn * xhat), acc[1] + eights(dn), acc[2] + dq, acc[3] + dv

    acc = lax.fori_loop(0, 8, back_one, (zero8, zero8, zero8, zero8))
    for i, a in zip((LN1G, LN1S, BQV, BQV + 1), acc):
        g.sums[i : i + 1, :] = jnp.sum(a, 0, keepdims=True)

    g.slot_out[...] = mm(pick, g.dx[...].astype(BF)).astype(BF)
    for by in (1, 2, 3):
        c = pltpu.make_async_remote_copy(
            src_ref=g.slot_out, dst_ref=g.slots.at[me], send_sem=xs_send.at[by - 1], recv_sem=xs_recv.at[by - 1],
            device_id=device(along(pos, 1, by), core), device_id_type=MESH)
        c.start()
        started.append(c)
    g.dx_mini[...] = jnp.zeros((16, D), F32)
    g.e_own[...] = jnp.zeros((16, D), BF)
    g.du_own[...] = jnp.zeros((16, FF), BF)
    g.dqo_own[...] = jnp.zeros((80, FF), BF)
    g.dxm_own[...] = jnp.zeros((16, D), BF)
    g.dxb_own[...] = jnp.zeros((64, D), F32)
    dh_go.wait_recv()
    act_go.wait_recv()
    act_local.wait()
    for k in range(2):
        v = mm_tn(g.f_act[:, 768 * k : 768 * k + 768], g.f_dh[...]).astype(BF)
        for j in range(3):
            g.w1_0[j, 768 * k : 768 * k + 768, :] = v[:, 256 * j : 256 * j + 256]
    each(lambda k: send_first(0, k))
    own_a(0)
    du_go.wait_recv()
    du_local.wait()
    n2_go.wait_recv()
    for k in range(3):
        g.w1_1[k] = mm_tn(g.f_n2[...], g.f_du[:, 512 * k : 512 * k + 512]).astype(BF)
    each(lambda k: send_first(1, k))
    dq_go = to_sibling(6, half(g.dqo, 1 - core, 1536), g.f_qo.at[hi])
    dq_local = local(4, half(g.dqo, core, 1536), g.f_qo.at[lo])
    for by in (1, 2, 3):
        src = near(1, 4 - by)[1]
        pltpu.make_async_remote_copy(
            src_ref=g.slot_out, dst_ref=g.slots.at[src], send_sem=xs_send.at[by - 1], recv_sem=xs_recv.at[by - 1],
            device_id=device(along(pos, 1, by), core), device_id_type=MESH).wait_recv()
    keep = iota((16, D), 0) % 8 <= 5

    def thought_back(i, _):
        t = 2 - i

        @pl.when(t >= me)
        def _():
            e = (g.slots[t + 1].astype(F32) + g.dx_mini[...]).astype(BF).astype(F32)
            e = jnp.where(keep, pltpu.roll(e, 15, 0), 0.0)
            eb = e.astype(BF)
            parts = []
            for k in range(2):
                dm = mm_nt(eb, g.wd[k * 1536 : (k + 1) * 1536, :])
                parts.append((dm * g.gpm[t, :, k * 1536 : (k + 1) * 1536]).astype(BF))
            du = jnp.concatenate(parts, 1)
            dn2 = mm_nt(du, g.wu[...])
            xhat2 = g.xh2m[t]
            dres = e + normalise_back(dn2, row(LN2G), xhat2, g.rs2m[t])
            da = dres.astype(BF)
            dmix = mm_nt(da, g.wo[...]).astype(BF)
            do_s = lane_heads(dmix, 16)
            q_s = lane_heads(g.qkvm[t, :, 0:D], 16)
            p = g.pm[t]
            dp = mm_nt(do_s, g.vall[t])
            ds = (p * (dp - jnp.sum(p * dp, -1, keepdims=True))).astype(BF)
            dq = (join_heads(mm(ds, g.kall[t]), 16) * SCALE).astype(BF)
            dk = (mm_tn(ds, q_s)[0:80] * SCALE).astype(BF)
            dv = mm_tn(p.astype(BF), do_s)[0:80].astype(BF)
            dq = jnp.concatenate([jnp.zeros((64, D), BF), dq], 0)
            dqkv = jnp.concatenate([dq, dk, dv], 1)
            dn1 = mm_nt(dqkv, g.wq[...])
            gain = row(LN1G)
            xhat1 = g.xh1m[t]
            dxm = dres + normalise_back(dn1[64:80], gain, xhat1, g.rs1m[t])
            g.dx_mini[...] = dxm

            @pl.when(t == me)
            def _():
                g.e_own[...] = eb
                g.du_own[...] = du
                g.dqo_own[:, 0 : 3 * D] = dqkv
                g.dqo_own[64:80, 3 * D : FF] = da
                g.dxm_own[...] = dxm.astype(BF)
                total = {}
                b0, b1 = g.xh1[0:32, :], g.xh1[128:160, :]
                g.dxb_own[0:32, :] = normalise_back(dn1[0:32], gain, b0, g.rs1[0:32, :])
                g.dxb_own[32:64, :] = normalise_back(dn1[32:64], gain, b1, g.rs1[128:160, :])
                total[LN1G] = column_sum(dn1[0:32] * b0) + column_sum(dn1[32:64] * b1) + column_sum(dn1[64:80] * xhat1)
                total[LN1S] = column_sum(dn1)
                total[BQV] = column_sum(dq.astype(F32))
                total[BQV + 1] = column_sum(dv.astype(F32))
                total[BOUT] = column_sum(da.astype(F32))
                total[LN2G] = column_sum(dn2 * xhat2)
                total[LN2S] = column_sum(dn2)
                total[BDOWN] = column_sum(e)
                for i, v in total.items():
                    g.sums[i : i + 1, :] += v
                for k in range(4):
                    g.sums[BUP + k : BUP + k + 1, :] += column_sum(du[:, k * D : (k + 1) * D].astype(F32))

        return 0

    lax.fori_loop(0, 3, thought_back, 0)

    g.c_e[0:16, :] = g.e_own[...]
    g.c_du[0:16, :] = g.du_own[:, pl.ds(pl.multiple_of(core * 1536, 128), 1536)]
    c_e_go = to_sibling(9, g.c_e.at[mini_lo], g.c_e.at[mini_hi])
    c_du_go = to_sibling(10, half(g.du_own, 1 - core, 1536), g.c_du.at[mini_hi])
    c_qo_go = to_sibling(8, half(g.dqo_own, 1 - core, 1536), g.c_qo)
    top = [slice(128 * q, 128 * q + TOP) for q in range(2)]

    def merge(first, own, cols, q, spread):
        rows = slice(first + 128 * q, first + 128 * q + TOP)
        base = jnp.concatenate([own[32 * q : 32 * q + 32, cols].astype(F32), jnp.zeros((16, 1536), F32)], 0)
        g.f_qo[rows, :] = (g.f_qo[rows, :].astype(F32) + mm(spread, own[64:80, cols]) + base).astype(BF)

    dq_local.wait()
    for q in range(2):
        merge(0, g.dqo_own, pl.ds(pl.multiple_of(core * 1536, 128), 1536), q, place[q])
    c_e_go.wait_recv()
    c_du_go.wait_recv()
    each(send_right)
    for c in (dq_go, c_qo_go, n1_go, o_go, spread_go):
        c.wait_recv()
    for q in range(2):
        merge(256, g.c_qo, slice(None), q, g.spread[1, q])
    left = mm_tn(g.f_n1[...], g.f_qo[:, 0:768]).astype(BF)
    g.w1_2[0] = left[:, 0:512]
    g.w1_2[1, :, 0:256] = left[:, 512:768]

    def right(factor):
        v = mm_tn(factor[...], g.f_qo[:, 768:1536]).astype(BF)
        g.w1_2[1, :, 256:512] = v[:, 0:256]
        g.w1_2[2] = v[:, 256:768]

    @pl.when(core == 0)
    def _():
        right(g.f_n1)

    @pl.when(core == 1)
    def _():
        right(g.f_o)

    each(ring_a)
    step(0, sum_first, rs2a)
    step(1, sum_first, rs2a)
    g.small_out_v[0] = g.sums[...]
    small_send(0)
    each(ring_b)
    later = (me > 0).astype(F32)
    for q, s in ((0, s0), (1, s1)):
        dx = g.dx[top[q], :] + mm(place[q], g.dxm_own[...])
        dx = dx + jnp.concatenate([g.dxb_own[32 * q : 32 * q + 32, :], jnp.zeros((16, D), F32)], 0)
        dx = dx * (1.0 - later * is_slot(s, TOP).astype(F32))
        g.dx[top[q], :] = dx
    own_a(1)
    own_b(0)
    step(0, rs2b, rs3a)
    step(1, rs2b, rs3a)
    small_take(0)
    small_send(1)
    each(ring_c)
    step(2, rs2a)
    step(0, rs3b)
    step(1, rs3b)
    small_take(1)
    small_send(2)
    step(2, rs2b, rs3a)
    step(0, ag3b, ag2a)
    step(1, ag3b, ag2a)
    own_b(1)
    step(2, rs3b)
    step(0, ag2b, ag1a)
    small_take(2)
    small_send(3)
    step(2, ag3b, ag2a)
    step(1, ag2b, ag1a)
    step(0, ag1b)
    step(2, ag2b, ag1a)
    step(1, ag1b)
    step(0, ag1c)
    small_take(3)
    small_out[...] = g.small_out_v[4]
    own_c(0)
    own_c(1)
    step(1, ag1c)
    step(2, ag1b)
    step(2, ag1c)
    for w in range(3):
        step(w, sib)
    for c in started:
        c.wait_send()


SCRATCH["small_out_v"] = ((5, 16, D), F32)
NAMES.append("small_out_v")


def passes(*args):
    smem = pl.BlockSpec(memory_space=pltpu.SMEM)
    hbm = pl.BlockSpec(memory_space=pl.ANY)
    vmem = pl.BlockSpec(memory_space=pltpu.VMEM)
    dma = pltpu.SemaphoreType.DMA
    return pl.pallas_call(
        kernel,
        out_shape=[
            pltpu.VMEM((ROWS, D), BF),
            pltpu.VMEM((ROWS, D), BF),
            pltpu.VMEM((16, D), F32),
            pltpu.VMEM((D, FF), BF),
            pltpu.VMEM((D, FF), BF),
            pltpu.VMEM((FF, D), BF),
        ],
        in_specs=[smem, smem] + [hbm] * (len(args) - 2),
        out_specs=[vmem] * 6,
        scratch_shapes=[pltpu.VMEM(s, t) for s, t in SCRATCH.values()]
        + [dma((21,)), dma((13,)), dma((13,)), dma((9, NMSG)), dma((9, NMSG)), dma((25,)), dma((25,))],
        compiler_params=pltpu.CompilerParams(
            collective_id=0, has_side_effects=True, vmem_limit_bytes=VMEM_LIMIT
        ),
        name="passes",
    )(*args)


VMEM_LIMIT = 48 * 2**20
SMALL = ((LN1G, 1), (LN1S, 1), (BQV, 2), (BOUT, 1), (LN2G, 1), (LN2S, 1), (BUP, 4), (BDOWN, 1))


def widen_kernel(act, own, small, qo, u, d, act_out, own_out, gq, go, gu, gd, *rest):
    small_outs, (wide, tall, sem, wide_sem, tall_sem) = rest[:8], rest[8:]
    pending = []

    def copy(src, dst, s):
        c = pltpu.make_async_copy(src, dst, s)
        c.start()
        return c

    pending.append(copy(act, act_out, sem.at[0]))
    pending.append(copy(own, own_out, sem.at[1]))
    n = 2
    for (first, count), ref in zip(SMALL, small_outs):
        for k in range(count):
            pending.append(copy(small.at[first + k], ref.at[pl.ds(k * D, D)], sem.at[n]))
            n += 1
    slots = {}

    def chunk(buf, sems, i, value, parts):
        slot = i % buf.shape[0]
        key = (buf is wide, slot)
        for c in slots.get(key, ()):
            c.wait()
        buf[slot] = value.astype(F32)
        slots[key] = [copy(buf.at[slot, :, pl.ds(l0, n)], dst, sems.at[slot, j]) for j, (l0, n, dst) in enumerate(parts)]

    for i in range(12):
        rows = pl.ds(64 * i, 64)
        chunk(wide, wide_sem, 2 * i, qo[64 * i : 64 * i + 64, :], ((0, 3 * D, gq.at[rows]), (3 * D, D, go.at[rows])))
        chunk(tall, tall_sem, i, d[256 * i : 256 * i + 256, :], ((0, D, gd.at[pl.ds(256 * i, 256)]),))
        chunk(wide, wide_sem, 2 * i + 1, u[64 * i : 64 * i + 64, :], ((0, FF, gu.at[rows]),))
    for cs in list(slots.values()) + [pending]:
        for c in cs:
            c.wait()


def widen(*arrays):
    hbm = pl.BlockSpec(memory_space=pl.ANY)
    vmem = pl.BlockSpec(memory_space=pltpu.VMEM)
    dma = pltpu.SemaphoreType.DMA
    shape = jax.ShapeDtypeStruct
    return pl.pallas_call(
        widen_kernel,
        in_specs=[vmem] * 6,
        out_specs=[hbm] * 14,
        out_shape=[shape((ROWS, D), BF), shape((ROWS, D), BF), shape((D, 3 * D), F32), shape((D, D), F32), shape((D, FF), F32),
                   shape((FF, D), F32)] + [shape((n * D,), F32) for _, n in SMALL],
        scratch_shapes=[pltpu.VMEM((6, 64, FF), F32), pltpu.VMEM((3, 256, D), F32), dma((14,)), dma((6, 2)), dma((3, 1))],
        compiler_params=pltpu.CompilerParams(vmem_limit_bytes=24 * 2**20),
        name="widen",
    )(*arrays)


def on_device(embedded, cotangent, lengths, starts, *params):
    gathered = passes(starts, lengths, embedded.reshape(ROWS, D), cotangent.reshape(ROWS, D), *params)
    act, own, gq, go, gu, gd, ln1g, ln1s, bqv, bout, ln2g, ln2s, bup, bdown = widen(*gathered)
    return (act.reshape(1, 2, 128, D), own.reshape(2, 128, D), ln1g, ln1s, gq, bqv, go, bout, ln2g, ln2s, gu, bup, gd, bdown)


def solution(mesh):
    rows = P("batch", None, None)
    passes_rows = P("pass", "batch", None, None)
    return jax.shard_map(
        on_device,
        mesh=mesh,
        in_specs=(rows, passes_rows, P("batch"), P("batch")) + (P(),) * 12,
        out_specs=(passes_rows, rows) + (P(),) * 12,
        check_vma=False,
    )
```

```python
import functools

import jax
import jax.numpy as jnp
from jax import lax
from jax.experimental import pallas as pl
from jax.experimental.pallas import tpu as pltpu
from jax.sharding import PartitionSpec as P

MESH = pl.DeviceIdType.MESH
BF, F32 = jnp.bfloat16, jnp.float32
HEADS = 12
D = 768
FF = 3072
ROWS = 256
TOP = 48
epsilon = 1e-05
SCALE = 0.125

LN1G, LN1S, BQV, BOUT, LN2G, LN2S, BUP, BDOWN = 0, 1, 2, 4, 5, 6, 7, 11

ORDERS = ((0, 1, 2), (1, 2, 0), (2, 0, 1))
NMSG = 32
WAVES = 3
SHAPES = ((1536, 256), (768, 512), (768, 512))
BLOCKS = ((384, 256), (768, 128), (192, 512))
PIECES = ((96, 256), (192, 128), (48, 512))
SUB = (48, 128)


def mm(a, b):
    return jnp.dot(a, b, preferred_element_type=F32)


def mm_nt(a, b):
    return lax.dot_general(a, b, (((1,), (1,)), ((), ())), preferred_element_type=F32)


def mm_tn(a, b):
    return lax.dot_general(a, b, (((0,), (0,)), ((), ())), preferred_element_type=F32)


def normalise(v):
    mu = jnp.sum(v, -1, keepdims=True) * (1.0 / D)
    c = v - mu
    var = jnp.sum(c * c, -1, keepdims=True) * (1.0 / D)
    rs = lax.rsqrt(var + epsilon)
    return c * rs, rs


def normalise_back(grad, gain, xhat, rs):
    gy = grad * gain
    m1 = jnp.sum(gy, -1, keepdims=True) * (1.0 / D)
    m2 = jnp.sum(gy * xhat, -1, keepdims=True) * (1.0 / D)
    return rs * (gy - m1 - xhat * m2)


def gelu_both(u):
    k = 0.7978845608028654
    u2 = u * u
    th = jnp.tanh(k * u * (1.0 + 0.044715 * u2))
    half = 0.5 * (1.0 + th)
    return u * half, half + 0.5 * u * (1.0 - th * th) * (k * (1.0 + 3 * 0.044715 * u2))


def eights(v):
    return jnp.sum(v.reshape(v.shape[0] // 8, 8, v.shape[1]), 0)


def column_sum(v):
    return jnp.sum(eights(v), 0, keepdims=True)


def coords():
    b = lax.axis_index("batch")
    y = lax.axis_index("pass")
    return (lax.div(b, 8), y, lax.rem(lax.div(b, 2), 4)), lax.rem(b, 2)


def device(pos, core):
    x, y, z = pos
    return ((x * 4 + z) * 2 + core, y)


def along(pos, axis, by):
    return tuple(lax.rem(c + by, 4) if i == axis else c for i, c in enumerate(pos))


def iota(shape, dim):
    return lax.broadcasted_iota(jnp.int32, shape, dim)


def lane_heads(v, rows):
    head = iota((rows, D), 1) // 64
    zero = jnp.zeros((rows, D), v.dtype)
    return jnp.concatenate([jnp.where(head == h, v, zero) for h in range(HEADS)], 0)


def join_heads(v, rows):
    head = iota((rows, D), 1) // 64
    total = jnp.zeros((rows, D), F32)
    for h in range(HEADS):
        total = jnp.where(head == h, v[h * rows : (h + 1) * rows], total)
    return total


def pair_rows(v):
    left = iota((128, 128), 1) < 64
    zero = jnp.zeros((128, 128), v.dtype)
    return jnp.concatenate([jnp.where(left, v, zero), jnp.where(left, zero, v)], 0)


def pair_join(v):
    left = iota((128, 128), 1) < 64
    return jnp.where(left, v[:128], v[128:])


SCRATCH = dict(
        par=((16, D), F32),
    xh1=((ROWS, D), F32), rs1=((ROWS, 1), F32), qkv=((ROWS, 3 * D), BF),
    prob=((12, 256, 128), F32), res=((ROWS, D), F32), xh2=((ROWS, D), F32), rs2=((ROWS, 1), F32),
    gp=((ROWS, FF), F32), act=((ROWS, FF), BF),
    tmp=((ROWS, D), F32), dmix=((ROWS, D), BF),
    du=((ROWS, FF), BF), dqo=((ROWS, FF), BF), sums=((16, D), F32),
    xm=((4, 16, D), F32), xh1m=((4, 16, D), F32), rs1m=((4, 16, 1), F32), qkvm=((4, 16, 3 * D), BF),
    kall=((3, 128, D), BF), vall=((3, 128, D), BF), pm=((3, 192, 128), F32),
    xh2m=((3, 16, D), F32), rs2m=((3, 16, 1), F32), gpm=((3, 16, FF), F32),
    slots=((4, 16, D), BF), slot_out=((16, D), BF),
    e_own=((16, D), BF), du_own=((16, FF), BF), dqo_own=((80, FF), BF), c_qo=((80, 1536), BF),
    dx_mini=((16, D), F32), dxm_own=((16, D), BF), dxb_own=((64, D), F32),
    f_n1=((512, D), BF), f_o=((512, D), BF), f_n2=((512, D), BF), f_dh=((512, D), BF),
    f_qo=((512, 1536), BF), f_du=((512, 1536), BF), f_act=((512, 1536), BF),
    w1_0=((3, 1536, 256), BF), w1_1=((3, 768, 512), BF), w1_2=((3, 768, 512), BF),
    relay=((3, 2, 192, 256), BF),
    in1_0=((3, 3, 384, 256), BF), in1_1=((3, 3, 768, 128), BF), in1_2=((3, 2, 192, 512), BF),
    w2_0=((3, 384, 256), BF), w2_1=((3, 768, 128), BF), w2_2=((3, 192, 512), BF),
    in2_0=((3, 3, 96, 256), BF), in2_1=((3, 3, 192, 128), BF), in2_2=((3, 3, 48, 512), BF),
    w3_0=((3, 96, 256), BF), w3_1=((3, 192, 128), BF), w3_2=((3, 48, 512), BF),
    in3_0=((3, 3, 48, 128), BF), in3_1=((3, 3, 48, 128), BF), in3_2=((3, 3, 48, 128), BF),
    spread=((2, 2, TOP, 16), BF), act_mini=((16, FF), BF), c_act=((32, 1536), BF), c_n2=((32, D), BF), c_e=((32, D), BF), c_du=((32, 1536), BF),
    ca_0=((3, 4, 32, 384), BF), cg_0=((3, 4, 32, 256), BF), ca_1=((3, 4, 32, D), BF), cg_1=((3, 4, 32, 128), BF),
    own=((2, 4, 32, D), BF), own_in=((2, 3, 32, D), BF),
    small_in=((10, 16, D), F32),
)
NAMES = list(SCRATCH)


def kernel(start_ref, length_ref, x_hbm, cot_hbm, ln1g_hbm, ln1s_hbm, wq_hbm, bqv_hbm, wo_hbm, bout_hbm, ln2g_hbm, ln2s_hbm,
           wu_hbm, bup_hbm, wd_hbm, bdown_hbm, x_v, own_out, small_out, w_qo, w_u, w_d, *scratch):
    r = dict(zip(NAMES, scratch))
    lsem, fsem, frem, ssem, rsem, xs_send, xs_recv = scratch[len(NAMES):]
    g = type("Refs", (), r)
    g.x_v, g.wu, g.wd = x_v, w_u, w_d
    g.wq, g.wo = w_qo.at[:, pl.ds(0, 3 * D)], w_qo.at[:, pl.ds(3 * D, D)]
    g.dqkv, g.da = g.dqo.at[:, pl.ds(0, 3 * D)], g.dqo.at[:, pl.ds(3 * D, D)]
    g.dx, g.dres, g.dn1, g.out_act = g.res, g.tmp, g.xh2, g.x_v
    g.cot_v = g.f_dh.at[pl.ds(0, 256)]
    pos, core = coords()
    me = pos[1]
    sibling = device(pos, 1 - core)

    barrier = pltpu.get_barrier_semaphore()
    for axis in range(3):
        for by in (1, 2, 3):
            pl.semaphore_signal(barrier, inc=1, device_id=device(along(pos, axis, by), core), device_id_type=MESH)
    pl.semaphore_signal(barrier, inc=1, device_id=sibling, device_id_type=MESH)

    def load(i, src, dst):
        c = pltpu.make_async_copy(src, dst, lsem.at[i])
        c.start()
        return c

    vectors = ((ln1g_hbm, LN1G), (ln1s_hbm, LN1S), (bqv_hbm, BQV), (bout_hbm, BOUT), (ln2g_hbm, LN2G), (ln2s_hbm, LN2S),
               (bup_hbm, BUP), (bdown_hbm, BDOWN))
    x_load = load(0, x_hbm, g.x_v)
    par_loads = []
    for src, first in vectors:
        for k in range(src.shape[0] // D):
            par_loads.append(load(9 + first + k, src.at[pl.ds(k * D, D)], g.par.at[first + k]))
    wq_load = load(2, wq_hbm, g.wq)
    w_loads = [load(3, wo_hbm, g.wo), load(4, wu_hbm, g.wu), load(5, wd_hbm, g.wd)]
    cot_load = load(6, cot_hbm, g.cot_v)

    def row(i, n=1):
        if n == 1:
            return g.par[i : i + 1, :]
        return jnp.concatenate([g.par[i + k : i + k + 1, :] for k in range(n)], 1)

    s0, s1 = start_ref[0], start_ref[1]
    n0, n1 = length_ref[0], length_ref[1]
    r16 = iota((16, 256), 0)
    want = jnp.where(r16 < 8, s0 - 1 + r16, 128 + s1 - 1 + r16 - 8)
    pick = (iota((16, 256), 1) == want).astype(BF)
    col16 = iota((TOP, 16), 1)
    row48 = iota((TOP, 16), 0)
    place = []
    place_slots = []
    for q, s in ((0, s0), (1, s1)):
        i = col16 - 8 * q
        hit = (i >= 0) & (i < 8) & (row48 == s - 1 + i)
        place.append(hit.astype(BF))
        place_slots.append((hit & (i >= 1) & (i <= 6)).astype(BF))

    def is_slot(s, rows):
        j = iota((rows, 1), 0)
        return (j >= s) & (j < s + 6)

    x_load.wait()
    for c in par_loads:
        c.wait()

    def norm_one(i, _):
        rows = pl.ds(pl.multiple_of(i * 64, 64), 64)
        xhat, rs = normalise(g.x_v[rows, :].astype(F32))
        g.xh1[rows, :] = xhat
        g.rs1[rows, :] = rs
        g.f_n1[rows, :] = (xhat * row(LN1G) + row(LN1S)).astype(BF)
        return 0

    lax.fori_loop(0, 4, norm_one, 0)
    wq_load.wait()
    qkv_bias = (row(BQV), jnp.zeros((1, D), F32), row(BQV + 1))
    for k in range(3):
        c = slice(k * D, (k + 1) * D)
        g.qkv[:, c] = (mm(g.f_n1[0:256, :], g.wq[:, c]) + qkv_bias[k]).astype(BF)

    xm = mm(pick, g.x_v[...])
    g.xm[0] = xm
    xhat, rs = normalise(xm)
    g.xh1m[0] = xhat
    g.rs1m[0] = rs
    g.qkvm[0] = mm(pick, g.qkv[...]).astype(BF)
    for t in range(3):
        for buf, lane in ((g.kall, D), (g.vall, 2 * D)):
            buf[t, 0:32, :] = g.qkv[0:32, lane : lane + D]
            buf[t, 32:64, :] = g.qkv[128:160, lane : lane + D]
            buf[t, 80:128, :] = jnp.zeros((48, D), BF)
    for c in w_loads:
        c.wait()

    rr = iota((192, 128), 0) % 16
    cc = iota((192, 128), 1)
    rq, ri = rr // 8, rr % 8
    base_ok = (cc < 64) & (cc // 32 == rq) & (cc % 32 < jnp.where(rq == 0, s0, s1))
    mi = cc - 64
    mini_ok = (mi >= 0) & (mi < 16) & (mi // 8 == rq) & (mi % 8 >= 1) & (mi % 8 <= ri)
    mini_allowed = base_ok | mini_ok
    mini_first = iota((16, D), 0) % 8 == 0

    def thought(t, _):
        g.kall[t, 64:80, :] = g.qkvm[t, :, D : 2 * D]
        g.vall[t, 64:80, :] = g.qkvm[t, :, 2 * D : 3 * D]
        s = mm_nt(lane_heads(g.qkvm[t, :, 0:D], 16), g.kall[t]) * SCALE
        s = jnp.where(mini_allowed, s, -1e30)
        e = jnp.exp(s - jnp.max(s, -1, keepdims=True))
        p = e / jnp.sum(e, -1, keepdims=True)
        g.pm[t] = p
        o = join_heads(mm(p.astype(BF), g.vall[t]), 16).astype(BF)
        res = g.xm[t] + mm(o, g.wo[...]) + row(BOUT)
        xhat, rs = normalise(res)
        g.xh2m[t] = xhat
        g.rs2m[t] = rs
        n2 = (xhat * row(LN2G) + row(LN2S)).astype(BF)
        parts = []
        for k in range(2):
            u = mm(n2, g.wu[:, k * 1536 : (k + 1) * 1536]) + row(BUP + 2 * k, 2)
            m, slope = gelu_both(u)
            g.gpm[t, :, k * 1536 : (k + 1) * 1536] = slope
            parts.append(m.astype(BF))
        h = res + mm(jnp.concatenate(parts, 1), g.wd[...]) + row(BDOWN)
        h = h.astype(BF).astype(F32)
        nxt = jnp.where(mini_first, g.xm[t], pltpu.roll(h, 1, 0))
        g.xm[t + 1] = nxt
        xhat, rs = normalise(nxt)
        g.xh1m[t + 1] = xhat
        g.rs1m[t + 1] = rs
        n1 = (xhat * row(LN1G) + row(LN1S)).astype(BF)
        for k in range(3):
            c = slice(k * D, (k + 1) * D)
            g.qkvm[t + 1, :, c] = (mm(n1, g.wq[:, c]) + qkv_bias[k]).astype(BF)
        return 0

    lax.fori_loop(0, 3, thought, 0)

    for q, s in ((0, s0), (1, s1)):
        rows = slice(128 * q, 128 * q + TOP)
        slot = is_slot(s, TOP)
        x = jnp.where(slot, mm(place_slots[q], g.xm[me].astype(BF)), g.x_v[rows, :].astype(F32))
        g.x_v[rows, :] = x.astype(BF)
        xhat, rs = normalise(x)
        g.xh1[rows, :] = xhat
        g.rs1[rows, :] = rs
        g.f_n1[rows, :] = (xhat * row(LN1G) + row(LN1S)).astype(BF)
        g.qkv[rows, :] = jnp.where(slot, mm(place_slots[q], g.qkvm[me]), g.qkv[rows, :].astype(F32)).astype(BF)

    qi = iota((256, 128), 0) % 128
    kj = iota((256, 128), 1)

    def attend(q, _):
        rows = pl.ds(pl.multiple_of(q * 128, 128), 128)
        ok = (kj <= qi) & (kj < jnp.where(q == 0, n0, n1))
        for hp in range(6):
            lanes = slice(128 * hp, 128 * hp + 128)
            q2 = pair_rows(g.qkv[rows, lanes])
            s = mm_nt(q2, g.qkv[rows, D + 128 * hp : D + 128 * hp + 128]) * SCALE
            s = jnp.where(ok, s, -1e30)
            e = jnp.exp(s - jnp.max(s, -1, keepdims=True))
            p = e / jnp.sum(e, -1, keepdims=True)
            g.prob[q * 6 + hp] = p
            o2 = mm(p.astype(BF), g.qkv[rows, 2 * D + 128 * hp : 2 * D + 128 * hp + 128])
            g.f_o[rows, lanes] = pair_join(o2).astype(BF)
        return 0

    lax.fori_loop(0, 2, attend, 0)

    g.tmp[...] = mm(g.f_o[0:256, :], g.wo[...])

    def norm_two(i, _):
        rows = pl.ds(pl.multiple_of(i * 64, 64), 64)
        res = g.x_v[rows, :].astype(F32) + g.tmp[rows, :] + row(BOUT)
        g.res[rows, :] = res
        xhat, rs = normalise(res)
        g.xh2[rows, :] = xhat
        g.rs2[rows, :] = rs
        g.f_n2[rows, :] = (xhat * row(LN2G) + row(LN2S)).astype(BF)
        return 0

    lax.fori_loop(0, 4, norm_two, 0)
    for k in range(4):
        c = slice(k * D, (k + 1) * D)
        m, slope = gelu_both(mm(g.f_n2[0:256, :], g.wu[:, c]) + row(BUP + k))
        g.gp[:, c] = slope
        g.act[:, c] = m.astype(BF)
    g.out_act[...] = (g.res[...] + mm(g.act[...], g.wd[...]) + row(BDOWN)).astype(BF)

    pl.semaphore_wait(barrier, 10)
    lo, hi = pl.ds(0, 256), pl.ds(256, 256)
    started = []

    def to_sibling(i, src, dst):
        c = pltpu.make_async_remote_copy(src_ref=src, dst_ref=dst, send_sem=fsem.at[i], recv_sem=frem.at[i],
                                         device_id=sibling, device_id_type=MESH)
        c.start()
        started.append(c)
        return c

    def local(i, src, dst):
        c = pltpu.make_async_copy(src, dst, lsem.at[i])
        c.start()
        return c

    def half(ref, which, width):
        return ref.at[:, pl.ds(pl.multiple_of(which * width, 128), width)]

    mini_lo, mini_hi = pl.ds(0, 16), pl.ds(16, 16)
    g.act_mini[...] = mm(pick, g.act[...]).astype(BF)
    g.c_act[0:16, :] = g.act_mini[:, pl.ds(pl.multiple_of(core * 1536, 128), 1536)]
    g.c_n2[0:16, :] = mm(pick, g.f_n2[0:256, :]).astype(BF)
    for q in range(2):
        g.spread[0, q] = place[q]
    spread_go = to_sibling(11, g.spread.at[0], g.spread.at[1])
    c_act_go = to_sibling(7, half(g.act_mini, 1 - core, 1536), g.c_act.at[mini_hi])
    c_n2_go = to_sibling(12, g.c_n2.at[mini_lo], g.c_n2.at[mini_hi])
    cot_load.wait()
    dh_go = to_sibling(4, g.f_dh.at[lo], g.f_dh.at[hi])
    act_go = to_sibling(3, half(g.act, 1 - core, 1536), g.f_act.at[hi])
    act_local = local(1, half(g.act, core, 1536), g.f_act.at[lo])
    n2_go = to_sibling(2, g.f_n2.at[lo], g.f_n2.at[hi])
    n1_go = to_sibling(0, g.f_n1.at[lo], g.f_n1.at[hi])
    o_go = to_sibling(1, g.f_o.at[lo], g.f_o.at[hi])

    def msg(w, k, m, src, dst, to):
        i = 3 * w + k
        return pltpu.make_async_remote_copy(src_ref=src, dst_ref=dst, send_sem=ssem.at[i, m], recv_sem=rsem.at[i, m],
                                            device_id=to, device_id_type=MESH)

    def send(w, k, m, src, dst, to):
        c = msg(w, k, m, src, dst, to)
        c.start()
        started.append(c)

    def arrived(w, k, m, dst):
        msg(w, k, m, dst, dst, sibling).wait_recv()

    w1s, in1s = (g.w1_0, g.w1_1, g.w1_2), (g.in1_0, g.in1_1, g.in1_2)
    w2s, in2s = (g.w2_0, g.w2_1, g.w2_2), (g.in2_0, g.in2_1, g.in2_2)
    w3s, in3s = (g.w3_0, g.w3_1, g.w3_2), (g.in3_0, g.in3_1, g.in3_2)
    cas, cgs = (g.ca_0, g.ca_1), (g.cg_0, g.cg_1)
    outs = (w_d, w_u, w_qo)
    memo = {}

    def near(axis, by):
        if (axis, by) not in memo:
            there = along(pos, axis, by)
            memo[axis, by] = (device(there, core), there[axis])
        return memo[axis, by]

    def ds(i, n, m):
        return pl.ds(i if isinstance(i, int) else pl.multiple_of(i, m), n)

    def window(ref, r0, l0, shape):
        return ref.at[ds(r0, shape[0], 16), ds(l0, shape[1], 128)]

    def block(w, c1):
        return ((384 * c1, 0), (0, 128 * c1), (192 * c1, 0))[w]

    def piece(w, c1, c2):
        r, l = block(w, c1)
        return r + PIECES[w][0] * c2, l

    def inner(w, c3):
        return ((48 * lax.div(c3, 2), 128 * lax.rem(c3, 2)), (48 * c3, 0), (0, 128 * c3))[w]

    HALVES = ((384, 128), (384, 128), (192, 256))

    def half_of(w, cols):
        return ((0, 128 * cols), (384 * cols, 0), (0, 256 * cols))[w]

    def send_first(w, k):
        axis = ORDERS[k][0]
        for d in (1, 2, 3):
            to, c = near(axis, d)
            send(w, k, d - 1, window(w1s[w].at[k], *block(w, c), BLOCKS[w]), in1s[w].at[k, d - 1], to)

    def send_left(k):
        axis = ORDERS[k][0]
        mine = near(axis, 0)[1]
        g.ca_0[k, 0] = g.c_act[:, ds(384 * mine, 384, 128)]
        g.ca_1[k, 0] = g.c_n2[...]
        for d in (1, 2, 3):
            to, c = near(axis, d)
            send(0, k, 2 + d, window(g.c_act, 0, 384 * c, (32, 384)), g.ca_0.at[k, d], to)
            send(1, k, 2 + d, g.c_n2, g.ca_1.at[k, d], to)

    def send_right(k):
        axis = ORDERS[k][0]
        mine = near(axis, 0)[1]
        g.cg_0[k, 0] = g.c_e[:, 256 * k : 256 * k + 256]
        g.cg_1[k, 0] = g.c_du[:, ds(512 * k + 128 * mine, 128, 128)]
        for d in (1, 2, 3):
            to, c = near(axis, d)
            send(0, k, 28 + d, window(g.c_e, 0, 256 * k, (32, 256)), g.cg_0.at[k, d], to)
            send(1, k, 28 + d, window(g.c_du, 0, 512 * k + 128 * c, (32, 128)), g.cg_1.at[k, d], to)

    def sum_first(w, k):
        mine = near(ORDERS[k][0], 0)[1]
        for d in (1, 2, 3):
            arrived(w, k, 2 + d, cas[w].at[k, d])
            arrived(w, k, 28 + d, cgs[w].at[k, d])
            arrived(w, k, d - 1, in1s[w].at[k, d - 1])
        n = BLOCKS[w][0]
        total = mm_tn(cas[w][k].reshape(128, n), cgs[w][k].reshape(128, BLOCKS[w][1]))
        total = total + window(w1s[w].at[k], *block(w, mine), BLOCKS[w])[...].astype(F32)
        for d in range(3):
            total = total + in1s[w][k, d].astype(F32)
        w2s[w][k] = total.astype(BF)

    A, B = pl.ds(0, 256), pl.ds(256, 256)

    def ring_a(k):
        axis = ORDERS[k][0]
        w1, inn = g.w1_2.at[k], g.in1_2.at[k]
        (up, c_up), (dn, c_dn), (_, far) = near(axis, 1), near(axis, 3), near(axis, 2)

        def blk(c):
            return ds(c * 192, 192, 16)

        send(2, k, 0, w1.at[blk(far), A], g.relay.at[k, 0], up)
        send(2, k, 1, w1.at[blk(far), B], g.relay.at[k, 1], dn)
        send(2, k, 2, w1.at[blk(c_up), B], inn.at[0, :, B], up)
        send(2, k, 3, w1.at[blk(c_dn), A], inn.at[1, :, A], dn)

    def ring_b(k):
        axis = ORDERS[k][0]
        for side, by, cols in ((0, 1, A), (1, 3, B)):
            to, c = near(axis, by)
            arrived(2, k, side, g.relay.at[k, side])
            g.relay[k, side] = (g.relay[k, side].astype(F32) + g.w1_2[k, ds(c * 192, 192, 16), cols].astype(F32)).astype(BF)
            send(2, k, 4 + side, g.relay.at[k, side], g.in1_2.at[k, side, :, cols], to)

    def ring_c(k):
        inn = g.in1_2
        arrived(2, k, 2, inn.at[k, 0, :, B])
        arrived(2, k, 3, inn.at[k, 1, :, A])
        arrived(2, k, 4, inn.at[k, 0, :, A])
        arrived(2, k, 5, inn.at[k, 1, :, B])
        mine = near(ORDERS[k][0], 0)[1]
        total = g.w1_2[k, ds(mine * 192, 192, 16), :].astype(F32) + inn[k, 0].astype(F32) + inn[k, 1].astype(F32)
        g.w2_2[k] = total.astype(BF)

    def rs2a(w, k):
        axis = ORDERS[k][1]
        for d in (1, 2, 3):
            to, c = near(axis, d)
            send(w, k, 5 + d, window(w2s[w].at[k], PIECES[w][0] * c, 0, PIECES[w]), in2s[w].at[k, d - 1], to)

    def rs2b(w, k):
        mine = near(ORDERS[k][1], 0)[1]
        for d in (1, 2, 3):
            arrived(w, k, 5 + d, in2s[w].at[k, d - 1])
        total = window(w2s[w].at[k], PIECES[w][0] * mine, 0, PIECES[w])[...].astype(F32)
        for d in range(3):
            total = total + in2s[w][k, d].astype(F32)
        w3s[w][k] = total.astype(BF)

    def rs3a(w, k):
        axis = ORDERS[k][2]
        for d in (1, 2, 3):
            to, c = near(axis, d)
            send(w, k, 8 + d, window(w3s[w].at[k], *inner(w, c), SUB), in3s[w].at[k, d - 1], to)

    def out_window(w, k, r, l, shape, c=None):
        c = core if c is None else c
        r0, l0 = (c * 1536, 256 * k) if w == 0 else (0, c * 1536 + 512 * k)
        return window(outs[w], r0 + r, l0 + l, shape)

    def out_block(w, k, c1, cols=None, c=None):
        r, l = block(w, c1)
        if cols is None:
            return out_window(w, k, r, l, BLOCKS[w], c)
        r1, l1 = half_of(w, cols)
        return out_window(w, k, r + r1, l + l1, HALVES[w], c)

    def out_piece(w, k, c1, c2):
        return out_window(w, k, *piece(w, c1, c2), PIECES[w])

    def out_sub(w, k, c1, c2, c3):
        (r, l), (r1, l1) = piece(w, c1, c2), inner(w, c3)
        return out_window(w, k, r + r1, l + l1, SUB)

    def at(k):
        return tuple(near(a, 0)[1] for a in ORDERS[k])

    def rs3b(w, k):
        axis = ORDERS[k][2]
        for d in (1, 2, 3):
            arrived(w, k, 8 + d, in3s[w].at[k, d - 1])
        total = window(w3s[w].at[k], *inner(w, near(axis, 0)[1]), SUB)[...].astype(F32)
        for d in range(3):
            total = total + in3s[w][k, d].astype(F32)
        mine = out_sub(w, k, *at(k))
        mine[...] = total.astype(BF)
        for d in (1, 2, 3):
            send(w, k, 11 + d, mine, mine, near(axis, d)[0])

    def ag3b(w, k):
        c1, c2, _ = at(k)
        for d in (1, 2, 3):
            arrived(w, k, 11 + d, out_sub(w, k, c1, c2, near(ORDERS[k][2], 4 - d)[1]))

    def ag2a(w, k):
        c1, c2, _ = at(k)
        mine = out_piece(w, k, c1, c2)
        for d in (1, 2, 3):
            send(w, k, 14 + d, mine, mine, near(ORDERS[k][1], d)[0])

    def ag2b(w, k):
        c1 = at(k)[0]
        for d in (1, 2, 3):
            arrived(w, k, 14 + d, out_piece(w, k, c1, near(ORDERS[k][1], 4 - d)[1]))

    def ag1a(w, k):
        axis = ORDERS[k][0]
        c1 = at(k)[0]
        for cols, m in ((0, 18), (1, 20)):
            up = out_block(w, k, c1, cols)
            send(w, k, m, up, up, near(axis, 1)[0])
            dn = out_block(w, k, c1, 1 - cols)
            send(w, k, m + 1, dn, dn, near(axis, 3)[0])
        mine = out_block(w, k, c1)
        send(w, k, 24, mine, mine, sibling)

    def ag1b(w, k):
        axis = ORDERS[k][0]
        left, right = near(axis, 3)[1], near(axis, 1)[1]
        a = out_block(w, k, left, 0)
        arrived(w, k, 18, a)
        send(w, k, 22, a, a, near(axis, 1)[0])
        b = out_block(w, k, right, 1)
        arrived(w, k, 19, b)
        send(w, k, 23, b, b, near(axis, 3)[0])
        arrived(w, k, 20, out_block(w, k, left, 1))
        send(w, k, 25, out_block(w, k, left), out_block(w, k, left), sibling)
        arrived(w, k, 21, out_block(w, k, right, 0))
        send(w, k, 26, out_block(w, k, right), out_block(w, k, right), sibling)

    def ag1c(w, k):
        far = near(ORDERS[k][0], 2)[1]
        for cols in range(2):
            v = out_block(w, k, far, cols)
            arrived(w, k, 22 + cols, v)
            send(w, k, 27 + cols, v, v, sibling)

    def sib(w, k):
        axis = ORDERS[k][0]
        for by, m in ((0, 24), (3, 25), (1, 26)):
            arrived(w, k, m, out_block(w, k, near(axis, by)[1], c=1 - core))
        for cols in range(2):
            arrived(w, k, 27 + cols, out_block(w, k, near(axis, 2)[1], cols, c=1 - core))

    def step(w, *fs):
        for f in fs:
            for k in range(3):
                f(w, k)

    def each(f):
        for k in range(3):
            f(k)

    def own_msg(i, src, dst, to):
        return pltpu.make_async_remote_copy(src_ref=src, dst_ref=dst, send_sem=xs_send.at[i], recv_sem=xs_recv.at[i],
                                            device_id=to, device_id_type=MESH)

    def own_rows(part, b):
        return ds(128 * lax.div(b, 2) + 64 * (1 - part) + 32 * lax.rem(b, 2), 32, 16)

    def own_a(part):
        for b in range(4):
            first = 128 * (b // 2) + 64 * (1 - part) + 32 * (b % 2)
            g.own[part, b] = g.dx[first : first + 32, :].astype(BF)
        for by in (1, 2, 3):
            to, c = near(1, by)
            m = own_msg(3 + 6 * part + by - 1, g.own.at[part, c], g.own_in.at[part, by - 1], to)
            m.start()
            started.append(m)

    def own_b(part):
        total = g.own[part, me].astype(F32)
        for by in (1, 2, 3):
            ref = g.own_in.at[part, by - 1]
            own_msg(3 + 6 * part + by - 1, ref, ref, sibling).wait_recv()
            total = total + g.own_in[part, by - 1].astype(F32)
        mine = own_out.at[own_rows(part, me)]
        mine[...] = total.astype(BF)
        for by in (1, 2, 3):
            m = own_msg(6 + 6 * part + by - 1, mine, mine, near(1, by)[0])
            m.start()
            started.append(m)

    def own_c(part):
        for by in (1, 2, 3):
            ref = own_out.at[own_rows(part, near(1, 4 - by)[1])]
            own_msg(6 + 6 * part + by - 1, ref, ref, sibling).wait_recv()

    def small_send(stage):
        n = 1 if stage == 0 else 3
        first = 0 if stage == 0 else 3 * stage - 2
        for k in range(n):
            to = sibling if stage == 0 else near(stage - 1, k + 1)[0]
            c = pltpu.make_async_remote_copy(
                src_ref=g.small_out_v.at[stage], dst_ref=g.small_in.at[first + k], send_sem=xs_send.at[15 + first + k],
                recv_sem=xs_recv.at[15 + first + k], device_id=to, device_id_type=MESH)
            c.start()
            started.append(c)

    def small_take(stage):
        n = 1 if stage == 0 else 3
        first = 0 if stage == 0 else 3 * stage - 2
        total = g.small_out_v[stage]
        for k in range(n):
            ref = g.small_in.at[first + k]
            pltpu.make_async_remote_copy(
                src_ref=ref, dst_ref=ref, send_sem=xs_send.at[15 + first + k],
                recv_sem=xs_recv.at[15 + first + k], device_id=sibling, device_id_type=MESH).wait_recv()
            total = total + g.small_in[first + k]
        g.small_out_v[stage + 1] = total

    for k in range(4):
        c = slice(k * D, (k + 1) * D)
        du = (mm_nt(g.cot_v[...], g.wd[c, :]) * g.gp[:, c]).astype(BF)
        g.du[:, c] = du
        g.sums[BUP + k : BUP + k + 1, :] = column_sum(du.astype(F32))
    du_go = to_sibling(5, half(g.du, 1 - core, 1536), g.f_du.at[hi])
    du_local = local(3, half(g.du, core, 1536), g.f_du.at[lo])
    g.sums[BDOWN : BDOWN + 1, :] = column_sum(g.cot_v[...].astype(F32))
    c_act_go.wait_recv()
    c_n2_go.wait_recv()
    each(send_left)
    g.tmp[...] = mm_nt(g.du[...], g.wu[...])
    zero8 = jnp.zeros((8, D), F32)

    def back_two(i, acc):
        rows = pl.ds(pl.multiple_of(i * 64, 64), 64)
        dn = g.tmp[rows, :]
        xhat = g.xh2[rows, :]
        dres = g.cot_v[rows, :].astype(F32) + normalise_back(dn, row(LN2G), xhat, g.rs2[rows, :])
        g.dres[rows, :] = dres
        da = dres.astype(BF)
        g.da[rows, :] = da
        return acc[0] + eights(dn * xhat), acc[1] + eights(dn), acc[2] + eights(da.astype(F32))

    acc = lax.fori_loop(0, 4, back_two, (zero8, zero8, zero8))
    for i, a in zip((LN2G, LN2S, BOUT), acc):
        g.sums[i : i + 1, :] = jnp.sum(a, 0, keepdims=True)
    g.dmix[...] = mm_nt(g.da[...], g.wo[...]).astype(BF)

    def attend_back(q, _):
        rows = pl.ds(pl.multiple_of(q * 128, 128), 128)
        for hp in range(6):
            lanes = slice(128 * hp, 128 * hp + 128)
            klanes = slice(D + 128 * hp, D + 128 * hp + 128)
            vlanes = slice(2 * D + 128 * hp, 2 * D + 128 * hp + 128)
            do2 = pair_rows(g.dmix[rows, lanes])
            p = g.prob[q * 6 + hp]
            dp = mm_nt(do2, g.qkv[rows, vlanes])
            ds = (p * (dp - jnp.sum(p * dp, -1, keepdims=True))).astype(BF)
            g.dqkv[rows, lanes] = (pair_join(mm(ds, g.qkv[rows, klanes])) * SCALE).astype(BF)
            g.dqkv[rows, klanes] = (mm_tn(ds, pair_rows(g.qkv[rows, lanes])) * SCALE).astype(BF)
            g.dqkv[rows, vlanes] = mm_tn(p.astype(BF), do2).astype(BF)
        return 0

    lax.fori_loop(0, 2, attend_back, 0)
    g.dn1[...] = mm_nt(g.dqkv[...], g.wq[...])

    def back_one(i, acc):
        rows = pl.ds(pl.multiple_of(i * 64, 64), 64)
        dn = g.dn1[rows, :]
        xhat = g.xh1[rows, :]
        g.dx[rows, :] = g.dres[rows, :] + normalise_back(dn, row(LN1G), xhat, g.rs1[rows, :])
        dq = eights(g.dqkv[rows, 0:D].astype(F32))
        dv = eights(g.dqkv[rows, 2 * D : 3 * D].astype(F32))
        return acc[0] + eights(dn * xhat), acc[1] + eights(dn), acc[2] + dq, acc[3] + dv

    acc = lax.fori_loop(0, 4, back_one, (zero8, zero8, zero8, zero8))
    for i, a in zip((LN1G, LN1S, BQV, BQV + 1), acc):
        g.sums[i : i + 1, :] = jnp.sum(a, 0, keepdims=True)

    g.slot_out[...] = mm(pick, g.dx[...].astype(BF)).astype(BF)
    for by in (1, 2, 3):
        c = pltpu.make_async_remote_copy(
            src_ref=g.slot_out, dst_ref=g.slots.at[me], send_sem=xs_send.at[by - 1], recv_sem=xs_recv.at[by - 1],
            device_id=device(along(pos, 1, by), core), device_id_type=MESH)
        c.start()
        started.append(c)
    g.dx_mini[...] = jnp.zeros((16, D), F32)
    g.e_own[...] = jnp.zeros((16, D), BF)
    g.du_own[...] = jnp.zeros((16, FF), BF)
    g.dqo_own[...] = jnp.zeros((80, FF), BF)
    g.dxm_own[...] = jnp.zeros((16, D), BF)
    g.dxb_own[...] = jnp.zeros((64, D), F32)
    dh_go.wait_recv()
    act_go.wait_recv()
    act_local.wait()
    for k in range(2):
        v = mm_tn(g.f_act[:, 768 * k : 768 * k + 768], g.f_dh[...]).astype(BF)
        for j in range(3):
            g.w1_0[j, 768 * k : 768 * k + 768, :] = v[:, 256 * j : 256 * j + 256]
    each(lambda k: send_first(0, k))
    own_a(0)
    du_go.wait_recv()
    du_local.wait()
    n2_go.wait_recv()
    for k in range(3):
        g.w1_1[k] = mm_tn(g.f_n2[...], g.f_du[:, 512 * k : 512 * k + 512]).astype(BF)
    each(lambda k: send_first(1, k))
    dq_go = to_sibling(6, half(g.dqo, 1 - core, 1536), g.f_qo.at[hi])
    dq_local = local(4, half(g.dqo, core, 1536), g.f_qo.at[lo])
    for by in (1, 2, 3):
        src = near(1, 4 - by)[1]
        pltpu.make_async_remote_copy(
            src_ref=g.slot_out, dst_ref=g.slots.at[src], send_sem=xs_send.at[by - 1], recv_sem=xs_recv.at[by - 1],
            device_id=device(along(pos, 1, by), core), device_id_type=MESH).wait_recv()
    keep = iota((16, D), 0) % 8 <= 5

    def thought_back(i, _):
        t = 2 - i

        @pl.when(t >= me)
        def _():
            e = (g.slots[t + 1].astype(F32) + g.dx_mini[...]).astype(BF).astype(F32)
            e = jnp.where(keep, pltpu.roll(e, 15, 0), 0.0)
            eb = e.astype(BF)
            parts = []
            for k in range(2):
                dm = mm_nt(eb, g.wd[k * 1536 : (k + 1) * 1536, :])
                parts.append((dm * g.gpm[t, :, k * 1536 : (k + 1) * 1536]).astype(BF))
            du = jnp.concatenate(parts, 1)
            dn2 = mm_nt(du, g.wu[...])
            xhat2 = g.xh2m[t]
            dres = e + normalise_back(dn2, row(LN2G), xhat2, g.rs2m[t])
            da = dres.astype(BF)
            dmix = mm_nt(da, g.wo[...]).astype(BF)
            do_s = lane_heads(dmix, 16)
            q_s = lane_heads(g.qkvm[t, :, 0:D], 16)
            p = g.pm[t]
            dp = mm_nt(do_s, g.vall[t])
            ds = (p * (dp - jnp.sum(p * dp, -1, keepdims=True))).astype(BF)
            dq = (join_heads(mm(ds, g.kall[t]), 16) * SCALE).astype(BF)
            dk = (mm_tn(ds, q_s)[0:80] * SCALE).astype(BF)
            dv = mm_tn(p.astype(BF), do_s)[0:80].astype(BF)
            dq = jnp.concatenate([jnp.zeros((64, D), BF), dq], 0)
            dqkv = jnp.concatenate([dq, dk, dv], 1)
            dn1 = mm_nt(dqkv, g.wq[...])
            gain = row(LN1G)
            xhat1 = g.xh1m[t]
            dxm = dres + normalise_back(dn1[64:80], gain, xhat1, g.rs1m[t])
            g.dx_mini[...] = dxm

            @pl.when(t == me)
            def _():
                g.e_own[...] = eb
                g.du_own[...] = du
                g.dqo_own[:, 0 : 3 * D] = dqkv
                g.dqo_own[64:80, 3 * D : FF] = da
                g.dxm_own[...] = dxm.astype(BF)
                total = {}
                b0, b1 = g.xh1[0:32, :], g.xh1[128:160, :]
                g.dxb_own[0:32, :] = normalise_back(dn1[0:32], gain, b0, g.rs1[0:32, :])
                g.dxb_own[32:64, :] = normalise_back(dn1[32:64], gain, b1, g.rs1[128:160, :])
                total[LN1G] = column_sum(dn1[0:32] * b0) + column_sum(dn1[32:64] * b1) + column_sum(dn1[64:80] * xhat1)
                total[LN1S] = column_sum(dn1)
                total[BQV] = column_sum(dq.astype(F32))
                total[BQV + 1] = column_sum(dv.astype(F32))
                total[BOUT] = column_sum(da.astype(F32))
                total[LN2G] = column_sum(dn2 * xhat2)
                total[LN2S] = column_sum(dn2)
                total[BDOWN] = column_sum(e)
                for i, v in total.items():
                    g.sums[i : i + 1, :] += v
                for k in range(4):
                    g.sums[BUP + k : BUP + k + 1, :] += column_sum(du[:, k * D : (k + 1) * D].astype(F32))

        return 0

    lax.fori_loop(0, 3, thought_back, 0)

    g.c_e[0:16, :] = g.e_own[...]
    g.c_du[0:16, :] = g.du_own[:, pl.ds(pl.multiple_of(core * 1536, 128), 1536)]
    c_e_go = to_sibling(9, g.c_e.at[mini_lo], g.c_e.at[mini_hi])
    c_du_go = to_sibling(10, half(g.du_own, 1 - core, 1536), g.c_du.at[mini_hi])
    c_qo_go = to_sibling(8, half(g.dqo_own, 1 - core, 1536), g.c_qo)
    top = [slice(128 * q, 128 * q + TOP) for q in range(2)]

    def merge(first, own, cols, q, spread):
        rows = slice(first + 128 * q, first + 128 * q + TOP)
        base = jnp.concatenate([own[32 * q : 32 * q + 32, cols].astype(F32), jnp.zeros((16, 1536), F32)], 0)
        g.f_qo[rows, :] = (g.f_qo[rows, :].astype(F32) + mm(spread, own[64:80, cols]) + base).astype(BF)

    dq_local.wait()
    for q in range(2):
        merge(0, g.dqo_own, pl.ds(pl.multiple_of(core * 1536, 128), 1536), q, place[q])
    c_e_go.wait_recv()
    c_du_go.wait_recv()
    each(send_right)
    for c in (dq_go, c_qo_go, n1_go, o_go, spread_go):
        c.wait_recv()
    for q in range(2):
        merge(256, g.c_qo, slice(None), q, g.spread[1, q])
    left = mm_tn(g.f_n1[...], g.f_qo[:, 0:768]).astype(BF)
    g.w1_2[0] = left[:, 0:512]
    g.w1_2[1, :, 0:256] = left[:, 512:768]

    def right(factor):
        v = mm_tn(factor[...], g.f_qo[:, 768:1536]).astype(BF)
        g.w1_2[1, :, 256:512] = v[:, 0:256]
        g.w1_2[2] = v[:, 256:768]

    @pl.when(core == 0)
    def _():
        right(g.f_n1)

    @pl.when(core == 1)
    def _():
        right(g.f_o)

    each(ring_a)
    step(0, sum_first, rs2a)
    step(1, sum_first, rs2a)
    g.small_out_v[0] = g.sums[...]
    small_send(0)
    each(ring_b)
    later = (me > 0).astype(F32)
    for q, s in ((0, s0), (1, s1)):
        dx = g.dx[top[q], :] + mm(place[q], g.dxm_own[...])
        dx = dx + jnp.concatenate([g.dxb_own[32 * q : 32 * q + 32, :], jnp.zeros((16, D), F32)], 0)
        dx = dx * (1.0 - later * is_slot(s, TOP).astype(F32))
        g.dx[top[q], :] = dx
    own_a(1)
    own_b(0)
    step(0, rs2b, rs3a)
    step(1, rs2b, rs3a)
    small_take(0)
    small_send(1)
    each(ring_c)
    step(2, rs2a)
    step(0, rs3b)
    step(1, rs3b)
    small_take(1)
    small_send(2)
    step(2, rs2b, rs3a)
    step(0, ag3b, ag2a)
    step(1, ag3b, ag2a)
    own_b(1)
    step(2, rs3b)
    step(0, ag2b, ag1a)
    small_take(2)
    small_send(3)
    step(2, ag3b, ag2a)
    step(1, ag2b, ag1a)
    step(0, ag1b)
    step(2, ag2b, ag1a)
    step(1, ag1b)
    step(0, ag1c)
    small_take(3)
    small_out[...] = g.small_out_v[4]
    own_c(0)
    own_c(1)
    step(1, ag1c)
    step(2, ag1b)
    step(2, ag1c)
    for w in range(3):
        step(w, sib)
    for c in started:
        c.wait_send()


SCRATCH["small_out_v"] = ((5, 16, D), F32)
NAMES.append("small_out_v")


def passes(*args):
    smem = pl.BlockSpec(memory_space=pltpu.SMEM)
    hbm = pl.BlockSpec(memory_space=pl.ANY)
    vmem = pl.BlockSpec(memory_space=pltpu.VMEM)
    dma = pltpu.SemaphoreType.DMA
    return pl.pallas_call(
        kernel,
        out_shape=[
            pltpu.VMEM((ROWS, D), BF),
            pltpu.VMEM((ROWS, D), BF),
            pltpu.VMEM((16, D), F32),
            pltpu.VMEM((D, FF), BF),
            pltpu.VMEM((D, FF), BF),
            pltpu.VMEM((FF, D), BF),
        ],
        in_specs=[smem, smem] + [hbm] * (len(args) - 2),
        out_specs=[vmem] * 6,
        scratch_shapes=[pltpu.VMEM(s, t) for s, t in SCRATCH.values()]
        + [dma((21,)), dma((13,)), dma((13,)), dma((9, NMSG)), dma((9, NMSG)), dma((25,)), dma((25,))],
        compiler_params=pltpu.CompilerParams(
            collective_id=0, has_side_effects=True, vmem_limit_bytes=VMEM_LIMIT
        ),
        name="passes",
    )(*args)


VMEM_LIMIT = 48 * 2**20
SMALL = ((LN1G, 1), (LN1S, 1), (BQV, 2), (BOUT, 1), (LN2G, 1), (LN2S, 1), (BUP, 4), (BDOWN, 1))


def widen_kernel(act, own, small, qo, u, d, act_out, own_out, gq, go, gu, gd, *rest):
    small_outs, (wide, tall, sem, wide_sem, tall_sem) = rest[:8], rest[8:]
    pending = []

    def copy(src, dst, s):
        c = pltpu.make_async_copy(src, dst, s)
        c.start()
        return c

    pending.append(copy(act, act_out, sem.at[0]))
    pending.append(copy(own, own_out, sem.at[1]))
    n = 2
    for (first, count), ref in zip(SMALL, small_outs):
        for k in range(count):
            pending.append(copy(small.at[first + k], ref.at[pl.ds(k * D, D)], sem.at[n]))
            n += 1
    slots = {}

    def chunk(buf, sems, i, value, parts):
        slot = i % buf.shape[0]
        key = (buf is wide, slot)
        for c in slots.get(key, ()):
            c.wait()
        buf[slot] = value.astype(F32)
        slots[key] = [copy(buf.at[slot, :, pl.ds(l0, n)], dst, sems.at[slot, j]) for j, (l0, n, dst) in enumerate(parts)]

    for i in range(12):
        rows = pl.ds(64 * i, 64)
        chunk(wide, wide_sem, 2 * i, qo[64 * i : 64 * i + 64, :], ((0, 3 * D, gq.at[rows]), (3 * D, D, go.at[rows])))
        chunk(tall, tall_sem, i, d[256 * i : 256 * i + 256, :], ((0, D, gd.at[pl.ds(256 * i, 256)]),))
        chunk(wide, wide_sem, 2 * i + 1, u[64 * i : 64 * i + 64, :], ((0, FF, gu.at[rows]),))
    for cs in list(slots.values()) + [pending]:
        for c in cs:
            c.wait()


def widen(*arrays):
    hbm = pl.BlockSpec(memory_space=pl.ANY)
    vmem = pl.BlockSpec(memory_space=pltpu.VMEM)
    dma = pltpu.SemaphoreType.DMA
    shape = jax.ShapeDtypeStruct
    return pl.pallas_call(
        widen_kernel,
        in_specs=[vmem] * 6,
        out_specs=[hbm] * 14,
        out_shape=[shape((ROWS, D), BF), shape((ROWS, D), BF), shape((D, 3 * D), F32), shape((D, D), F32), shape((D, FF), F32),
                   shape((FF, D), F32)] + [shape((n * D,), F32) for _, n in SMALL],
        scratch_shapes=[pltpu.VMEM((6, 64, FF), F32), pltpu.VMEM((3, 256, D), F32), dma((14,)), dma((6, 2)), dma((3, 1))],
        compiler_params=pltpu.CompilerParams(vmem_limit_bytes=24 * 2**20),
        name="widen",
    )(*arrays)


def on_device(embedded, cotangent, lengths, starts, *params):
    gathered = passes(starts, lengths, embedded.reshape(ROWS, D), cotangent.reshape(ROWS, D), *params)
    act, own, gq, go, gu, gd, ln1g, ln1s, bqv, bout, ln2g, ln2s, bup, bdown = widen(*gathered)
    return (act.reshape(1, 2, 128, D), own.reshape(2, 128, D), ln1g, ln1s, gq, bqv, go, bout, ln2g, ln2s, gu, bup, gd, bdown)


def solution(mesh):
    rows = P("batch", None, None)
    passes_rows = P("pass", "batch", None, None)
    return jax.shard_map(
        on_device,
        mesh=mesh,
        in_specs=(rows, passes_rows, P("batch"), P("batch")) + (P(),) * 12,
        out_specs=(passes_rows, rows) + (P(),) * 12,
        check_vma=False,
    )
```
